32 devices in a mesh: dp: 8 (over z, y), tensor: 4 (over x, core).
Axes of the slice: x: 2, y: 2, z: 4, core: 2. Of those that a mesh axis runs over, the one named last changes fastest.
Arguments:
- inputs: bfloat16 [8192, 2048], P(('dp', 'tensor')), may hold values from -6 to 6
- cotangent: bfloat16 [8192, 2048], P(('dp', 'tensor')), may hold values from -6 to 6
- w_query: bfloat16 [2048, 1280], P('dp', 'tensor'), may hold values from -0.125 to 0.125
- w_kv: bfloat16 [2048, 640], P('dp'), may hold values from -0.125 to 0.125
- w_out: bfloat16 [1280, 2048], P('tensor', 'dp'), may hold values from -1.25 to 1.25
- w_in: bfloat16 [2048, 2, 6144], P('dp', None, 'tensor'), may hold values from -0.125 to 0.125
- w_down: bfloat16 [6144, 2048], P('tensor', 'dp'), may hold values from -0.078125 to 0.078125
- norm_gains: bfloat16 [2, 2048], P(None, 'dp'), may hold values from 0.099609375 to 1.8984375
- head_gains: bfloat16 [2, 64], replicated, may hold values from 0.099609375 to 1.8984375
- lengths: int32 [4], replicated, may hold values from 64 to 2048, as said below
- slot_blocks: int32 [128], replicated, may hold values from 0 to 127, as said below
Outputs:
- outputs: bfloat16 [8192, 2048], P(('dp', 'tensor'))
- grad_inputs: bfloat16 [8192, 2048], P(('dp', 'tensor'))
- grad_w_query: float32 [2048, 1280], P('dp', 'tensor')
- grad_w_kv: float32 [2048, 640], P('dp')
- grad_w_out: float32 [1280, 2048], P('tensor', 'dp')
- grad_w_in: float32 [2048, 2, 6144], P('dp', None, 'tensor')
- grad_w_down: float32 [6144, 2048], P('tensor', 'dp')
- grad_norm_gains: float32 [2, 2048], P(None, 'dp')
- grad_head_gains: float32 [2, 64], replicated
The draws below stay inside these ranges and needn't reach their ends.
Inputs may be any that keep to these rules, and one draw needn't show every extreme that they name: `lengths`: one row, drawn from the seed, has all 2048 slots live. Lengths are multiples of 64, at least 64. `slot_blocks`: each block number appears once. The slots of one dp index hold its rows in order, 4 blocks of each row, and its g-th block of a row comes from the g-th aligned group of 8 consecutive blocks of that row; every dp index holds a different block of each such group.
All inputs are finite; a program needn't handle non-finite values.
Results may differ from the reference program's by a relative error of at most 0.028.
Values may be sent and summed in bfloat16 or wider, within the bound.
No kernel may reach another device: no remote copies, remote signals or barrier semaphores. Data moves between devices by JAX's collectives and lax.ppermute only.
A program may use at most 576 MiB of HBM per device.

```python
import jax
import jax.numpy as jnp
from jax import lax

D = 2048
HEADS_Q = 20
HEADS_KV = 5
HEAD = 64
FF = 6144
SLOTS = 2048
STRETCH = 64
MIN_LEN = 64
TOKENS = 8192
ROWS = 4
QD = 1280
KVD = 320
N_DP = 8


def draw_lengths(key, part):
    key = jax.random.fold_in(key, 3)
    first_key, third_key = jax.random.split(key, 2)
    drawn = jax.random.randint(first_key, (ROWS,), MIN_LEN, SLOTS)
    ragged = jnp.maximum(drawn // STRETCH * STRETCH, MIN_LEN)
    full_row = jax.random.randint(third_key, (), 0, ROWS)
    return jnp.where(jnp.arange(ROWS) == full_row, SLOTS, ragged).astype(jnp.int32)


def draw_slot_blocks(key, part):
    key = jax.random.fold_in(key, 7)
    per_row = SLOTS // STRETCH
    groups = per_row // N_DP
    group_keys = jax.random.split(key, ROWS * groups)
    perms = jax.vmap(lambda one_key: jax.random.permutation(one_key, N_DP))(group_keys)
    perms = perms.reshape(ROWS, groups, N_DP)
    base = jnp.arange(ROWS)[:, None] * per_row + jnp.arange(groups)[None, :] * N_DP
    table = base[:, :, None] + perms
    return jnp.transpose(table, (2, 0, 1)).reshape(-1).astype(jnp.int32)


def block_levels(own_key, extent, pieces, least, top_value):
    def one(dim, blocks):
        heights = jax.random.uniform(jax.random.fold_in(jax.random.fold_in(own_key, 6), dim), (blocks,), jnp.float32, least / len(pieces), top_value / len(pieces))
        return jnp.repeat(jnp.exp(heights), extent[dim] // blocks).reshape((-1,) + (1,) * (len(extent) - dim - 1))

    loudness = one(*pieces[0])
    for cut in pieces[1:]:
        loudness = loudness * one(*cut)
    return loudness


def bell_draw(rng, shape, scale, bound, shards=(), held_as=jnp.bfloat16):
    array = scale * jax.random.normal(rng, shape, jnp.float32)
    if shards:
        array = array * block_levels(rng, shape, shards, -0.22, 0.18)
    return jnp.clip(array, -bound, bound).astype(held_as)


def setup_inputs(seed: int = 0) -> dict:
    arg_keys = jax.random.split(jax.random.key(seed), 12)
    return {
        "inputs": bell_draw(arg_keys[0], (TOKENS, D), 1.0, 6.0, ((0, 32),)),
        "cotangent": bell_draw(arg_keys[1], (TOKENS, D), 1.0, 6.0, ((0, 32),)),
        "w_query": bell_draw(arg_keys[2], (D, QD), D ** -0.5, 0.125, ((0, 8), (1, 4))),
        "w_kv": bell_draw(arg_keys[3], (D, 2 * KVD), D ** -0.5, 0.125, ((0, 8),)),
        "w_out": bell_draw(arg_keys[4], (QD, D), HEADS_Q ** -0.5, 1.25, ((0, 4), (1, 8))),
        "w_in": bell_draw(arg_keys[5], (D, 2, FF), D ** -0.5, 0.125, ((0, 8), (2, 4))),
        "w_down": bell_draw(arg_keys[6], (FF, D), FF ** -0.5, 0.078125, ((0, 4), (1, 8))),
        "norm_gains": jnp.clip(1.0 + 0.18 * jax.random.normal(arg_keys[7], (2, D), jnp.float32), 0.099609375, 1.8984375).astype(jnp.bfloat16),
        "head_gains": jnp.clip(1.0 + 0.18 * jax.random.normal(arg_keys[8], (2, HEAD), jnp.float32), 0.099609375, 1.8984375).astype(jnp.bfloat16),
        "lengths": draw_lengths(jax.random.fold_in(arg_keys[11], 71), 0),
        "slot_blocks": draw_slot_blocks(jax.random.fold_in(arg_keys[11], 71), 0),
    }


@jax.custom_vjp
def low(v):
    return lax.optimization_barrier(v.astype(jnp.bfloat16)).astype(jnp.float32)

@jax.custom_vjp
def low_back(v):
    return v

def low_keep(v):
    return (low(v), None)

def low_pass(kept, grad):
    return (grad,)

def back_keep(v):
    return (v, None)

def back_low(kept, grad):
    return (low(grad),)
low.defvjp(low_keep, low_pass)
low_back.defvjp(back_keep, back_low)
eps_norm = 1e-06
rope_base = 10000.0
neg_large = -1e+30
highest = lax.Precision.HIGHEST

def scaled_norm(value_in, gain_vec):
    return value_in * lax.rsqrt(lax.optimization_barrier(jnp.mean(value_in * value_in, axis=-1, keepdims=True)) + eps_norm) * gain_vec

def rotate(raw_value, gain_vec, positions, factor):
    row_total = raw_value.shape[0]
    per_head = scaled_norm(raw_value.reshape(row_total, -1, HEAD), gain_vec)
    half_head = HEAD // 2
    frequency = rope_base ** (-2.0 * jnp.arange(half_head, dtype=jnp.float32) / HEAD)
    angles = positions.astype(jnp.float32)[:, None] * frequency[None, :]
    cosine = jnp.cos(angles)[:, None, :]
    sine_tab = jnp.sin(angles)[:, None, :]
    first_half = per_head[..., :half_head]
    second = per_head[..., half_head:]
    turned = jnp.concatenate([first_half * cosine - second * sine_tab, second * cosine + first_half * sine_tab], axis=-1)
    return (turned * factor).reshape(row_total, -1)

def attend(query_seq, key_seq, value_seq, lengths):
    block_rows = min(512, SLOTS)
    key_pos = jnp.arange(SLOTS, dtype=jnp.int32)
    group_size = HEADS_Q // HEADS_KV

    def one_row(row_args):
        query_row, key_row, value_row, length_row = row_args
        key_all = jnp.tile(key_row, (1, group_size, 1))
        value_all = jnp.tile(value_row, (1, group_size, 1))
        blocks = query_row.reshape(SLOTS // block_rows, block_rows, HEADS_Q, HEAD)
        starts = jnp.arange(SLOTS // block_rows, dtype=jnp.int32) * block_rows

        def one_block(block_args):
            query_block, first_row = block_args
            query_pos = first_row + jnp.arange(block_rows, dtype=jnp.int32)
            scores = low_back(jnp.einsum('qhd,khd->hqk', query_block, key_all, precision=highest))
            visible = (key_pos[None, :] <= query_pos[:, None]) & (key_pos[None, :] < length_row)
            scores = jnp.where(visible[None], scores, neg_large)
            row_peak = lax.optimization_barrier(jnp.max(scores, axis=-1, keepdims=True))
            exponent = jnp.exp(scores - row_peak)
            probs = low(exponent / lax.optimization_barrier(jnp.sum(exponent, axis=-1, keepdims=True)))
            return jnp.einsum('hqk,khd->qhd', probs, value_all, precision=highest)
        heads_out = lax.map(jax.checkpoint(one_block), (blocks, starts))
        return heads_out.reshape(SLOTS, HEADS_Q * HEAD)
    return lax.map(jax.checkpoint(one_row), (query_seq, key_seq, value_seq, lengths))

def forward(inputs, w_query, w_kv, w_out, w_in, w_down, norm_gains, head_gains, positions, live, order, back, lengths):
    h_one = low(scaled_norm(inputs, norm_gains[0]))
    q_raw = low_back(jnp.dot(h_one, w_query, precision=highest))
    kv_raw = low_back(jnp.dot(h_one, w_kv, precision=highest))
    queries = low(rotate(q_raw, head_gains[0], positions, 0.125))
    keys_part = low(rotate(kv_raw[:, :KVD], head_gains[1], positions, 1.0))
    values_part = low(kv_raw[:, KVD:])
    query_seq = queries[order].reshape(ROWS, SLOTS, HEADS_Q, HEAD)
    key_seq = keys_part[order].reshape(ROWS, SLOTS, HEADS_KV, HEAD)
    value_seq = values_part[order].reshape(ROWS, SLOTS, HEADS_KV, HEAD)
    heads_seq = attend(query_seq, key_seq, value_seq, lengths)
    attn_heads = low_back(low(heads_seq.reshape(TOKENS, QD)[back]))
    attn = low_back(jnp.dot(attn_heads, w_out, precision=highest))
    mixed = inputs + live[:, None] * attn
    h_two = low(scaled_norm(mixed, norm_gains[1]))
    gate = low_back(jnp.dot(h_two, w_in[:, 0, :], precision=highest))
    up_part = low_back(jnp.dot(h_two, w_in[:, 1, :], precision=highest))
    hidden = low(gate * jax.nn.sigmoid(gate) * up_part)
    ffn = low_back(jnp.dot(hidden, w_down, precision=highest))
    return mixed + live[:, None] * ffn

def reference(inputs, cotangent, w_query, w_kv, w_out, w_in, w_down, norm_gains, head_gains, lengths, slot_blocks):
    per_row = SLOTS // STRETCH
    inside = jnp.tile(jnp.arange(STRETCH, dtype=jnp.int32), TOKENS // STRETCH)
    block_of = jnp.repeat(slot_blocks.astype(jnp.int32), STRETCH)
    back = (block_of * STRETCH + inside).astype(jnp.int32)
    order = jnp.zeros((TOKENS,), jnp.int32).at[back].set(jnp.arange(TOKENS, dtype=jnp.int32))
    positions = (block_of % per_row * STRETCH + inside).astype(jnp.int32)
    live = (positions < lengths[block_of // per_row]).astype(jnp.float32)
    floats = (inputs, w_query, w_kv, w_out, w_in, w_down, norm_gains, head_gains)
    floats = tuple((array_in.astype(jnp.float32) for array_in in floats))

    def layer_fn(*params):
        return forward(*params, positions, live, order, back, lengths)
    outputs, pull = jax.vjp(layer_fn, *floats)
    gradients = pull(cotangent.astype(jnp.float32))
    return (outputs.astype(jnp.bfloat16), gradients[0].astype(jnp.bfloat16), gradients[1], gradients[2], gradients[3], gradients[4], gradients[5], gradients[6], gradients[7])
```

```python
import functools

import jax
import jax.numpy as jnp
from jax import lax
from jax.experimental import pallas as pl
from jax.experimental.pallas import tpu as pltpu
from jax.sharding import PartitionSpec as P

HEADS_KV = 5
HEAD = 64
SLOTS = 2048
STRETCH = 64
LANES = 128
FF_CHUNKS = 3
VMEM_LIMIT = 48 * 1024 * 1024

eps_norm = 1e-06
rope_base = 10000.0
neg_large = -1e30
f32 = jnp.float32
bf16 = jnp.bfloat16
contract_rows = (((0,), (0,)), ((), ()))
contract_cols = (((1,), (1,)), ((), ()))


def dot(a, b, dims=(((1,), (0,)), ((), ()))):
    return lax.dot_general(a, b, dims, preferred_element_type=f32)


def after(value, *deps):
    return lax.optimization_barrier((value, *deps))[0]


def levels(size):
    out, bit = [], 1
    while bit < size:
        if bit > 1 and 2 * bit < size:
            out.append([bit, 2 * bit, 3 * bit])
            bit *= 4
        else:
            out.append([bit])
            bit *= 2
    return out


def swap(value, axis, mask):
    size = lax.axis_size(axis)
    return lax.ppermute(value, axis, [(i, i ^ mask) for i in range(size)])


def gather_rel(value, axis):
    pieces = {0: value}
    for masks in reversed(levels(lax.axis_size(axis))):
        pieces.update({r ^ m: swap(p, axis, m) for r, p in list(pieces.items()) for m in masks})
    return [pieces[r] for r in range(lax.axis_size(axis))]


def gather_stacked(value, axis):
    stack = value[None]
    for masks in reversed(levels(lax.axis_size(axis))):
        parts = [stack] + [swap(stack, axis, m) for m in masks]
        stack = jnp.stack(parts, axis=1).reshape((-1,) + value.shape)
    return stack


def gather_rows(value, axis):
    index = lax.axis_index(axis)
    stack = value
    size = lax.axis_size(axis)
    bit = size // 2
    at = value.ndim - 2
    while bit:
        other = swap(stack, axis, bit)
        upper = (index & bit) != 0
        stack = jnp.stack(
            [jnp.where(upper, other, stack), jnp.where(upper, stack, other)], axis=at
        )
        bit //= 2
        at += 1
    lead = value.shape[:-2]
    return stack.reshape(lead + (size,) + value.shape[-2:])


def reduce_rel(make, axis):
    size = lax.axis_size(axis)
    held = None
    keep = list(range(size))
    arrived = {}
    for masks in levels(size):
        bits = functools.reduce(lambda a, b: a | b, masks)
        rest = [r for r in keep if not r & bits]
        for m in masks:
            group = [r ^ m for r in rest]
            for r, part in zip(group, make(group)):
                total = part
                for other in arrived.get(r, ()):
                    total = total + other.astype(f32)
                arrived.setdefault(r ^ m, []).append(swap(total.astype(bf16), axis, m))
        keep = rest
    (total,) = make([0])
    for other in arrived[0]:
        total = total + other.astype(f32)
    return total


def scaled_norm(value_in, gain_vec):
    return (
        value_in
        * lax.rsqrt(jnp.mean(value_in * value_in, axis=-1, keepdims=True) + eps_norm)
        * gain_vec
    )


def silu_product(gate, up_part):
    return gate * jax.nn.sigmoid(gate) * up_part


def params(steps=1):
    return pltpu.CompilerParams(
        dimension_semantics=("arbitrary",) * steps, vmem_limit_bytes=VMEM_LIMIT
    )


def swap_halves(value):
    half = HEAD // 2
    return jnp.concatenate([value[:, half:], value[:, :half]], axis=1)


def rope_one(raw, gain, cos, sin, factor):
    scale = lax.rsqrt(jnp.mean(raw * raw, axis=-1, keepdims=True) + eps_norm)
    normed = raw * scale * gain
    return (normed * cos + swap_halves(normed) * sin) * factor


def rope_back(raw, gain, cos, sin, factor, grad):
    grad = grad * factor
    grad = grad * cos - swap_halves(grad) * sin
    scale = lax.rsqrt(jnp.mean(raw * raw, axis=-1, keepdims=True) + eps_norm)
    weighted = grad * gain
    back = scale * weighted - raw * (
        scale * scale * scale * jnp.mean(raw * weighted, axis=-1, keepdims=True)
    )
    return back, jnp.sum(grad * raw * scale, axis=0, keepdims=True)


def query_kernel(h_ref, w_ref, cos_ref, sin_ref, gain_ref, raw_ref, out_ref):
    raw = dot(h_ref[...], w_ref[0])
    raw_ref[0] = raw
    rows, blocks = out_ref.shape[0], out_ref.shape[2]
    for h in range(HEADS_KV):
        turned = rope_one(
            raw[:, h * HEAD : (h + 1) * HEAD], gain_ref[...], cos_ref[...], sin_ref[...], 0.125
        )
        wide = jnp.concatenate([turned, jnp.zeros_like(turned)], axis=1).astype(bf16)
        out_ref[:, h, :, 0] = wide.reshape(rows, blocks, STRETCH, LANES)


def key_kernel(h_ref, w_ref, cos_ref, sin_ref, gain_ref, raw_ref, out_ref):
    raw = dot(h_ref[...], w_ref[...])
    raw_ref[...] = raw
    rows, blocks = out_ref.shape[0], out_ref.shape[2]
    for h in range(HEADS_KV):
        turned = rope_one(
            raw[:, h * HEAD : (h + 1) * HEAD], gain_ref[...], cos_ref[...], sin_ref[...], 1.0
        )
        start = (HEADS_KV + h) * HEAD
        wide = jnp.concatenate([turned, raw[:, start : start + HEAD]], axis=1).astype(bf16)
        out_ref[:, h] = wide.reshape(rows, blocks, STRETCH, LANES)


def attend_kernel(q_ref, limit_ref, keypos_ref, *rest):
    pieces, (out_ref, kv, kvt) = rest[:-3], rest[-3:]
    blocks = q_ref.shape[2]
    n = len(pieces)
    group = n * STRETCH
    for r, piece in enumerate(pieces):
        for g in range(blocks):
            kv[g * group + r * STRETCH : g * group + (r + 1) * STRETCH, :] = piece[0, 0, g]
    kvt[...] = kv[...].T
    for b in range(blocks):
        span = (b + 1) * group
        q = q_ref[0, 0, b].reshape(-1, LANES)
        scores = dot(kv[:span], q, contract_cols)
        scores = jnp.where(keypos_ref[0, :span] <= limit_ref[0, b], scores, neg_large)
        top = jnp.max(scores, axis=0, keepdims=True)
        weights = jnp.exp(scores - top)
        total = jnp.sum(weights, axis=0, keepdims=True)
        heads = dot(kvt[:, :span], weights.astype(bf16)) / total
        out_ref[0, 0, b] = heads.T.astype(bf16).reshape(q_ref.shape[3:])


def attend_back_kernel(q_ref, g_ref, limit_ref, keypos_ref, *rest):
    n = (len(rest) - 4) // 2
    pieces, dq_ref, outs, (kv, kvt, acc) = rest[:n], rest[n], rest[n + 1 : -3], rest[-3:]
    blocks = q_ref.shape[2]
    group = n * STRETCH
    for r, piece in enumerate(pieces):
        for g in range(blocks):
            kv[g * group + r * STRETCH : g * group + (r + 1) * STRETCH, :] = piece[0, 0, g]
    kvt[...] = kv[...].T
    acc[...] = jnp.zeros_like(acc)
    for b in range(blocks):
        span = (b + 1) * group
        q = q_ref[0, 0, b].reshape(-1, LANES)
        grad = g_ref[0, 0, b].reshape(-1, LANES)
        scores = dot(kv[:span], q, contract_cols)
        scores = jnp.where(keypos_ref[0, :span] <= limit_ref[0, b], scores, neg_large)
        top = jnp.max(scores, axis=0, keepdims=True)
        weights = jnp.exp(scores - top)
        probs = weights * (1.0 / jnp.sum(weights, axis=0, keepdims=True))
        d_probs = dot(kv[:span], grad, contract_cols)
        delta = jnp.sum(probs * d_probs, axis=0, keepdims=True)
        d_scores = (probs * (d_probs - delta)).astype(bf16)
        dq = dot(kvt[:, :span], d_scores)
        dq_ref[0, 0, b] = dq.T.reshape(q_ref.shape[3:])
        acc[:span] += dot(d_scores, q) + dot(probs.astype(bf16), grad)
    for r, out in enumerate(outs):
        for g in range(blocks):
            out[0, 0, g] = acc[g * group + r * STRETCH : g * group + (r + 1) * STRETCH].astype(bf16)


def out_kernel(o_ref, w_ref, attn_ref, heads_ref):
    rows = heads_ref.shape[1]

    @pl.when(pl.program_id(0) == 0)
    def _():
        for s in range(heads_ref.shape[0]):
            heads_ref[s] = jnp.concatenate(
                [o_ref[:, h, :, s].reshape(rows, LANES)[:, HEAD:] for h in range(HEADS_KV)], axis=1
            )

    attn_ref[0] = sum(dot(heads_ref[s], w_ref[s, 0]) for s in range(heads_ref.shape[0]))


def heads_back_kernel(d_ref, w_ref, out_ref, acc):
    step = pl.program_id(0)

    @pl.when(step == 0)
    def _():
        acc[...] = jnp.zeros_like(acc)

    for s in range(acc.shape[0]):
        acc[s] += dot(d_ref[0], w_ref[s, 0], contract_cols)

    @pl.when(step == pl.num_programs(0) - 1)
    def _():
        rows, blocks = out_ref.shape[0], out_ref.shape[2]
        for s in range(acc.shape[0]):
            for h in range(HEADS_KV):
                part = acc[s, :, h * HEAD : (h + 1) * HEAD]
                wide = jnp.concatenate([jnp.zeros_like(part), part], axis=1).astype(bf16)
                out_ref[:, h, :, s] = wide.reshape(rows, blocks, STRETCH, LANES)


def query_back_kernel(dq_ref, raw_ref, cos_ref, sin_ref, gain_ref, out_ref, dgain_ref):
    @pl.when(pl.program_id(0) == 0)
    def _():
        dgain_ref[...] = jnp.zeros_like(dgain_ref)

    raw = raw_ref[0]
    parts = []
    for h in range(HEADS_KV):
        grad = dq_ref[:, h, :, 0].reshape(raw.shape[0], LANES)[:, :HEAD]
        back, dgain = rope_back(
            raw[:, h * HEAD : (h + 1) * HEAD],
            gain_ref[...],
            cos_ref[...],
            sin_ref[...],
            0.125,
            grad,
        )
        parts.append(back)
        dgain_ref[...] += dgain
    out_ref[0] = jnp.concatenate(parts, axis=1).astype(bf16)


def key_back_kernel(sum_ref, raw_ref, cos_ref, sin_ref, gain_ref, out_ref, dgain_ref):
    raw = raw_ref[...]
    keys, values = [], []
    total = jnp.zeros_like(dgain_ref)
    for h in range(HEADS_KV):
        both = sum_ref[:, h].reshape(raw.shape[0], LANES)
        back, dgain = rope_back(
            raw[:, h * HEAD : (h + 1) * HEAD],
            gain_ref[...],
            cos_ref[...],
            sin_ref[...],
            1.0,
            both[:, :HEAD],
        )
        keys.append(back)
        values.append(both[:, HEAD:])
        total = total + dgain
    dgain_ref[...] = total
    out_ref[...] = jnp.concatenate(keys + values, axis=1).astype(bf16)


def back_kernel(dq_ref, wq_ref, dkv_ref, wkv_ref, out_ref):
    @pl.when(pl.program_id(0) == 0)
    def _():
        out_ref[...] = dot(dkv_ref[...], wkv_ref[...], contract_cols)

    out_ref[...] += dot(dq_ref[0], wq_ref[0], contract_cols)


def whole(shape):
    return pl.BlockSpec(shape, lambda *_: (0,) * len(shape))


def local(
    inputs,
    cotangent,
    w_query,
    w_kv,
    w_out,
    w_in,
    w_down,
    norm_gains,
    head_gains,
    lengths,
    slot_blocks,
):
    sp_rows, width = inputs.shape
    n = lax.axis_size("dp")
    n_tensor = lax.axis_size("tensor")
    dp = lax.axis_index("dp")
    tensor = lax.axis_index("tensor")
    seq_count = lengths.shape[0]
    row_span = sp_rows * n_tensor // seq_count
    blocks = row_span // STRETCH
    rows = sp_rows // row_span
    per_row = SLOTS // STRETCH
    cols = width // n
    q_cols = w_query.shape[1]
    kv_cols = w_kv.shape[1]
    ff = w_down.shape[0]
    rels = jnp.arange(n, dtype=jnp.int32)

    def reorder(value):
        return jnp.concatenate(
            [lax.dynamic_slice_in_dim(value, (dp ^ r) * cols, cols, axis=1) for r in range(n)],
            axis=1,
        )

    table = slot_blocks.reshape(n, n_tensor, rows, blocks)
    mine = lax.dynamic_index_in_dim(table, tensor, axis=1, keepdims=False)[dp ^ rels]
    inside = jnp.arange(STRETCH, dtype=jnp.int32)
    key_pos = (mine % per_row * STRETCH)[..., None] + inside
    own_pos = key_pos[0]
    own_len = lengths[mine[0] // per_row][..., None]
    live = (own_pos < own_len).astype(f32).reshape(sp_rows, 1)
    limit = jnp.minimum(own_pos, own_len - 1)
    limit = jnp.broadcast_to(limit[:, :, None, None, :], (rows, blocks, 1, n_tensor, STRETCH))
    limit = limit.reshape(rows, blocks, 1, n_tensor * STRETCH)
    key_pos = key_pos.transpose(1, 2, 0, 3).reshape(rows, SLOTS, 1)
    half = HEAD // 2
    frequency = rope_base ** (-2.0 * jnp.arange(half, dtype=f32) / HEAD)
    angles = own_pos.reshape(sp_rows, 1).astype(f32) * frequency
    cosine, sine = jnp.cos(angles), jnp.sin(angles)
    cos = jnp.concatenate([cosine, cosine], axis=1)
    sin = jnp.concatenate([-sine, sine], axis=1)
    head_float = head_gains.astype(f32)
    q_gain, k_gain = head_float[0:1], head_float[1:2]

    gains = reorder(jnp.concatenate(gather_rel(norm_gains, "dp"), axis=1)).astype(f32)
    gain_one, gain_two = gains[0], gains[1]
    part = w_kv.shape[0] // n_tensor
    kv_shard = lax.dynamic_slice_in_dim(w_kv, tensor * part, part, axis=0)
    kv_all = gather_rows(gather_stacked(kv_shard, "dp"), "tensor").reshape(width, kv_cols)
    query_all = gather_stacked(gather_stacked(w_query, "dp"), "tensor").reshape(
        n_tensor, width, q_cols
    )
    out_all = gather_stacked(gather_stacked(w_out, "dp"), "tensor")

    inputs_f = inputs.astype(f32)
    h_one_sp = scaled_norm(inputs_f, gain_one).astype(bf16)
    h_one_rel = reorder(h_one_sp)

    packed = (rows, HEADS_KV, blocks, n_tensor, STRETCH, LANES)
    packed_kv = (rows, HEADS_KV, blocks, STRETCH, LANES)
    kv_raw, kv_own = pl.pallas_call(
        key_kernel,
        out_shape=(
            jax.ShapeDtypeStruct((sp_rows, kv_cols), f32),
            jax.ShapeDtypeStruct(packed_kv, bf16),
        ),
        compiler_params=pltpu.CompilerParams(vmem_limit_bytes=VMEM_LIMIT),
        name="key_value",
    )(h_one_rel, kv_all, cos, sin, k_gain)
    kv_pieces = gather_rel(kv_own, "dp")
    one_head = (sp_rows, HEAD)
    part_spec = pl.BlockSpec(
        (rows, HEADS_KV, blocks, 1, STRETCH, LANES), lambda s: (0, 0, 0, s, 0, 0)
    )
    q_raw, queries = pl.pallas_call(
        query_kernel,
        grid=(n_tensor,),
        in_specs=[
            whole((sp_rows, width)),
            pl.BlockSpec((1, width, q_cols), lambda s: (s, 0, 0)),
            whole(one_head),
            whole(one_head),
            whole((1, HEAD)),
        ],
        out_specs=(pl.BlockSpec((1, sp_rows, q_cols), lambda s: (s, 0, 0)), part_spec),
        out_shape=(
            jax.ShapeDtypeStruct((n_tensor, sp_rows, q_cols), f32),
            jax.ShapeDtypeStruct(packed, bf16),
        ),
        compiler_params=params(),
        name="query",
    )(h_one_rel, query_all, cos, sin, q_gain)

    q_spec = pl.BlockSpec(
        (1, 1, blocks, n_tensor, STRETCH, LANES), lambda i, h: (i, h, 0, 0, 0, 0)
    )
    kv_spec = pl.BlockSpec((1, 1, blocks, STRETCH, LANES), lambda i, h: (i, h, 0, 0, 0))
    limit_spec = pl.BlockSpec(
        (1, blocks, 1, n_tensor * STRETCH), lambda i, h: (i, 0, 0, 0)
    )
    pos_spec = pl.BlockSpec((1, SLOTS, 1), lambda i, h: (i, 0, 0))
    heads_packed = pl.pallas_call(
        attend_kernel,
        grid=(rows, HEADS_KV),
        in_specs=[q_spec, limit_spec, pos_spec] + [kv_spec] * n,
        out_specs=q_spec,
        out_shape=jax.ShapeDtypeStruct(packed, bf16),
        scratch_shapes=[pltpu.VMEM((SLOTS, LANES), bf16), pltpu.VMEM((LANES, SLOTS), bf16)],
        compiler_params=params(2),
        name="attend",
    )(queries, limit, key_pos, *kv_pieces)

    out_spec = pl.BlockSpec((n_tensor, 1, q_cols, cols), lambda r: (0, r, 0, 0))
    col_spec = pl.BlockSpec((1, sp_rows, cols), lambda r: (r, 0, 0))
    heads_shape = (n_tensor, sp_rows, q_cols)
    attn_rel, attn_heads = pl.pallas_call(
        out_kernel,
        grid=(n,),
        in_specs=[whole(packed), out_spec],
        out_specs=(col_spec, whole(heads_shape)),
        out_shape=(
            jax.ShapeDtypeStruct((n, sp_rows, cols), f32),
            jax.ShapeDtypeStruct(heads_shape, bf16),
        ),
        compiler_params=params(),
        name="out",
    )(heads_packed, out_all)
    attn = jnp.concatenate(
        [lax.dynamic_index_in_dim(attn_rel, dp ^ r, axis=0, keepdims=False) for r in range(n)],
        axis=1,
    )
    mixed = inputs_f + live * attn
    h_two_sp = scaled_norm(mixed, gain_two).astype(bf16)

    d_ffn_sp = cotangent * live.astype(bf16)
    d_ffn = gather_stacked(d_ffn_sp, "tensor").reshape(-1, width)
    h_two = gather_stacked(h_two_sp, "tensor").reshape(-1, width)
    down_all = lax.all_gather(w_down, "dp", axis=0).transpose(1, 0, 2).reshape(ff, width)
    ff_part = ff // FF_CHUNKS
    in_parts = [
        lax.all_gather(
            w_in[:, :, c * ff_part : (c + 1) * ff_part].reshape(cols, 2 * ff_part),
            "dp",
            axis=0,
            tiled=True,
        )
        for c in range(FF_CHUNKS)
    ]
    d_hidden = dot(d_ffn, down_all, contract_cols)

    def block_of(value, r):
        return lax.dynamic_slice_in_dim(value, (dp ^ r) * cols, cols, axis=1)

    hidden_parts, d_gate_up_parts, sum_in_parts = [], [], []
    for c in range(FF_CHUNKS):
        gate_up = dot(h_two, in_parts[c])
        gate, up = gate_up[:, :ff_part], gate_up[:, ff_part:]
        hidden_parts.append(silu_product(gate, up).astype(bf16))
        pull = jax.vjp(silu_product, gate, up)[1]
        d_gate, d_up = pull(d_hidden[:, c * ff_part : (c + 1) * ff_part])
        d_gate_up = jnp.concatenate([d_gate, d_up], axis=1).astype(bf16)
        d_gate_up_parts.append(d_gate_up)
        sum_in_parts.append(
            reduce_rel(
                lambda rs, d=d_gate_up: [dot(block_of(h_two, r), d, contract_rows) for r in rs],
                "dp",
            ).reshape(cols, 2, ff_part)
        )
    sum_in = jnp.concatenate(sum_in_parts, axis=2)
    hidden = jnp.concatenate(hidden_parts, axis=1)
    d_gate_up = jnp.concatenate(d_gate_up_parts, axis=1)
    in_all = jnp.concatenate(in_parts, axis=1)
    sum_down = reduce_rel(
        lambda rs: [dot(hidden, block_of(d_ffn, r), contract_rows) for r in rs], "dp"
    )

    def rows_of(value, s):
        return value[s * sp_rows : (s + 1) * sp_rows]

    d_h_two = reduce_rel(
        lambda ss: [dot(rows_of(d_gate_up, s), in_all, contract_cols) for s in ss], "tensor"
    )
    norm_two_pull = jax.vjp(scaled_norm, mixed, gain_two)[1]
    d_mixed_norm, d_gain_two = norm_two_pull(d_h_two)
    d_mixed = cotangent.astype(f32) + d_mixed_norm
    ffn = reduce_rel(lambda ss: [dot(rows_of(hidden, s), down_all) for s in ss], "tensor")
    outputs = (mixed + live * ffn).astype(bf16)

    d_attn_sp = (live * d_mixed).astype(bf16)
    d_attn_rel = jnp.stack([block_of(d_attn_sp, r) for r in range(n)])
    d_heads = pl.pallas_call(
        heads_back_kernel,
        grid=(n,),
        in_specs=[col_spec, out_spec],
        out_specs=whole(packed),
        out_shape=jax.ShapeDtypeStruct(packed, bf16),
        scratch_shapes=[pltpu.VMEM(heads_shape, f32)],
        compiler_params=params(),
        name="heads_back",
    )(d_attn_rel, out_all)
    d_query, *d_kv_pieces = pl.pallas_call(
        attend_back_kernel,
        grid=(rows, HEADS_KV),
        in_specs=[q_spec, q_spec, limit_spec, pos_spec] + [kv_spec] * n,
        out_specs=[q_spec] + [kv_spec] * n,
        out_shape=[jax.ShapeDtypeStruct(packed, f32)]
        + [jax.ShapeDtypeStruct(packed_kv, bf16)] * n,
        scratch_shapes=[
            pltpu.VMEM((SLOTS, LANES), bf16),
            pltpu.VMEM((LANES, SLOTS), bf16),
            pltpu.VMEM((SLOTS, LANES), f32),
        ],
        compiler_params=params(2),
        name="attend_back",
    )(queries, d_heads, limit, key_pos, *kv_pieces)
    d_kv = reduce_rel(lambda rs: [d_kv_pieces[r].astype(f32) for r in rs], "dp")
    d_q_low, d_q_gain = pl.pallas_call(
        query_back_kernel,
        grid=(n_tensor,),
        in_specs=[
            part_spec,
            pl.BlockSpec((1, sp_rows, q_cols), lambda s: (s, 0, 0)),
            whole(one_head),
            whole(one_head),
            whole((1, HEAD)),
        ],
        out_specs=(pl.BlockSpec((1, sp_rows, q_cols), lambda s: (s, 0, 0)), whole((1, HEAD))),
        out_shape=(
            jax.ShapeDtypeStruct((n_tensor, sp_rows, q_cols), bf16),
            jax.ShapeDtypeStruct((1, HEAD), f32),
        ),
        compiler_params=params(),
        name="query_back",
    )(d_query, q_raw, cos, sin, q_gain)
    d_kv_low, d_k_gain = pl.pallas_call(
        key_back_kernel,
        out_shape=(
            jax.ShapeDtypeStruct((sp_rows, kv_cols), bf16),
            jax.ShapeDtypeStruct((1, HEAD), f32),
        ),
        compiler_params=pltpu.CompilerParams(vmem_limit_bytes=VMEM_LIMIT),
        name="key_value_back",
    )(d_kv, kv_raw, cos, sin, k_gain)
    d_h_one_rel = pl.pallas_call(
        back_kernel,
        grid=(n_tensor,),
        in_specs=[
            pl.BlockSpec((1, sp_rows, q_cols), lambda s: (s, 0, 0)),
            pl.BlockSpec((1, width, q_cols), lambda s: (s, 0, 0)),
            whole((sp_rows, kv_cols)),
            whole((width, kv_cols)),
        ],
        out_specs=whole((sp_rows, width)),
        out_shape=jax.ShapeDtypeStruct((sp_rows, width), f32),
        compiler_params=params(),
        name="h_one_back",
    )(d_q_low, query_all, d_kv_low, kv_all)
    d_h_one = reorder(d_h_one_rel)
    norm_one_pull = jax.vjp(scaled_norm, inputs_f, gain_one)[1]
    d_inputs_norm, d_gain_one = norm_one_pull(d_h_one)
    grad_inputs = (d_mixed + d_inputs_norm).astype(bf16)

    h_one = gather_stacked(after(h_one_sp, h_two_sp), "tensor").reshape(-1, width)
    d_attn = gather_stacked(d_attn_sp, "tensor").reshape(-1, width)

    def to_owner(parts):
        return jnp.concatenate(
            [parts[0]] + [swap(parts[s], "tensor", s) for s in range(1, n_tensor)], axis=0
        )

    heads_mine = to_owner(attn_heads)
    d_q_mine = to_owner(d_q_low)
    kv_part = kv_cols // n_tensor
    d_kv_mine = to_owner(
        [
            lax.dynamic_slice_in_dim(d_kv_low, (tensor ^ s) * kv_part, kv_part, axis=1)
            for s in range(n_tensor)
        ]
    )
    sum_out = reduce_rel(
        lambda rs: [dot(heads_mine, block_of(d_attn, r), contract_rows) for r in rs], "dp"
    )
    sum_query = reduce_rel(
        lambda rs: [dot(block_of(h_one, r), d_q_mine, contract_rows) for r in rs], "dp"
    )
    sum_kv_part = reduce_rel(
        lambda rs: [dot(block_of(h_one, r), d_kv_mine, contract_rows) for r in rs], "dp"
    )
    sum_kv = gather_rows(sum_kv_part.astype(bf16), "tensor")
    sum_kv = sum_kv.transpose(1, 0, 2).reshape(cols, kv_cols) if False else jnp.concatenate(
        [sum_kv[s] for s in range(n_tensor)], axis=1
    )

    grad_gains = jnp.stack([d_gain_one, d_gain_two])
    small = jnp.concatenate([grad_gains, jnp.tile(jnp.concatenate([d_q_gain, d_k_gain]), (1, 2))], axis=1)
    small = sum(gather_rel(small, "tensor"))
    heads_sum = small[:, width : width + HEAD]
    sum_gains = block_of(small, 0)
    for r in range(1, n):
        sum_gains = sum_gains + swap(block_of(small, r), "dp", r)
    sum_heads = heads_sum
    for r in range(1, n):
        sum_heads = sum_heads + swap(heads_sum, "dp", r)
    return (
        outputs,
        grad_inputs,
        sum_query,
        sum_kv.astype(f32),
        sum_out,
        sum_in,
        sum_down,
        sum_gains,
        sum_heads,
    )


def solution(mesh):
    in_specs = (
        P(("dp", "tensor"), None),
        P(("dp", "tensor"), None),
        P("dp", "tensor"),
        P("dp", None),
        P("tensor", "dp"),
        P("dp", None, "tensor"),
        P("tensor", "dp"),
        P(None, "dp"),
        P(),
        P(),
        P(),
    )
    out_specs = (
        P(("dp", "tensor"), None),
        P(("dp", "tensor"), None),
        P("dp", "tensor"),
        P("dp", None),
        P("tensor", "dp"),
        P("dp", None, "tensor"),
        P("tensor", "dp"),
        P(None, "dp"),
        P(),
    )
    return jax.shard_map(local, mesh=mesh, in_specs=in_specs, out_specs=out_specs, check_vma=False)
```

```python
import functools

import jax
import jax.numpy as jnp
from jax import lax
from jax.experimental import layout
from jax.experimental import pallas as pl
from jax.experimental.pallas import tpu as pltpu
from jax.sharding import PartitionSpec as P

HEADS_KV = 5
HEAD = 64
SLOTS = 2048
STRETCH = 64
LANES = 128
FF_PARTS = (1, 1, 1, 1, 1, 1)
VMEM_LIMIT = 48 * 1024 * 1024
SMALL = pl.CostEstimate(flops=1000, bytes_accessed=1000, transcendentals=0)

eps_norm = 1e-06
rope_base = 10000.0
neg_large = -1e30
f32 = jnp.float32
bf16 = jnp.bfloat16
contract_rows = (((0,), (0,)), ((), ()))
contract_cols = (((1,), (1,)), ((), ()))


def dot(a, b, dims=(((1,), (0,)), ((), ()))):
    return lax.dot_general(a, b, dims, preferred_element_type=f32)


def after(value, *deps):
    return lax.optimization_barrier((value, *deps))[0]


def masks_of(axis):
    size = lax.axis_size(axis)
    bits = [1 << i for i in range(1, size.bit_length() - 1)]
    return bits + [1]


def order_of(axis):
    order = [0]
    for mask in masks_of(axis):
        order = order + [r ^ mask for r in order]
    return order


def swap(value, axis, mask):
    size = lax.axis_size(axis)
    return lax.ppermute(value, axis, [(i, i ^ mask) for i in range(size)])


def join(first, second):
    both = jnp.concatenate([first, second], axis=0)
    return layout.with_layout_constraint(both, layout.Layout(tuple(range(both.ndim))))


def gather(value, axis):
    stack = value[None]
    for mask in masks_of(axis):
        stack = join(stack, swap(stack, axis, mask))
    return stack


def gather_rows(value, axis):
    index = lax.axis_index(axis)
    stack = value
    size = lax.axis_size(axis)
    bit = size // 2
    at = value.ndim - 2
    while bit:
        other = swap(stack, axis, bit)
        upper = (index & bit) != 0
        stack = jnp.stack(
            [jnp.where(upper, other, stack), jnp.where(upper, stack, other)], axis=at
        )
        bit //= 2
        at += 1
    return stack.reshape(value.shape[:-2] + (size,) + value.shape[-2:])


def scatter(make, axis):
    half = lax.axis_size(axis)
    arrived = []
    for mask in reversed(masks_of(axis)):
        half //= 2
        sent = make(half, 2 * half, [x[half : 2 * half] for x in arrived], bf16)
        arrived = [x[:half] for x in arrived] + [swap(sent, axis, mask)]
    return make(0, 1, arrived, f32)[0]


def phases():
    masks = masks_of("dp")
    return [masks[:1], masks[1:-1], masks[-1:]]


class Item:
    late = ()

    def bring(self, value, axis, mask):
        got = swap(value, axis, mask)
        return after(got, *self.late) if self.late else got


class Gather(Item):
    def __init__(self, value):
        self.stack, self.halves, self.phase = value[None], None, 0

    def value(self):
        return self.stack

    def advance(self, value):
        for mask in phases()[self.phase]:
            got = self.bring(value, "dp", mask)
            self.halves = (value, got)
            value = join(value, got)
        self.stack = value
        self.phase += 1
        return got

    def pieces(self):
        half = order_of("dp")[: lax.axis_size("dp") // 2]
        return [(x, [r ^ m for r in half]) for x, m in zip(self.halves, (0, masks_of("dp")[-1]))]


class GatherLate(Item):
    def __init__(self, value):
        self.parts, self.phase = [(value[None], [0])], 0

    def value(self):
        return self.parts[max(self.phase - 2, 0)][0]

    def advance(self, value):
        masks = masks_of("dp")
        masks = [masks[-1:], masks[:1], masks[1:-1], masks[1:-1]][self.phase]
        at = max(self.phase - 2, 0)
        places = self.parts[at][1]
        for mask in masks:
            got = self.bring(value, "dp", mask)
            halves = [(value, places), (got, [r ^ mask for r in places])]
            places = places + halves[1][1]
            if mask != masks[-1] or self.phase == 0:
                value = join(value, got)
        if self.phase == 0:
            self.parts = [(value, places)]
        elif self.phase == 1:
            self.parts = halves
        elif self.phase == 2:
            self.parts, self.first = [None, self.parts[1]], halves
        else:
            self.parts = self.first + halves
        self.phase += 1
        return got

    def pieces(self):
        return self.parts


class Scatter(Item):
    def __init__(self, make):
        self.make, self.half, self.arrived, self.phase = make, lax.axis_size("dp"), [], 2

    def value(self):
        half = self.half // 2
        return self.make(half, 2 * half, [x[half : 2 * half] for x in self.arrived], bf16)

    def advance(self, value):
        for k, mask in enumerate(reversed(phases()[self.phase])):
            if k:
                value = self.value()
            self.half //= 2
            got = self.bring(value, "dp", mask)
            self.arrived = [x[: self.half] for x in self.arrived] + [got]
        self.phase -= 1
        return got

    def result(self):
        return self.make(0, 1, self.arrived, f32)[0]


class TensorGather(Item):
    def __init__(self, value):
        self.stack, self.masks = value[None], masks_of("tensor")

    def value(self):
        return self.stack

    def advance(self, value):
        got = self.bring(value, "tensor", self.masks[0])
        self.stack, self.masks = join(value, got), self.masks[1:]
        return got


class PairRows(Item):
    def __init__(self, value):
        self.stack = value

    def value(self):
        return self.stack

    def advance(self, value):
        got = self.bring(value, "tensor", 1)
        upper = (lax.axis_index("tensor") & 1) != 0
        self.stack = jnp.stack(
            [jnp.where(upper, got, value), jnp.where(upper, value, got)], axis=value.ndim - 2
        )
        return got


class TensorScatter(Item):
    def __init__(self, sums):
        self.sums, self.masks, self.arrived = sums, masks_of("tensor")[::-1], []

    def value(self):
        half = 1 << (len(self.masks) - 1)
        if half == self.sums[1].shape[0]:
            return self.sums[1]
        return plus(
            self.sums[0][half : 2 * half].astype(f32),
            [x[half : 2 * half] for x in self.arrived],
            bf16,
        )

    def advance(self, value):
        self.arrived.append(self.bring(value, "tensor", self.masks[0]))
        self.masks = self.masks[1:]
        return self.arrived[-1]

    def terms(self):
        return [self.sums[0], *self.arrived]


class TensorExchange(Item):
    def __init__(self, stack):
        self.stack, self.masks = stack[:, None], masks_of("tensor")

    def value(self):
        return self.stack[1::2]

    def advance(self, value):
        got = self.bring(value, "tensor", self.masks[0])
        self.stack = jnp.concatenate([self.stack[0::2], got], axis=1)
        self.masks = self.masks[1:]
        return got

    def rows(self):
        return self.stack.reshape((-1,) + self.stack.shape[3:])


class Direct(Item):
    def __init__(self, parts):
        self.parts = parts

    def value(self):
        return jnp.stack(self.parts)

    def advance(self, value):
        order = order_of("tensor")
        got = [value[0]] + [
            self.bring(value[p], "tensor", order[p]) for p in range(1, len(order))
        ]
        self.all = jnp.concatenate(got, axis=0)
        return self.all

    def rows(self):
        return self.all


class Rounds:
    def __init__(self):
        self.done = []

    def go(self, *items, ends=(), during=()):
        done = list(ends)
        for item in items:
            value = item.value()
            if self.done:
                value = after(value, *self.done)
            item.late = during
            done.append(item.advance(value))
        self.done = done


def plus(total, arrived, kind):
    for other in arrived:
        total = total + other.astype(f32)
    return total.astype(kind)


def scaled_norm(value_in, gain_vec):
    return (
        value_in
        * lax.rsqrt(jnp.mean(value_in * value_in, axis=-1, keepdims=True) + eps_norm)
        * gain_vec
    )


def silu_product(gate, up_part):
    return gate * jax.nn.sigmoid(gate) * up_part


def params(steps=1):
    return pltpu.CompilerParams(
        dimension_semantics=("arbitrary",) * steps, vmem_limit_bytes=VMEM_LIMIT
    )


def swap_halves(value):
    half = HEAD // 2
    return jnp.concatenate([value[:, half:], value[:, :half]], axis=1)


def rope_one(raw, gain, cos, sin, factor):
    scale = lax.rsqrt(jnp.mean(raw * raw, axis=-1, keepdims=True) + eps_norm)
    normed = raw * scale * gain
    return (normed * cos + swap_halves(normed) * sin) * factor


def rope_back(raw, gain, cos, sin, factor, grad):
    grad = grad * factor
    grad = grad * cos - swap_halves(grad) * sin
    scale = lax.rsqrt(jnp.mean(raw * raw, axis=-1, keepdims=True) + eps_norm)
    weighted = grad * gain
    back = scale * weighted - raw * (
        scale * scale * scale * jnp.mean(raw * weighted, axis=-1, keepdims=True)
    )
    return back, jnp.sum(grad * raw * scale, axis=0, keepdims=True)


def query_kernel(h_ref, w_ref, cos_ref, sin_ref, gain_ref, raw_ref, out_ref):
    cols = w_ref.shape[3]
    raw = sum(
        dot(h_ref[:, r * cols : (r + 1) * cols], w_ref[0, r], contract_cols)
        for r in range(w_ref.shape[1])
    )
    raw_ref[0] = raw
    rows, blocks = out_ref.shape[0], out_ref.shape[2]
    for h in range(HEADS_KV):
        turned = rope_one(
            raw[:, h * HEAD : (h + 1) * HEAD], gain_ref[...], cos_ref[...], sin_ref[...], 0.125
        )
        wide = jnp.concatenate([turned, jnp.zeros_like(turned)], axis=1).astype(bf16)
        out_ref[:, h, :, 0] = wide.reshape(rows, blocks, STRETCH, LANES)


def key_kernel(h_ref, w_ref, cos_ref, sin_ref, gain_ref, raw_ref, out_ref):
    raw = dot(h_ref[...], w_ref[...])
    raw_ref[...] = raw
    rows, blocks = out_ref.shape[0], out_ref.shape[2]
    for h in range(HEADS_KV):
        turned = rope_one(
            raw[:, h * HEAD : (h + 1) * HEAD], gain_ref[...], cos_ref[...], sin_ref[...], 1.0
        )
        start = (HEADS_KV + h) * HEAD
        wide = jnp.concatenate([turned, raw[:, start : start + HEAD]], axis=1).astype(bf16)
        out_ref[:, h] = wide.reshape(rows, blocks, STRETCH, LANES)


def load_keys(halves, kv, kvt):
    places = [(half, i) for half in halves for i in range(half.shape[0])]
    group = len(places) * STRETCH
    for g in range(halves[0].shape[3]):
        for r, (half, i) in enumerate(places):
            start = g * group + r * STRETCH
            kv[start : start + STRETCH, :] = half[i, 0, 0, g]
    kvt[...] = kv[...].T
    return group


def attend_kernel(q_ref, limit_ref, keypos_ref, low_ref, high_ref, out_ref, kv, kvt):
    blocks = q_ref.shape[2]
    group = load_keys((low_ref, high_ref), kv, kvt)
    for b in range(blocks):
        span = (b + 1) * group
        q = q_ref[0, 0, b].reshape(-1, LANES)
        scores = dot(kv[:span], q, contract_cols)
        scores = jnp.where(keypos_ref[0, :span] <= limit_ref[0, b], scores, neg_large)
        top = jnp.max(scores, axis=0, keepdims=True)
        weights = jnp.exp(scores - top)
        total = jnp.sum(weights, axis=0, keepdims=True)
        heads = dot(kvt[:, :span], weights.astype(bf16)) / total
        out_ref[0, 0, b] = heads.T.astype(bf16).reshape(q_ref.shape[3:])


def attend_back_kernel(
    q_ref, g_ref, limit_ref, keypos_ref, low_ref, high_ref, dq_ref, dlow_ref, dhigh_ref, kv, kvt, acc
):
    blocks = q_ref.shape[2]
    group = load_keys((low_ref, high_ref), kv, kvt)
    acc[...] = jnp.zeros_like(acc)
    for b in range(blocks):
        span = (b + 1) * group
        q = q_ref[0, 0, b].reshape(-1, LANES)
        grad = g_ref[0, 0, b].reshape(-1, LANES)
        scores = dot(kv[:span], q, contract_cols)
        scores = jnp.where(keypos_ref[0, :span] <= limit_ref[0, b], scores, neg_large)
        top = jnp.max(scores, axis=0, keepdims=True)
        weights = jnp.exp(scores - top)
        probs = weights * (1.0 / jnp.sum(weights, axis=0, keepdims=True))
        d_probs = dot(kv[:span], grad, contract_cols)
        delta = jnp.sum(probs * d_probs, axis=0, keepdims=True)
        d_scores = (probs * (d_probs - delta)).astype(bf16)
        dq = dot(kvt[:, :span], d_scores)
        dq_ref[0, 0, b] = dq.T.reshape(q_ref.shape[3:])
        acc[:span] += dot(d_scores, q) + dot(probs.astype(bf16), grad)
    count = dlow_ref.shape[0]
    for out, first in ((dlow_ref, 0), (dhigh_ref, count)):
        for r in range(count):
            for g in range(blocks):
                start = g * group + (first + r) * STRETCH
                out[r, 0, 0, g] = acc[start : start + STRETCH].astype(bf16)


def out_kernel(o_ref, w_ref, x_ref, live_ref, gain_ref, mixed_ref, h_ref, heads_ref):
    rows = heads_ref.shape[1]
    heads = jnp.concatenate(
        [o_ref[:, h, :, 0].reshape(rows, LANES)[:, HEAD:] for h in range(HEADS_KV)], axis=1
    )
    heads_ref[0] = heads
    cols = w_ref.shape[3]

    @pl.when(pl.program_id(0) == 0)
    def _():
        mixed_ref[...] = jnp.zeros_like(mixed_ref)

    for r in range(w_ref.shape[1]):
        mixed_ref[:, r * cols : (r + 1) * cols] += dot(heads, w_ref[0, r])

    @pl.when(pl.program_id(0) == pl.num_programs(0) - 1)
    def _():
        mixed = x_ref[...].astype(f32) + live_ref[...] * mixed_ref[...]
        mixed_ref[...] = mixed
        h_ref[...] = scaled_norm(mixed, gain_ref[...]).astype(bf16)


def norm_back(value, gain, grad):
    scale = lax.rsqrt(jnp.mean(value * value, axis=-1, keepdims=True) + eps_norm)
    weighted = grad * gain
    inner = jnp.mean(value * weighted, axis=-1, keepdims=True)
    back = scale * weighted - value * (scale * scale * scale * inner)
    return back, jnp.sum(grad * value * scale, axis=0, keepdims=True)


def mixed_back_kernel(mixed_ref, cot_ref, gain_ref, live_ref, *rest):
    terms, (d_mixed_ref, d_attn_ref, dgain_ref) = rest[:-3], rest[-3:]
    grad = sum(ref[0].astype(f32) for ref in terms)
    back, dgain_ref[...] = norm_back(mixed_ref[...], gain_ref[...], grad)
    d_mixed = cot_ref[...].astype(f32) + back
    d_mixed_ref[...] = d_mixed
    d_attn_ref[...] = (live_ref[...] * d_mixed).astype(bf16)


def heads_back_kernel(d_ref, w_ref, out_ref):
    cols = w_ref.shape[3]
    grad = sum(
        dot(d_ref[:, r * cols : (r + 1) * cols], w_ref[0, r], contract_cols)
        for r in range(w_ref.shape[1])
    )
    rows, blocks = out_ref.shape[0], out_ref.shape[2]
    for h in range(HEADS_KV):
        part = grad[:, h * HEAD : (h + 1) * HEAD]
        wide = jnp.concatenate([jnp.zeros_like(part), part], axis=1).astype(bf16)
        out_ref[:, h, :, 0] = wide.reshape(rows, blocks, STRETCH, LANES)


def query_back_kernel(dq_ref, raw_ref, cos_ref, sin_ref, gain_ref, out_ref, dgain_ref):
    @pl.when(pl.program_id(0) == 0)
    def _():
        dgain_ref[...] = jnp.zeros_like(dgain_ref)

    raw = raw_ref[0]
    parts = []
    for h in range(HEADS_KV):
        grad = dq_ref[:, h, :, 0].reshape(raw.shape[0], LANES)[:, :HEAD]
        back, dgain = rope_back(
            raw[:, h * HEAD : (h + 1) * HEAD],
            gain_ref[...],
            cos_ref[...],
            sin_ref[...],
            0.125,
            grad,
        )
        parts.append(back)
        dgain_ref[...] += dgain
    out_ref[0] = jnp.concatenate(parts, axis=1).astype(bf16)


def key_back_kernel(sum_ref, raw_ref, cos_ref, sin_ref, gain_ref, out_ref, dgain_ref):
    raw = raw_ref[...]
    keys, values = [], []
    total = jnp.zeros_like(dgain_ref)
    for h in range(HEADS_KV):
        both = sum_ref[:, h].reshape(raw.shape[0], LANES)
        back, dgain = rope_back(
            raw[:, h * HEAD : (h + 1) * HEAD],
            gain_ref[...],
            cos_ref[...],
            sin_ref[...],
            1.0,
            both[:, :HEAD],
        )
        keys.append(back)
        values.append(both[:, HEAD:])
        total = total + dgain
    dgain_ref[...] = total
    out_ref[...] = jnp.concatenate(keys + values, axis=1).astype(bf16)


def back_kernel(
    dq_ref, wq_ref, dkv_ref, wkv_ref, x_ref, gain_ref, d_mixed_ref, out_ref, dgain_ref, acc
):
    @pl.when(pl.program_id(0) == 0)
    def _():
        acc[...] = dot(dkv_ref[...], wkv_ref[...], contract_cols)

    cols = wq_ref.shape[3]
    for r in range(wq_ref.shape[1]):
        acc[:, r * cols : (r + 1) * cols] += dot(dq_ref[0], wq_ref[0, r])

    @pl.when(pl.program_id(0) == pl.num_programs(0) - 1)
    def _():
        back, dgain_ref[...] = norm_back(x_ref[...].astype(f32), gain_ref[...], acc[...])
        out_ref[...] = (d_mixed_ref[...] + back).astype(bf16)


def shards_kernel(in_ref, down_ref, query_ref, *refs):
    parts, query_out_ref = refs[:-1], refs[-1]
    ff = down_ref.shape[0]
    start = 0
    for ref in parts:
        part = ref.shape[1] // 3
        ref[:, :part] = in_ref[:, start : start + part]
        ref[:, part : 2 * part] = in_ref[:, ff + start : ff + start + part]
        ref[:, 2 * part :] = down_ref[start : start + part, :].T
        start += part
    query_out_ref[...] = query_ref[...].T


def columns_kernel(order, back, index_ref, *refs):
    count = len(refs) // 2
    index = index_ref[0]
    size = len(order)
    for x_ref, o_ref in zip(refs[:count], refs[count:]):
        cols = x_ref.shape[1] // size

        def pick(value, places):
            return jnp.concatenate(
                [value[:, p * cols : (p + 1) * cols] for p in places], axis=1
            )

        value = x_ref[...].astype(f32)
        if back:
            value = pick(value, [order.index(i) for i in range(size)])
        bit = 1
        while bit < size:
            value = jnp.where(
                (index & bit) != 0, pick(value, [i ^ bit for i in range(size)]), value
            )
            bit *= 2
        if not back:
            value = pick(value, order)
        o_ref[...] = value.astype(o_ref.dtype)


def pick_columns(ref, places, cols):
    if places == list(range(places[0], places[0] + len(places))):
        return ref[:, places[0] * cols : (places[-1] + 1) * cols]
    return jnp.concatenate([ref[:, p * cols : (p + 1) * cols] for p in places], axis=1)


def hidden_kernel(all_places, h_ref, d_ref, *refs):
    pieces, (hidden_ref, d_gate_up_ref, turned_ref) = refs[:-3], refs[-3:]
    part = hidden_ref.shape[1]
    gate_up = d_hidden = None
    for places, ref in zip(all_places, pieces):
        cols = ref.shape[0] // len(places)
        first = dot(pick_columns(h_ref, places, cols), ref[:, : 2 * part])
        second = dot(pick_columns(d_ref, places, cols), ref[:, 2 * part :])
        gate_up = first if gate_up is None else gate_up + first
        d_hidden = second if d_hidden is None else d_hidden + second
    gate, up = gate_up[:, :part], gate_up[:, part:]
    sig = jax.nn.sigmoid(gate)
    swish = gate * sig
    hidden = (swish * up).astype(bf16)
    d_gate = (d_hidden * up * (sig + swish * (1.0 - sig))).astype(bf16)
    d_up = (d_hidden * swish).astype(bf16)
    hidden_ref[...] = hidden
    d_gate_up_ref[:, :part] = d_gate
    d_gate_up_ref[:, part:] = d_up
    turned_ref[:part] = d_gate.T
    turned_ref[part : 2 * part] = d_up.T
    turned_ref[2 * part :] = hidden.T


def grads_kernel(h_ref, d_ref, turned_ref, low_ref, high_ref):
    split = turned_ref.shape[0] // 3 * 2
    first = dot(turned_ref[:split], h_ref[...]).astype(bf16)
    second = dot(turned_ref[split:], d_ref[...]).astype(bf16)
    low = pl.program_id(0) < pl.num_programs(0) // 2
    for out_ref, here in ((low_ref, low), (high_ref, jnp.logical_not(low))):

        @pl.when(here)
        def _(out_ref=out_ref):
            out_ref[0, :split] = first
            out_ref[0, split:] = second


def back_sum_kernel(all_places, *refs):
    count = len(all_places)
    half = refs[-1].shape[1] // 2
    totals = [None, None]
    at = count
    for c, pieces in enumerate(all_places):
        terms = [dot(refs[c][...], refs[at + i][...], contract_cols) for i in range(len(pieces))]
        at += len(pieces)
        if len(pieces) > 2:
            blocks = {}
            for places, term in zip(pieces, terms):
                cols = term.shape[1] // len(places)
                for i, p in enumerate(places):
                    blocks[p] = term[:, i * cols : (i + 1) * cols]
            middle = len(blocks) // 2
            terms = [
                jnp.concatenate([blocks[side * middle + i] for i in range(middle)], axis=1)
                for side in range(2)
            ]
        totals = [t if old is None else old + t for old, t in zip(totals, terms)]
    low = pl.program_id(0) < pl.num_programs(0) // 2
    for out_ref, here in ((refs[-2], low), (refs[-1], jnp.logical_not(low))):

        @pl.when(here)
        def _(out_ref=out_ref):
            for side in range(2):
                out_ref[:, side * half : (side + 1) * half] = totals[side].astype(bf16)


def whole(shape):
    return pl.BlockSpec(shape, lambda *_: (0,) * len(shape))


def local(
    inputs,
    cotangent,
    w_query,
    w_kv,
    w_out,
    w_in,
    w_down,
    norm_gains,
    head_gains,
    lengths,
    slot_blocks,
):
    sp_rows, width = inputs.shape
    n = lax.axis_size("dp")
    n_tensor = lax.axis_size("tensor")
    dp = lax.axis_index("dp")
    tensor = lax.axis_index("tensor")
    seq_count = lengths.shape[0]
    row_span = sp_rows * n_tensor // seq_count
    blocks = row_span // STRETCH
    rows = sp_rows // row_span
    per_row = SLOTS // STRETCH
    cols = width // n
    q_cols = w_query.shape[1]
    kv_cols = w_kv.shape[1]
    ff = w_down.shape[0]
    order = order_of("dp")
    tensor_order = order_of("tensor")
    rels = jnp.array(order, jnp.int32)

    def columns(back, *values):
        return pl.pallas_call(
            functools.partial(columns_kernel, tuple(order), back),
            in_specs=[pl.BlockSpec(memory_space=pltpu.SMEM)]
            + [pl.BlockSpec(memory_space=pltpu.VMEM)] * len(values),
            out_shape=[jax.ShapeDtypeStruct(v.shape, bf16) for v in values],
            compiler_params=pltpu.CompilerParams(vmem_limit_bytes=VMEM_LIMIT),
            cost_estimate=SMALL,
        name="columns",
        )(dp.reshape(1), *values)

    table = slot_blocks.reshape(n, n_tensor, rows, blocks)
    mine = lax.dynamic_index_in_dim(table, tensor, axis=1, keepdims=False)[dp ^ rels]
    inside = jnp.arange(STRETCH, dtype=jnp.int32)
    key_pos = (mine % per_row * STRETCH)[..., None] + inside
    own_pos = key_pos[0]
    own_len = lengths[mine[0] // per_row][..., None]
    live = (own_pos < own_len).astype(f32).reshape(sp_rows, 1)
    limit = jnp.minimum(own_pos, own_len - 1)
    limit = jnp.broadcast_to(limit[:, :, None, None, :], (rows, blocks, 1, n_tensor, STRETCH))
    limit = limit.reshape(rows, blocks, 1, n_tensor * STRETCH)
    key_pos = key_pos.transpose(1, 2, 0, 3).reshape(rows, SLOTS, 1)
    half = HEAD // 2
    frequency = rope_base ** (-2.0 * jnp.arange(half, dtype=f32) / HEAD)
    angles = own_pos.reshape(sp_rows, 1).astype(f32) * frequency
    cosine, sine = jnp.cos(angles), jnp.sin(angles)
    cos = jnp.concatenate([cosine, cosine], axis=1)
    sin = jnp.concatenate([-sine, sine], axis=1)
    head_float = head_gains.astype(f32)
    q_gain, k_gain = head_float[0:1], head_float[1:2]

    inputs, cotangent = columns(False, inputs, cotangent)
    inputs_f = inputs.astype(f32)
    part = w_kv.shape[0] // 2
    kv_shard = lax.dynamic_slice_in_dim(w_kv, (tensor & 1) * part, part, axis=0)
    unit = ff // sum(FF_PARTS)
    sizes = [size * unit for size in FF_PARTS]
    *shards, query_shard = pl.pallas_call(
        shards_kernel,
        out_shape=[jax.ShapeDtypeStruct((cols, 3 * part), bf16) for part in sizes]
        + [jax.ShapeDtypeStruct((q_cols, cols), bf16)],
        compiler_params=pltpu.CompilerParams(vmem_limit_bytes=VMEM_LIMIT),
        cost_estimate=SMALL,
        name="shards",
    )(w_in.reshape(cols, 2 * ff), w_down, w_query)
    link = Rounds()
    g_kv, g_gains = Gather(kv_shard), Gather(norm_gains)
    g_query, g_out = Gather(query_shard), Gather(w_out)
    g_ff = [Gather(x) for x in shards[:-1]] + [GatherLate(shards[-1])]
    link.go(g_kv, g_query, g_gains)
    link.go(g_kv, g_gains, g_out, g_ff[0])
    link.go(g_kv, g_gains, g_query)
    gains = g_gains.stack.transpose(1, 0, 2).reshape(2, width).astype(f32)
    gain_one, gain_two = gains[0], gains[1]
    h_one = scaled_norm(inputs_f, gain_one).astype(bf16)
    t_kv = PairRows(g_kv.stack)
    link.go(t_kv, g_query, g_out, g_ff[5])
    t_query = TensorGather(g_query.stack)
    kv_all = t_kv.stack.reshape(width, kv_cols)
    t_d_ffn = TensorGather(cotangent * live.astype(bf16))

    packed = (rows, HEADS_KV, blocks, n_tensor, STRETCH, LANES)
    packed_kv = (rows, HEADS_KV, blocks, STRETCH, LANES)
    both_spec = pl.BlockSpec((1, n, q_cols, cols), lambda s: (s, 0, 0, 0))
    kv_raw, kv_own = pl.pallas_call(
        key_kernel,
        out_shape=(
            jax.ShapeDtypeStruct((sp_rows, kv_cols), f32),
            jax.ShapeDtypeStruct(packed_kv, bf16),
        ),
        compiler_params=pltpu.CompilerParams(vmem_limit_bytes=VMEM_LIMIT),
        cost_estimate=SMALL,
        name="key_value",
    )(h_one, kv_all, cos, sin, k_gain)
    g_keys = Gather(kv_own)
    link.go(t_query, g_out, g_ff[0], g_keys)
    t_out = TensorGather(g_out.stack)
    link.go(t_query, t_out, g_keys, g_ff[0], g_ff[1])
    query_all = t_query.stack
    one_head = (sp_rows, HEAD)
    part_spec = pl.BlockSpec(
        (rows, HEADS_KV, blocks, 1, STRETCH, LANES), lambda s: (0, 0, 0, s, 0, 0)
    )
    q_raw, queries = pl.pallas_call(
        query_kernel,
        grid=(n_tensor,),
        in_specs=[
            whole((sp_rows, width)),
            both_spec,
            whole(one_head),
            whole(one_head),
            whole((1, HEAD)),
        ],
        out_specs=(pl.BlockSpec((1, sp_rows, q_cols), lambda s: (s, 0, 0)), part_spec),
        out_shape=(
            jax.ShapeDtypeStruct((n_tensor, sp_rows, q_cols), f32),
            jax.ShapeDtypeStruct(packed, bf16),
        ),
        compiler_params=params(),
        cost_estimate=SMALL,
        name="query",
    )(h_one, query_all, cos, sin, q_gain)
    link.go(t_out, t_d_ffn, g_keys, g_ff[1], g_ff[2], during=[queries])
    out_all = t_out.stack
    kv_halves = g_keys.halves
    q_spec = pl.BlockSpec(
        (1, 1, blocks, n_tensor, STRETCH, LANES), lambda i, h: (i, h, 0, 0, 0, 0)
    )
    kv_spec = pl.BlockSpec(
        (n // 2, 1, 1, blocks, STRETCH, LANES), lambda i, h: (0, i, h, 0, 0, 0)
    )
    limit_spec = pl.BlockSpec(
        (1, blocks, 1, n_tensor * STRETCH), lambda i, h: (i, 0, 0, 0)
    )
    pos_spec = pl.BlockSpec((1, SLOTS, 1), lambda i, h: (i, 0, 0))
    heads_packed = pl.pallas_call(
        attend_kernel,
        grid=(rows, HEADS_KV),
        in_specs=[q_spec, limit_spec, pos_spec] + [kv_spec] * 2,
        out_specs=q_spec,
        out_shape=jax.ShapeDtypeStruct(packed, bf16),
        scratch_shapes=[pltpu.VMEM((SLOTS, LANES), bf16), pltpu.VMEM((LANES, SLOTS), bf16)],
        compiler_params=params(2),
        cost_estimate=SMALL,
        name="attend",
    )(queries, limit, key_pos, *kv_halves)

    heads_shape = (n_tensor, sp_rows, q_cols)
    head_spec = pl.BlockSpec((1, sp_rows, q_cols), lambda s: (s, 0, 0))
    square = whole((sp_rows, width))
    mixed, h_two_own, attn_heads = pl.pallas_call(
        out_kernel,
        grid=(n_tensor,),
        in_specs=[part_spec, both_spec, square, whole((sp_rows, 1)), whole((1, width))],
        out_specs=(square, square, head_spec),
        out_shape=(
            jax.ShapeDtypeStruct((sp_rows, width), f32),
            jax.ShapeDtypeStruct((sp_rows, width), bf16),
            jax.ShapeDtypeStruct(heads_shape, bf16),
        ),
        compiler_params=params(),
        cost_estimate=SMALL,
        name="out",
    )(heads_packed, out_all, inputs, live, gain_two[None])
    t_heads = TensorExchange(attn_heads)

    t_h_two = TensorGather(h_two_own)
    t_h_one = TensorGather(h_one)
    rows_all = sp_rows * n_tensor
    link.go(t_d_ffn, g_ff[1], g_ff[2], g_ff[3], during=[h_two_own])
    d_ffn = t_d_ffn.stack.reshape(-1, width)
    link.go(t_h_two, g_ff[2], g_ff[3], g_ff[4])
    link.go(t_h_two, t_h_one, g_ff[3], g_ff[4], g_ff[5])
    h_two = t_h_two.stack.reshape(-1, width)
    row_spec = pl.BlockSpec((sp_rows, width), lambda i: (i, 0))
    row_block = lambda span: pl.BlockSpec((sp_rows, span), lambda i: (i, 0))
    weights, hiddens, d_gate_ups, turned = [], [], [], []

    def hidden_part(g, part):
        pieces = [
            (x.reshape(len(rs) * cols, 3 * part), [order.index(r) for r in rs])
            for x, rs in g.pieces()
        ]
        weights.append(pieces)
        hidden, d_gate_up, flipped = pl.pallas_call(
            functools.partial(hidden_kernel, [places for _, places in pieces]),
            grid=(n_tensor,),
            in_specs=[row_spec, row_spec] + [whole(x.shape) for x, _ in pieces],
            out_specs=(
                row_block(part),
                row_block(2 * part),
                pl.BlockSpec((3 * part, sp_rows), lambda i: (0, i)),
            ),
            out_shape=(
                jax.ShapeDtypeStruct((rows_all, part), bf16),
                jax.ShapeDtypeStruct((rows_all, 2 * part), bf16),
                jax.ShapeDtypeStruct((3 * part, rows_all), bf16),
            ),
            compiler_params=params(),
            cost_estimate=SMALL,
        name="hidden",
        )(h_two, d_ffn, *[x for x, _ in pieces])
        hiddens.append(hidden)
        d_gate_ups.append(d_gate_up)
        turned.append(flipped)

    def grads_of(flipped):
        wide = flipped.shape[0]
        count = width // 256
        low_spec = pl.BlockSpec((1, wide, 256), lambda j: (jnp.minimum(j, count // 2 - 1), 0, 0))
        high_spec = pl.BlockSpec((1, wide, 256), lambda j: (jnp.maximum(j - count // 2, 0), 0, 0))
        block = pl.BlockSpec((rows_all, 256), lambda j: (0, j))
        halves = pl.pallas_call(
            grads_kernel,
            grid=(count,),
            in_specs=[block, block, whole(flipped.shape)],
            out_specs=(low_spec, high_spec),
            out_shape=[jax.ShapeDtypeStruct((count // 2, wide, 256), bf16)] * 2,
            compiler_params=params(),
            cost_estimate=SMALL,
            name="weight_grads",
        )(h_two, d_ffn, flipped)
        if cols != 256:
            halves = [
                x.reshape(count // 2, wide, 256 // cols, cols)
                .transpose(0, 2, 1, 3)
                .reshape(n // 2, wide, cols)
                for x in halves
            ]

        def make(begin, end, arrived, kind):
            if begin >= n // 2:
                return halves[1]
            return plus(halves[0][begin:end].astype(f32), arrived, kind)

        return Scatter(make), halves[1]

    s_ff, sent = [], []

    def add_grads(c):
        item, first = grads_of(turned[c])
        s_ff.append(item)
        sent.append(first)

    def back_sum(parts, down):
        def weight_spec(x, w):
            span = x.shape[1]
            at = (w.shape[1] - span) // span if down else 0
            return pl.BlockSpec(
                (w.shape[0], span), lambda i: (0, at), pipeline_mode=pl.Buffered(1)
            )

        return pl.pallas_call(
            functools.partial(
                back_sum_kernel, [[places for _, places in pieces] for pieces in weights]
            ),
            grid=(n_tensor,),
            in_specs=[row_block(x.shape[1]) for x in parts]
            + [weight_spec(x, w) for x, pieces in zip(parts, weights) for w, _ in pieces],
            out_specs=(
                pl.BlockSpec((sp_rows, width), lambda i: (jnp.minimum(i, n_tensor // 2 - 1), 0)),
                pl.BlockSpec((sp_rows, width), lambda i: (jnp.maximum(i - n_tensor // 2, 0), 0)),
            ),
            out_shape=[jax.ShapeDtypeStruct((rows_all // 2, width), bf16)] * 2,
            compiler_params=params(),
            cost_estimate=SMALL,
            name="back_sum",
        )(*parts, *[w for pieces in weights for w, _ in pieces])

    def row_sums(parts, down):
        return TensorScatter(
            [x.reshape(n_tensor // 2, sp_rows, width) for x in back_sum(parts, down)]
        )

    hidden_part(g_ff[0], sizes[0])
    hidden_part(g_ff[1], sizes[1])
    add_grads(0)
    link.go(t_h_one, t_heads, g_ff[4], g_ff[5], during=[*turned, *sent])
    h_one_all = t_h_one.stack.reshape(-1, width)
    hidden_part(g_ff[2], sizes[2])
    hidden_part(g_ff[3], sizes[3])
    add_grads(1)
    add_grads(2)
    link.go(t_heads, s_ff[0], g_ff[5], during=[*turned[2:], *sent[1:]])
    hidden_part(g_ff[4], sizes[4])
    hidden_part(g_ff[5], sizes[5])
    t_back = row_sums(d_gate_ups, False)
    link.go(s_ff[1], s_ff[0], during=t_back.sums)
    add_grads(3)
    add_grads(4)
    t_ffn = row_sums(hiddens, True)
    link.go(t_back, s_ff[2], s_ff[1], s_ff[0], during=[*t_ffn.sums, *sent[3:]])
    add_grads(5)
    link.go(t_back, t_ffn, s_ff[3], s_ff[2], s_ff[1], during=sent[5:])
    first_spec = pl.BlockSpec((1, sp_rows, width), lambda i: (0, 0, 0))
    back_terms = t_back.terms()
    d_mixed, d_attn_own, d_gain_two = pl.pallas_call(
        mixed_back_kernel,
        grid=(1,),
        in_specs=[square, square, whole((1, width)), whole((sp_rows, 1))]
        + [first_spec] * len(back_terms),
        out_specs=(square, square, whole((1, width))),
        out_shape=(
            jax.ShapeDtypeStruct((sp_rows, width), f32),
            jax.ShapeDtypeStruct((sp_rows, width), bf16),
            jax.ShapeDtypeStruct((1, width), f32),
        ),
        compiler_params=params(),
        cost_estimate=SMALL,
        name="mixed_back",
    )(mixed, cotangent, gain_two[None], live, *back_terms)

    d_heads = pl.pallas_call(
        heads_back_kernel,
        grid=(n_tensor,),
        in_specs=[whole((sp_rows, width)), both_spec],
        out_specs=part_spec,
        out_shape=jax.ShapeDtypeStruct(packed, bf16),
        compiler_params=params(),
        cost_estimate=SMALL,
        name="heads_back",
    )(d_attn_own, out_all)
    d_query, d_low, d_high = pl.pallas_call(
        attend_back_kernel,
        grid=(rows, HEADS_KV),
        in_specs=[q_spec, q_spec, limit_spec, pos_spec] + [kv_spec] * 2,
        out_specs=[q_spec] + [kv_spec] * 2,
        out_shape=[jax.ShapeDtypeStruct(packed, f32)]
        + [jax.ShapeDtypeStruct((n // 2,) + packed_kv, bf16)] * 2,
        scratch_shapes=[
            pltpu.VMEM((SLOTS, LANES), bf16),
            pltpu.VMEM((LANES, SLOTS), bf16),
            pltpu.VMEM((SLOTS, LANES), f32),
        ],
        compiler_params=params(2),
        cost_estimate=SMALL,
        name="attend_back",
    )(queries, d_heads, limit, key_pos, *kv_halves)

    def key_grads(begin, end, arrived, kind):
        if begin >= n // 2:
            return d_high
        return plus(d_low[begin:end].astype(f32), arrived, kind)

    s_keys = Scatter(key_grads)
    t_attn = TensorGather(d_attn_own)
    d_q_low, d_q_gain = pl.pallas_call(
        query_back_kernel,
        grid=(n_tensor,),
        in_specs=[part_spec, head_spec, whole(one_head), whole(one_head), whole((1, HEAD))],
        out_specs=(head_spec, whole((1, HEAD))),
        out_shape=(
            jax.ShapeDtypeStruct(heads_shape, bf16),
            jax.ShapeDtypeStruct((1, HEAD), f32),
        ),
        compiler_params=params(),
        cost_estimate=SMALL,
        name="query_back",
    )(d_query, q_raw, cos, sin, q_gain)

    def product(left, right):
        def make(begin, end, arrived, kind):
            rows_here = left[:, begin * cols : end * cols]
            total = dot(rows_here, right, contract_rows).reshape(end - begin, cols, -1)
            return plus(total, arrived, kind)

        return make

    t_query_back = TensorExchange(d_q_low)
    link.go(t_ffn, s_ff[4], s_ff[3], s_ff[2], during=[d_query])
    link.go(t_attn, t_query_back, s_keys, s_ff[4], s_ff[3], during=[d_q_low])
    ffn = sum(x[0].astype(f32) for x in t_ffn.terms())
    (outputs,) = columns(True, (mixed + live * ffn).astype(bf16))
    link.go(t_attn, t_query_back, s_keys, s_ff[5], s_ff[4], during=[outputs])
    d_attn = t_attn.stack.reshape(-1, width)
    s_out = Scatter(product(d_attn, t_heads.rows()))
    s_query = Scatter(product(h_one_all, t_query_back.rows()))
    link.go(s_keys, s_out)
    d_kv = s_keys.result()
    d_kv_low, d_k_gain = pl.pallas_call(
        key_back_kernel,
        out_shape=(
            jax.ShapeDtypeStruct((sp_rows, kv_cols), bf16),
            jax.ShapeDtypeStruct((1, HEAD), f32),
        ),
        compiler_params=pltpu.CompilerParams(vmem_limit_bytes=VMEM_LIMIT),
        cost_estimate=SMALL,
        name="key_value_back",
    )(d_kv, kv_raw, cos, sin, k_gain)
    kv_part = kv_cols // n_tensor
    t_kv_back = Direct(
        [
            lax.dynamic_slice_in_dim(d_kv_low, (tensor ^ s) * kv_part, kv_part, axis=1)
            for s in tensor_order
        ]
    )
    grad_rel, d_gain_one = pl.pallas_call(
        back_kernel,
        grid=(n_tensor,),
        in_specs=[
            head_spec,
            both_spec,
            whole((sp_rows, kv_cols)),
            whole((width, kv_cols)),
            square,
            whole((1, width)),
            square,
        ],
        out_specs=(square, whole((1, width))),
        out_shape=(
            jax.ShapeDtypeStruct((sp_rows, width), bf16),
            jax.ShapeDtypeStruct((1, width), f32),
        ),
        scratch_shapes=[pltpu.VMEM((sp_rows, width), f32)],
        compiler_params=params(),
        cost_estimate=SMALL,
        name="h_one_back",
    )(d_q_low, query_all, d_kv_low, kv_all, inputs, gain_one[None], d_mixed)
    link.go(t_kv_back, s_query, s_out, during=[grad_rel])
    (grad_inputs,) = columns(True, grad_rel)

    gain_parts = jnp.concatenate([d_gain_one, d_gain_two]).reshape(2, n, cols)
    gain_parts = gain_parts.transpose(1, 0, 2).reshape(n, 2 * cols)
    head_parts = jnp.broadcast_to(
        jnp.concatenate([d_q_gain, d_k_gain]).reshape(1, 2 * HEAD), (n, 2 * HEAD)
    )
    small_parts = jnp.concatenate([gain_parts, head_parts], axis=1)
    extra = -(-small_parts.shape[1] // kv_part)
    small_parts = jnp.pad(
        small_parts, ((0, 0), (0, extra * kv_part - small_parts.shape[1]))
    ).reshape(n, extra, kv_part)
    kv_product = product(h_one_all, t_kv_back.rows())

    def kv_grads(begin, end, arrived, kind):
        own = jnp.concatenate([kv_product(begin, end, [], f32), small_parts[begin:end]], axis=1)
        return plus(own, arrived, kind)

    s_kv = Scatter(kv_grads)
    link.go(s_kv, s_query, s_out)
    link.go(s_kv, s_query, s_ff[5])
    link.go(s_kv, s_ff[5])
    sum_kv = s_kv.result()
    t_small = TensorGather(sum_kv[cols:])
    t_sums = TensorGather(sum_kv[:cols].astype(bf16))
    link.go(t_small, t_sums)
    link.go(t_small, t_sums)
    small = jnp.sum(t_small.stack, axis=0).reshape(-1)
    sum_gains = small[: 2 * cols].reshape(2, cols)
    sum_heads = small[2 * cols : 2 * cols + 2 * HEAD].reshape(2, HEAD)
    stack = t_sums.stack
    sum_kv = jnp.concatenate(
        [
            lax.dynamic_index_in_dim(
                stack, places[i], axis=0, keepdims=False
            )
            for places in [jnp.argsort(tensor ^ jnp.array(tensor_order, jnp.int32))]
            for i in range(n_tensor)
        ],
        axis=1,
    )
    sum_out = s_out.result().T
    sum_query = s_query.result()
    sums = [s.result() for s in s_ff]
    sum_in = jnp.concatenate(
        [x[: 2 * part].reshape(2, part, cols) for part, x in zip(sizes, sums)], axis=1
    ).transpose(2, 0, 1)
    sum_down = jnp.concatenate([x[2 * part :] for part, x in zip(sizes, sums)], axis=0)
    return (
        outputs,
        grad_inputs,
        sum_query,
        sum_kv.astype(f32),
        sum_out,
        sum_in,
        sum_down,
        sum_gains,
        sum_heads,
    )


def solution(mesh):
    in_specs = (
        P(("dp", "tensor"), None),
        P(("dp", "tensor"), None),
        P("dp", "tensor"),
        P("dp", None),
        P("tensor", "dp"),
        P("dp", None, "tensor"),
        P("tensor", "dp"),
        P(None, "dp"),
        P(),
        P(),
        P(),
    )
    out_specs = (
        P(("dp", "tensor"), None),
        P(("dp", "tensor"), None),
        P("dp", "tensor"),
        P("dp", None),
        P("tensor", "dp"),
        P("dp", None, "tensor"),
        P("tensor", "dp"),
        P(None, "dp"),
        P(),
    )
    return jax.shard_map(local, mesh=mesh, in_specs=in_specs, out_specs=out_specs, check_vma=False)
```

```python
import functools

import jax
import jax.numpy as jnp
from jax import lax
from jax.experimental import layout
from jax.experimental import pallas as pl
from jax.experimental.pallas import tpu as pltpu
from jax.sharding import PartitionSpec as P

HEADS_KV = 5
HEAD = 64
SLOTS = 2048
STRETCH = 64
LANES = 128
FF_PARTS = (1, 1, 1, 1, 1, 1)
VMEM_LIMIT = 48 * 1024 * 1024
SMALL = pl.CostEstimate(flops=1000, bytes_accessed=1000, transcendentals=0)

eps_norm = 1e-06
rope_base = 10000.0
neg_large = -1e30
f32 = jnp.float32
bf16 = jnp.bfloat16
contract_rows = (((0,), (0,)), ((), ()))
contract_cols = (((1,), (1,)), ((), ()))


def dot(a, b, dims=(((1,), (0,)), ((), ()))):
    return lax.dot_general(a, b, dims, preferred_element_type=f32)


def after(value, *deps):
    return lax.optimization_barrier((value, *deps))[0]


def masks_of(axis):
    size = lax.axis_size(axis)
    bits = [1 << i for i in range(1, size.bit_length() - 1)]
    return bits + [1]


def order_of(axis):
    order = [0]
    for mask in masks_of(axis):
        order = order + [r ^ mask for r in order]
    return order


def swap(value, axis, mask):
    size = lax.axis_size(axis)
    return lax.ppermute(value, axis, [(i, i ^ mask) for i in range(size)])


def join(first, second):
    both = jnp.concatenate([first, second], axis=0)
    return layout.with_layout_constraint(both, layout.Layout(tuple(range(both.ndim))))


def gather(value, axis):
    stack = value[None]
    for mask in masks_of(axis):
        stack = join(stack, swap(stack, axis, mask))
    return stack


def gather_rows(value, axis):
    index = lax.axis_index(axis)
    stack = value
    size = lax.axis_size(axis)
    bit = size // 2
    at = value.ndim - 2
    while bit:
        other = swap(stack, axis, bit)
        upper = (index & bit) != 0
        stack = jnp.stack(
            [jnp.where(upper, other, stack), jnp.where(upper, stack, other)], axis=at
        )
        bit //= 2
        at += 1
    return stack.reshape(value.shape[:-2] + (size,) + value.shape[-2:])


def scatter(make, axis):
    half = lax.axis_size(axis)
    arrived = []
    for mask in reversed(masks_of(axis)):
        half //= 2
        sent = make(half, 2 * half, [x[half : 2 * half] for x in arrived], bf16)
        arrived = [x[:half] for x in arrived] + [swap(sent, axis, mask)]
    return make(0, 1, arrived, f32)[0]


def phases():
    masks = masks_of("dp")
    return [masks[:1], masks[1:-1], masks[-1:]]


class Item:
    late = ()

    def bring(self, value, axis, mask):
        got = swap(value, axis, mask)
        return after(got, *self.late) if self.late else got


class Gather(Item):
    def __init__(self, value):
        self.stack, self.halves, self.phase = value[None], None, 0

    def value(self):
        return self.stack

    def advance(self, value):
        for mask in phases()[self.phase]:
            got = self.bring(value, "dp", mask)
            self.halves = (value, got)
            value = join(value, got)
        self.stack = value
        self.phase += 1
        return got

    def pieces(self):
        half = order_of("dp")[: lax.axis_size("dp") // 2]
        return [(x, [r ^ m for r in half]) for x, m in zip(self.halves, (0, masks_of("dp")[-1]))]


class GatherLate(Item):
    def __init__(self, value):
        self.parts, self.phase = [(value[None], [0])], 0

    def value(self):
        return self.parts[max(self.phase - 2, 0)][0]

    def advance(self, value):
        masks = masks_of("dp")
        masks = [masks[-1:], masks[:1], masks[1:-1], masks[1:-1]][self.phase]
        at = max(self.phase - 2, 0)
        places = self.parts[at][1]
        for mask in masks:
            got = self.bring(value, "dp", mask)
            halves = [(value, places), (got, [r ^ mask for r in places])]
            places = places + halves[1][1]
            if mask != masks[-1] or self.phase == 0:
                value = join(value, got)
        if self.phase == 0:
            self.parts = [(value, places)]
        elif self.phase == 1:
            self.parts = halves
        elif self.phase == 2:
            self.parts, self.first = [None, self.parts[1]], halves
        else:
            self.parts = self.first + halves
        self.phase += 1
        return got

    def pieces(self):
        return self.parts


class Scatter(Item):
    def __init__(self, make):
        self.make, self.half, self.arrived, self.phase = make, lax.axis_size("dp"), [], 2

    def value(self):
        half = self.half // 2
        return self.make(half, 2 * half, [x[half : 2 * half] for x in self.arrived], bf16)

    def advance(self, value):
        for k, mask in enumerate(reversed(phases()[self.phase])):
            if k:
                value = self.value()
            self.half //= 2
            got = self.bring(value, "dp", mask)
            self.arrived = [x[: self.half] for x in self.arrived] + [got]
        self.phase -= 1
        return got

    def result(self):
        return self.make(0, 1, self.arrived, f32)[0]


class TensorGather(Item):
    def __init__(self, value):
        self.stack, self.masks = value[None], masks_of("tensor")

    def value(self):
        return self.stack

    def advance(self, value):
        got = self.bring(value, "tensor", self.masks[0])
        self.stack, self.masks = join(value, got), self.masks[1:]
        return got


class PairRows(Item):
    def __init__(self, value):
        self.stack = value

    def value(self):
        return self.stack

    def advance(self, value):
        got = self.bring(value, "tensor", 1)
        upper = (lax.axis_index("tensor") & 1) != 0
        self.stack = jnp.stack(
            [jnp.where(upper, got, value), jnp.where(upper, value, got)], axis=value.ndim - 2
        )
        return got


class TensorScatter(Item):
    def __init__(self, sums):
        self.sums, self.masks, self.arrived = sums, masks_of("tensor")[::-1], []

    def value(self):
        half = 1 << (len(self.masks) - 1)
        if half == self.sums[1].shape[0]:
            return self.sums[1]
        return plus(
            self.sums[0][half : 2 * half].astype(f32),
            [x[half : 2 * half] for x in self.arrived],
            bf16,
        )

    def advance(self, value):
        self.arrived.append(self.bring(value, "tensor", self.masks[0]))
        self.masks = self.masks[1:]
        return self.arrived[-1]

    def terms(self):
        return [self.sums[0], *self.arrived]


class TensorExchange(Item):
    def __init__(self, stack):
        self.stack, self.masks = stack[:, None], masks_of("tensor")

    def value(self):
        return self.stack[1::2]

    def advance(self, value):
        got = self.bring(value, "tensor", self.masks[0])
        self.stack = jnp.concatenate([self.stack[0::2], got], axis=1)
        self.masks = self.masks[1:]
        return got

    def rows(self):
        return self.stack.reshape((-1,) + self.stack.shape[3:])


class Direct(Item):
    def __init__(self, parts):
        self.parts = parts

    def value(self):
        return jnp.stack(self.parts)

    def advance(self, value):
        order = order_of("tensor")
        got = [value[0]] + [
            self.bring(value[p], "tensor", order[p]) for p in range(1, len(order))
        ]
        self.all = jnp.concatenate(got, axis=0)
        return self.all

    def rows(self):
        return self.all


class Rounds:
    def __init__(self):
        self.done = []

    def go(self, *items, ends=(), during=()):
        done = list(ends)
        for item in items:
            value = item.value()
            if self.done:
                value = after(value, *self.done)
            item.late = during
            done.append(item.advance(value))
        self.done = done


def plus(total, arrived, kind):
    for other in arrived:
        total = total + other.astype(f32)
    return total.astype(kind)


def scaled_norm(value_in, gain_vec):
    return (
        value_in
        * lax.rsqrt(jnp.mean(value_in * value_in, axis=-1, keepdims=True) + eps_norm)
        * gain_vec
    )


def silu_product(gate, up_part):
    return gate * jax.nn.sigmoid(gate) * up_part


def params(steps=1):
    return pltpu.CompilerParams(
        dimension_semantics=("arbitrary",) * steps, vmem_limit_bytes=VMEM_LIMIT
    )


def swap_halves(value):
    half = HEAD // 2
    return jnp.concatenate([value[:, half:], value[:, :half]], axis=1)


def rope_one(raw, gain, cos, sin, factor):
    scale = lax.rsqrt(jnp.mean(raw * raw, axis=-1, keepdims=True) + eps_norm)
    normed = raw * scale * gain
    return (normed * cos + swap_halves(normed) * sin) * factor


def rope_back(raw, gain, cos, sin, factor, grad):
    grad = grad * factor
    grad = grad * cos - swap_halves(grad) * sin
    scale = lax.rsqrt(jnp.mean(raw * raw, axis=-1, keepdims=True) + eps_norm)
    weighted = grad * gain
    back = scale * weighted - raw * (
        scale * scale * scale * jnp.mean(raw * weighted, axis=-1, keepdims=True)
    )
    return back, jnp.sum(grad * raw * scale, axis=0, keepdims=True)


def query_kernel(h_ref, w_ref, cos_ref, sin_ref, gain_ref, raw_ref, out_ref):
    cols = w_ref.shape[3]
    raw = sum(
        dot(h_ref[:, r * cols : (r + 1) * cols], w_ref[0, r], contract_cols)
        for r in range(w_ref.shape[1])
    )
    raw_ref[0] = raw
    rows, blocks = out_ref.shape[0], out_ref.shape[2]
    for h in range(HEADS_KV):
        turned = rope_one(
            raw[:, h * HEAD : (h + 1) * HEAD], gain_ref[...], cos_ref[...], sin_ref[...], 0.125
        )
        wide = jnp.concatenate([turned, jnp.zeros_like(turned)], axis=1).astype(bf16)
        out_ref[:, h, :, 0] = wide.reshape(rows, blocks, STRETCH, LANES)


def key_kernel(h_ref, w_ref, cos_ref, sin_ref, gain_ref, raw_ref, out_ref):
    raw = dot(h_ref[...], w_ref[...])
    raw_ref[...] = raw
    rows, blocks = out_ref.shape[0], out_ref.shape[2]
    for h in range(HEADS_KV):
        turned = rope_one(
            raw[:, h * HEAD : (h + 1) * HEAD], gain_ref[...], cos_ref[...], sin_ref[...], 1.0
        )
        start = (HEADS_KV + h) * HEAD
        wide = jnp.concatenate([turned, raw[:, start : start + HEAD]], axis=1).astype(bf16)
        out_ref[:, h] = wide.reshape(rows, blocks, STRETCH, LANES)


def load_keys(halves, kv, kvt):
    places = [(half, i) for half in halves for i in range(half.shape[0])]
    group = len(places) * STRETCH
    for g in range(halves[0].shape[3]):
        for r, (half, i) in enumerate(places):
            start = g * group + r * STRETCH
            kv[start : start + STRETCH, :] = half[i, 0, 0, g]
    kvt[...] = kv[...].T
    return group


def attend_kernel(q_ref, limit_ref, keypos_ref, low_ref, high_ref, out_ref, kv, kvt):
    blocks = q_ref.shape[2]
    group = load_keys((low_ref, high_ref), kv, kvt)
    for b in range(blocks):
        span = (b + 1) * group
        q = q_ref[0, 0, b].reshape(-1, LANES)
        scores = dot(kv[:span], q, contract_cols)
        scores = jnp.where(keypos_ref[0, :span] <= limit_ref[0, b], scores, neg_large)
        top = jnp.max(scores, axis=0, keepdims=True)
        weights = jnp.exp(scores - top)
        total = jnp.sum(weights, axis=0, keepdims=True)
        heads = dot(kvt[:, :span], weights.astype(bf16)) / total
        out_ref[0, 0, b] = heads.T.astype(bf16).reshape(q_ref.shape[3:])


def attend_back_kernel(
    q_ref, g_ref, limit_ref, keypos_ref, low_ref, high_ref, dq_ref, dlow_ref, dhigh_ref, kv, kvt, acc
):
    blocks = q_ref.shape[2]
    group = load_keys((low_ref, high_ref), kv, kvt)
    acc[...] = jnp.zeros_like(acc)
    for b in range(blocks):
        span = (b + 1) * group
        q = q_ref[0, 0, b].reshape(-1, LANES)
        grad = g_ref[0, 0, b].reshape(-1, LANES)
        scores = dot(kv[:span], q, contract_cols)
        scores = jnp.where(keypos_ref[0, :span] <= limit_ref[0, b], scores, neg_large)
        top = jnp.max(scores, axis=0, keepdims=True)
        weights = jnp.exp(scores - top)
        probs = weights * (1.0 / jnp.sum(weights, axis=0, keepdims=True))
        d_probs = dot(kv[:span], grad, contract_cols)
        delta = jnp.sum(probs * d_probs, axis=0, keepdims=True)
        d_scores = (probs * (d_probs - delta)).astype(bf16)
        dq = dot(kvt[:, :span], d_scores)
        dq_ref[0, 0, b] = dq.T.reshape(q_ref.shape[3:])
        acc[:span] += dot(d_scores, q) + dot(probs.astype(bf16), grad)
    count = dlow_ref.shape[0]
    for out, first in ((dlow_ref, 0), (dhigh_ref, count)):
        for r in range(count):
            for g in range(blocks):
                start = g * group + (first + r) * STRETCH
                out[r, 0, 0, g] = acc[start : start + STRETCH].astype(bf16)


def out_kernel(o_ref, w_ref, x_ref, live_ref, gain_ref, mixed_ref, h_ref, heads_ref):
    rows = heads_ref.shape[1]
    heads = jnp.concatenate(
        [o_ref[:, h, :, 0].reshape(rows, LANES)[:, HEAD:] for h in range(HEADS_KV)], axis=1
    )
    heads_ref[0] = heads
    cols = w_ref.shape[3]

    @pl.when(pl.program_id(0) == 0)
    def _():
        mixed_ref[...] = jnp.zeros_like(mixed_ref)

    for r in range(w_ref.shape[1]):
        mixed_ref[:, r * cols : (r + 1) * cols] += dot(heads, w_ref[0, r])

    @pl.when(pl.program_id(0) == pl.num_programs(0) - 1)
    def _():
        mixed = x_ref[...].astype(f32) + live_ref[...] * mixed_ref[...]
        mixed_ref[...] = mixed
        h_ref[...] = scaled_norm(mixed, gain_ref[...]).astype(bf16)


def norm_back(value, gain, grad):
    scale = lax.rsqrt(jnp.mean(value * value, axis=-1, keepdims=True) + eps_norm)
    weighted = grad * gain
    inner = jnp.mean(value * weighted, axis=-1, keepdims=True)
    back = scale * weighted - value * (scale * scale * scale * inner)
    return back, jnp.sum(grad * value * scale, axis=0, keepdims=True)


def mixed_back_kernel(mixed_ref, cot_ref, gain_ref, live_ref, *rest):
    terms, (d_mixed_ref, d_attn_ref, dgain_ref) = rest[:-3], rest[-3:]
    grad = sum(ref[0].astype(f32) for ref in terms)
    back, dgain_ref[...] = norm_back(mixed_ref[...], gain_ref[...], grad)
    d_mixed = cot_ref[...].astype(f32) + back
    d_mixed_ref[...] = d_mixed
    d_attn_ref[...] = (live_ref[...] * d_mixed).astype(bf16)


def heads_back_kernel(d_ref, w_ref, out_ref):
    cols = w_ref.shape[3]
    grad = sum(
        dot(d_ref[:, r * cols : (r + 1) * cols], w_ref[0, r], contract_cols)
        for r in range(w_ref.shape[1])
    )
    rows, blocks = out_ref.shape[0], out_ref.shape[2]
    for h in range(HEADS_KV):
        part = grad[:, h * HEAD : (h + 1) * HEAD]
        wide = jnp.concatenate([jnp.zeros_like(part), part], axis=1).astype(bf16)
        out_ref[:, h, :, 0] = wide.reshape(rows, blocks, STRETCH, LANES)


def query_back_kernel(dq_ref, raw_ref, cos_ref, sin_ref, gain_ref, out_ref, dgain_ref):
    @pl.when(pl.program_id(0) == 0)
    def _():
        dgain_ref[...] = jnp.zeros_like(dgain_ref)

    raw = raw_ref[0]
    parts = []
    for h in range(HEADS_KV):
        grad = dq_ref[:, h, :, 0].reshape(raw.shape[0], LANES)[:, :HEAD]
        back, dgain = rope_back(
            raw[:, h * HEAD : (h + 1) * HEAD],
            gain_ref[...],
            cos_ref[...],
            sin_ref[...],
            0.125,
            grad,
        )
        parts.append(back)
        dgain_ref[...] += dgain
    out_ref[0] = jnp.concatenate(parts, axis=1).astype(bf16)


def key_back_kernel(sum_ref, raw_ref, cos_ref, sin_ref, gain_ref, out_ref, dgain_ref):
    raw = raw_ref[...]
    keys, values = [], []
    total = jnp.zeros_like(dgain_ref)
    for h in range(HEADS_KV):
        both = sum_ref[:, h].reshape(raw.shape[0], LANES)
        back, dgain = rope_back(
            raw[:, h * HEAD : (h + 1) * HEAD],
            gain_ref[...],
            cos_ref[...],
            sin_ref[...],
            1.0,
            both[:, :HEAD],
        )
        keys.append(back)
        values.append(both[:, HEAD:])
        total = total + dgain
    dgain_ref[...] = total
    out_ref[...] = jnp.concatenate(keys + values, axis=1).astype(bf16)


def back_kernel(
    dq_ref, wq_ref, dkv_ref, wkv_ref, x_ref, gain_ref, d_mixed_ref, out_ref, dgain_ref, acc
):
    @pl.when(pl.program_id(0) == 0)
    def _():
        acc[...] = dot(dkv_ref[...], wkv_ref[...], contract_cols)

    cols = wq_ref.shape[3]
    for r in range(wq_ref.shape[1]):
        acc[:, r * cols : (r + 1) * cols] += dot(dq_ref[0], wq_ref[0, r])

    @pl.when(pl.program_id(0) == pl.num_programs(0) - 1)
    def _():
        back, dgain_ref[...] = norm_back(x_ref[...].astype(f32), gain_ref[...], acc[...])
        out_ref[...] = (d_mixed_ref[...] + back).astype(bf16)


def shards_kernel(in_ref, down_ref, query_ref, *refs):
    parts, query_out_ref = refs[:-1], refs[-1]
    ff = down_ref.shape[0]
    start = 0
    for ref in parts:
        part = ref.shape[1] // 3
        ref[:, :part] = in_ref[:, start : start + part]
        ref[:, part : 2 * part] = in_ref[:, ff + start : ff + start + part]
        ref[:, 2 * part :] = down_ref[start : start + part, :].T
        start += part
    query_out_ref[...] = query_ref[...].T


def turn_columns(order, back, index, value):
    size = len(order)
    cols = value.shape[1] // size

    def pick(value, places):
        return jnp.concatenate([value[:, p * cols : (p + 1) * cols] for p in places], axis=1)

    if back:
        value = pick(value, [order.index(i) for i in range(size)])
    bit = 1
    while bit < size:
        value = jnp.where((index & bit) != 0, pick(value, [i ^ bit for i in range(size)]), value)
        bit *= 2
    return value if back else pick(value, order)


def enter_kernel(order, index_ref, x_ref, cot_ref, live_ref, x_out, cot_out, d_ffn_out):
    x_out[...] = turn_columns(order, False, index_ref[0], x_ref[...].astype(f32)).astype(bf16)
    cot = turn_columns(order, False, index_ref[0], cot_ref[...].astype(f32))
    cot_out[...] = cot.astype(bf16)
    d_ffn_out[...] = (cot * live_ref[...]).astype(bf16)


def leave_kernel(order, index_ref, x_ref, out_ref):
    value = x_ref[...].astype(f32)
    out_ref[...] = turn_columns(order, True, index_ref[0], value).astype(bf16)


def finish_kernel(order, index_ref, mixed_ref, live_ref, *rest):
    terms, out_ref = rest[:-1], rest[-1]
    ffn = sum(ref[0].astype(f32) for ref in terms)
    value = mixed_ref[...] + live_ref[...] * ffn
    out_ref[...] = turn_columns(order, True, index_ref[0], value).astype(bf16)


def product_kernel(left_ref, right_ref, low_ref, high_ref, turned):
    @pl.when(pl.program_id(0) == 0)
    def _():
        turned[...] = right_ref[...].T

    out = dot(turned[...], left_ref[...]).astype(bf16)
    low = pl.program_id(0) < pl.num_programs(0) // 2
    for out_ref, here in ((low_ref, low), (high_ref, jnp.logical_not(low))):

        @pl.when(here)
        def _(out_ref=out_ref):
            out_ref[0] = out


def pick_columns(ref, places, cols):
    if places == list(range(places[0], places[0] + len(places))):
        return ref[:, places[0] * cols : (places[-1] + 1) * cols]
    return jnp.concatenate([ref[:, p * cols : (p + 1) * cols] for p in places], axis=1)


def hidden_kernel(all_places, h_ref, d_ref, *refs):
    pieces, (hidden_ref, d_gate_up_ref, turned_ref) = refs[:-3], refs[-3:]
    part = hidden_ref.shape[1]
    gate_up = d_hidden = None
    for places, ref in zip(all_places, pieces):
        cols = ref.shape[0] // len(places)
        first = dot(pick_columns(h_ref, places, cols), ref[:, : 2 * part])
        second = dot(pick_columns(d_ref, places, cols), ref[:, 2 * part :])
        gate_up = first if gate_up is None else gate_up + first
        d_hidden = second if d_hidden is None else d_hidden + second
    gate, up = gate_up[:, :part], gate_up[:, part:]
    sig = jax.nn.sigmoid(gate)
    swish = gate * sig
    hidden = (swish * up).astype(bf16)
    d_gate = (d_hidden * up * (sig + swish * (1.0 - sig))).astype(bf16)
    d_up = (d_hidden * swish).astype(bf16)
    hidden_ref[...] = hidden
    d_gate_up_ref[:, :part] = d_gate
    d_gate_up_ref[:, part:] = d_up
    turned_ref[:part] = d_gate.T
    turned_ref[part : 2 * part] = d_up.T
    turned_ref[2 * part :] = hidden.T


def grads_kernel(h_ref, d_ref, turned_ref, low_ref, high_ref):
    split = turned_ref.shape[0] // 3 * 2
    first = dot(turned_ref[:split], h_ref[...]).astype(bf16)
    second = dot(turned_ref[split:], d_ref[...]).astype(bf16)
    low = pl.program_id(0) < pl.num_programs(0) // 2
    span = low_ref.shape[2]
    for out_ref, here in ((low_ref, low), (high_ref, jnp.logical_not(low))):

        @pl.when(here)
        def _(out_ref=out_ref):
            for p in range(out_ref.shape[0]):
                out_ref[p, :split] = first[:, p * span : (p + 1) * span]
                out_ref[p, split:] = second[:, p * span : (p + 1) * span]


def back_sum_kernel(all_places, *refs):
    count = len(all_places)
    half = refs[-1].shape[1] // 2
    totals = [None, None]
    at = count
    for c, pieces in enumerate(all_places):
        terms = [dot(refs[c][...], refs[at + i][...], contract_cols) for i in range(len(pieces))]
        at += len(pieces)
        if len(pieces) > 2:
            blocks = {}
            for places, term in zip(pieces, terms):
                cols = term.shape[1] // len(places)
                for i, p in enumerate(places):
                    blocks[p] = term[:, i * cols : (i + 1) * cols]
            middle = len(blocks) // 2
            terms = [
                jnp.concatenate([blocks[side * middle + i] for i in range(middle)], axis=1)
                for side in range(2)
            ]
        totals = [t if old is None else old + t for old, t in zip(totals, terms)]
    low = pl.program_id(0) < pl.num_programs(0) // 2
    for out_ref, here in ((refs[-2], low), (refs[-1], jnp.logical_not(low))):

        @pl.when(here)
        def _(out_ref=out_ref):
            for side in range(2):
                out_ref[:, side * half : (side + 1) * half] = totals[side].astype(bf16)


def whole(shape):
    return pl.BlockSpec(shape, lambda *_: (0,) * len(shape))


def local(
    inputs,
    cotangent,
    w_query,
    w_kv,
    w_out,
    w_in,
    w_down,
    norm_gains,
    head_gains,
    lengths,
    slot_blocks,
):
    sp_rows, width = inputs.shape
    n = lax.axis_size("dp")
    n_tensor = lax.axis_size("tensor")
    dp = lax.axis_index("dp")
    tensor = lax.axis_index("tensor")
    seq_count = lengths.shape[0]
    row_span = sp_rows * n_tensor // seq_count
    blocks = row_span // STRETCH
    rows = sp_rows // row_span
    per_row = SLOTS // STRETCH
    cols = width // n
    q_cols = w_query.shape[1]
    kv_cols = w_kv.shape[1]
    ff = w_down.shape[0]
    order = order_of("dp")
    tensor_order = order_of("tensor")
    rels = jnp.array(order, jnp.int32)

    smem = pl.BlockSpec(memory_space=pltpu.SMEM)

    def call(kernel, out_shape, name, *args, specs=None):
        return pl.pallas_call(
            kernel,
            in_specs=specs,
            out_shape=out_shape,
            compiler_params=pltpu.CompilerParams(vmem_limit_bytes=VMEM_LIMIT),
            cost_estimate=SMALL,
            name=name,
        )(*args)

    table = slot_blocks.reshape(n, n_tensor, rows, blocks)
    mine = lax.dynamic_index_in_dim(table, tensor, axis=1, keepdims=False)[dp ^ rels]
    inside = jnp.arange(STRETCH, dtype=jnp.int32)
    key_pos = (mine % per_row * STRETCH)[..., None] + inside
    own_pos = key_pos[0]
    own_len = lengths[mine[0] // per_row][..., None]
    live = (own_pos < own_len).astype(f32).reshape(sp_rows, 1)
    limit = jnp.minimum(own_pos, own_len - 1)
    limit = jnp.broadcast_to(limit[:, :, None, None, :], (rows, blocks, 1, n_tensor, STRETCH))
    limit = limit.reshape(rows, blocks, 1, n_tensor * STRETCH)
    key_pos = key_pos.transpose(1, 2, 0, 3).reshape(rows, SLOTS, 1)
    half = HEAD // 2
    frequency = rope_base ** (-2.0 * jnp.arange(half, dtype=f32) / HEAD)
    angles = own_pos.reshape(sp_rows, 1).astype(f32) * frequency
    cosine, sine = jnp.cos(angles), jnp.sin(angles)
    cos = jnp.concatenate([cosine, cosine], axis=1)
    sin = jnp.concatenate([-sine, sine], axis=1)
    head_float = head_gains.astype(f32)
    q_gain, k_gain = head_float[0:1], head_float[1:2]

    vmem = pl.BlockSpec(memory_space=pltpu.VMEM)
    index = dp.reshape(1)
    low_square = jax.ShapeDtypeStruct((sp_rows, width), bf16)
    inputs, cotangent, d_ffn_own = call(
        functools.partial(enter_kernel, tuple(order)),
        [low_square] * 3,
        "enter",
        index,
        inputs,
        cotangent,
        live,
        specs=[smem, vmem, vmem, vmem],
    )
    inputs_f = inputs.astype(f32)
    part = w_kv.shape[0] // 2
    kv_shard = lax.dynamic_slice_in_dim(w_kv, (tensor & 1) * part, part, axis=0)
    unit = ff // sum(FF_PARTS)
    sizes = [size * unit for size in FF_PARTS]
    *shards, query_shard = pl.pallas_call(
        shards_kernel,
        out_shape=[jax.ShapeDtypeStruct((cols, 3 * part), bf16) for part in sizes]
        + [jax.ShapeDtypeStruct((q_cols, cols), bf16)],
        compiler_params=pltpu.CompilerParams(vmem_limit_bytes=VMEM_LIMIT),
        cost_estimate=SMALL,
        name="shards",
    )(w_in.reshape(cols, 2 * ff), w_down, w_query)
    link = Rounds()
    g_kv, g_gains = Gather(kv_shard), Gather(norm_gains)
    g_query, g_out = Gather(query_shard), Gather(w_out)
    g_ff = [Gather(x) for x in shards[:-1]] + [GatherLate(shards[-1])]
    link.go(g_kv, g_query, g_gains)
    link.go(g_kv, g_gains, g_out)
    link.go(g_kv, g_gains, g_query, g_ff[0])
    gains = g_gains.stack.transpose(1, 0, 2).reshape(2, width).astype(f32)
    gain_one, gain_two = gains[0], gains[1]
    h_one = scaled_norm(inputs_f, gain_one).astype(bf16)
    t_kv = PairRows(g_kv.stack)
    link.go(t_kv, g_query, g_out, g_ff[5])
    t_query = TensorGather(g_query.stack)
    kv_all = t_kv.stack.reshape(width, kv_cols)
    t_d_ffn = TensorGather(d_ffn_own)

    packed = (rows, HEADS_KV, blocks, n_tensor, STRETCH, LANES)
    packed_kv = (rows, HEADS_KV, blocks, STRETCH, LANES)
    both_spec = pl.BlockSpec((1, n, q_cols, cols), lambda s: (s, 0, 0, 0))
    kv_raw, kv_own = pl.pallas_call(
        key_kernel,
        out_shape=(
            jax.ShapeDtypeStruct((sp_rows, kv_cols), f32),
            jax.ShapeDtypeStruct(packed_kv, bf16),
        ),
        compiler_params=pltpu.CompilerParams(vmem_limit_bytes=VMEM_LIMIT),
        cost_estimate=SMALL,
        name="key_value",
    )(h_one, kv_all, cos, sin, k_gain)
    g_keys = Gather(kv_own)
    link.go(t_query, g_out, g_ff[0], g_keys)
    t_out = TensorGather(g_out.stack)
    link.go(t_query, t_out, g_keys, g_ff[0], g_ff[1])
    query_all = t_query.stack
    one_head = (sp_rows, HEAD)
    part_spec = pl.BlockSpec(
        (rows, HEADS_KV, blocks, 1, STRETCH, LANES), lambda s: (0, 0, 0, s, 0, 0)
    )
    q_raw, queries = pl.pallas_call(
        query_kernel,
        grid=(n_tensor,),
        in_specs=[
            whole((sp_rows, width)),
            both_spec,
            whole(one_head),
            whole(one_head),
            whole((1, HEAD)),
        ],
        out_specs=(pl.BlockSpec((1, sp_rows, q_cols), lambda s: (s, 0, 0)), part_spec),
        out_shape=(
            jax.ShapeDtypeStruct((n_tensor, sp_rows, q_cols), f32),
            jax.ShapeDtypeStruct(packed, bf16),
        ),
        compiler_params=params(),
        cost_estimate=SMALL,
        name="query",
    )(h_one, query_all, cos, sin, q_gain)
    link.go(t_out, t_d_ffn, g_keys, g_ff[1], g_ff[2], during=[queries])
    out_all = t_out.stack
    kv_halves = g_keys.halves
    q_spec = pl.BlockSpec(
        (1, 1, blocks, n_tensor, STRETCH, LANES), lambda i, h: (i, h, 0, 0, 0, 0)
    )
    kv_spec = pl.BlockSpec(
        (n // 2, 1, 1, blocks, STRETCH, LANES), lambda i, h: (0, i, h, 0, 0, 0)
    )
    limit_spec = pl.BlockSpec(
        (1, blocks, 1, n_tensor * STRETCH), lambda i, h: (i, 0, 0, 0)
    )
    pos_spec = pl.BlockSpec((1, SLOTS, 1), lambda i, h: (i, 0, 0))
    heads_packed = pl.pallas_call(
        attend_kernel,
        grid=(rows, HEADS_KV),
        in_specs=[q_spec, limit_spec, pos_spec] + [kv_spec] * 2,
        out_specs=q_spec,
        out_shape=jax.ShapeDtypeStruct(packed, bf16),
        scratch_shapes=[pltpu.VMEM((SLOTS, LANES), bf16), pltpu.VMEM((LANES, SLOTS), bf16)],
        compiler_params=params(2),
        cost_estimate=SMALL,
        name="attend",
    )(queries, limit, key_pos, *kv_halves)

    heads_shape = (n_tensor, sp_rows, q_cols)
    head_spec = pl.BlockSpec((1, sp_rows, q_cols), lambda s: (s, 0, 0))
    square = whole((sp_rows, width))
    mixed, h_two_own, attn_heads = pl.pallas_call(
        out_kernel,
        grid=(n_tensor,),
        in_specs=[part_spec, both_spec, square, whole((sp_rows, 1)), whole((1, width))],
        out_specs=(square, square, head_spec),
        out_shape=(
            jax.ShapeDtypeStruct((sp_rows, width), f32),
            jax.ShapeDtypeStruct((sp_rows, width), bf16),
            jax.ShapeDtypeStruct(heads_shape, bf16),
        ),
        compiler_params=params(),
        cost_estimate=SMALL,
        name="out",
    )(heads_packed, out_all, inputs, live, gain_two[None])
    t_heads = TensorExchange(attn_heads)

    t_h_two = TensorGather(h_two_own)
    t_h_one = TensorGather(h_one)
    rows_all = sp_rows * n_tensor
    link.go(t_d_ffn, g_ff[1], g_ff[2], g_ff[3], during=[h_two_own])
    d_ffn = t_d_ffn.stack.reshape(-1, width)
    link.go(t_h_two, g_ff[2], g_ff[3], g_ff[4])
    link.go(t_h_two, t_h_one, g_ff[3], g_ff[4], g_ff[5])
    h_two = t_h_two.stack.reshape(-1, width)
    steps = n_tensor // 2
    row_block = lambda span: pl.BlockSpec((rows_all // steps, span), lambda i: (i, 0))
    row_spec = row_block(width)
    weights, hiddens, d_gate_ups, turned = [], [], [], []

    def hidden_part(g, part):
        pieces = [
            (x.reshape(len(rs) * cols, 3 * part), [order.index(r) for r in rs])
            for x, rs in g.pieces()
        ]
        weights.append(pieces)
        hidden, d_gate_up, flipped = pl.pallas_call(
            functools.partial(hidden_kernel, [places for _, places in pieces]),
            grid=(steps,),
            in_specs=[row_spec, row_spec] + [whole(x.shape) for x, _ in pieces],
            out_specs=(
                row_block(part),
                row_block(2 * part),
                pl.BlockSpec((3 * part, rows_all // steps), lambda i: (0, i)),
            ),
            out_shape=(
                jax.ShapeDtypeStruct((rows_all, part), bf16),
                jax.ShapeDtypeStruct((rows_all, 2 * part), bf16),
                jax.ShapeDtypeStruct((3 * part, rows_all), bf16),
            ),
            compiler_params=params(),
            cost_estimate=SMALL,
        name="hidden",
        )(h_two, d_ffn, *[x for x, _ in pieces])
        hiddens.append(hidden)
        d_gate_ups.append(d_gate_up)
        turned.append(flipped)

    def split_places(halves, wide):
        if cols == 256:
            return halves
        return [
            x.reshape(-1, wide, 256 // cols, cols).transpose(0, 2, 1, 3).reshape(n // 2, wide, cols)
            for x in halves
        ]

    def grads_of(flipped):
        wide = flipped.shape[0]
        count = width // 256
        grid = width // 512
        low_spec = pl.BlockSpec((2, wide, 256), lambda j: (jnp.minimum(j, grid // 2 - 1), 0, 0))
        high_spec = pl.BlockSpec((2, wide, 256), lambda j: (jnp.maximum(j - grid // 2, 0), 0, 0))
        block = pl.BlockSpec((rows_all, 512), lambda j: (0, j))
        halves = pl.pallas_call(
            grads_kernel,
            grid=(grid,),
            in_specs=[block, block, whole(flipped.shape)],
            out_specs=(low_spec, high_spec),
            out_shape=[jax.ShapeDtypeStruct((count // 2, wide, 256), bf16)] * 2,
            compiler_params=params(),
            cost_estimate=SMALL,
            name="weight_grads",
        )(h_two, d_ffn, flipped)
        halves = split_places(halves, wide)

        def make(begin, end, arrived, kind):
            if begin >= n // 2:
                return halves[1]
            return plus(halves[0][begin:end].astype(f32), arrived, kind)

        return Scatter(make), halves[1]

    s_ff, sent = [], []

    def add_grads(c):
        item, first = grads_of(after(turned[c], *link.done) if c > 2 else turned[c])
        s_ff.append(item)
        sent.append(first)

    def back_sum(parts, down):
        def weight_spec(x, w):
            span = x.shape[1]
            at = (w.shape[1] - span) // span if down else 0
            return pl.BlockSpec(
                (w.shape[0], span), lambda i: (0, at), pipeline_mode=pl.Buffered(1)
            )

        return pl.pallas_call(
            functools.partial(
                back_sum_kernel, [[places for _, places in pieces] for pieces in weights]
            ),
            grid=(steps,),
            in_specs=[row_block(x.shape[1]) for x in parts]
            + [weight_spec(x, w) for x, pieces in zip(parts, weights) for w, _ in pieces],
            out_specs=(
                pl.BlockSpec(
                    (rows_all // steps, width), lambda i: (jnp.minimum(i, steps // 2 - 1), 0)
                ),
                pl.BlockSpec(
                    (rows_all // steps, width), lambda i: (jnp.maximum(i - steps // 2, 0), 0)
                ),
            ),
            out_shape=[jax.ShapeDtypeStruct((rows_all // 2, width), bf16)] * 2,
            compiler_params=params(),
            cost_estimate=SMALL,
            name="back_sum",
        )(*parts, *[w for pieces in weights for w, _ in pieces])

    def row_sums(parts, down):
        return TensorScatter(
            [x.reshape(n_tensor // 2, sp_rows, width) for x in back_sum(parts, down)]
        )

    hidden_part(g_ff[0], sizes[0])
    hidden_part(g_ff[1], sizes[1])
    add_grads(0)
    link.go(t_h_one, t_heads, g_ff[4], g_ff[5], during=[*turned, *sent])
    h_one_all = t_h_one.stack.reshape(-1, width)
    hidden_part(g_ff[2], sizes[2])
    hidden_part(g_ff[3], sizes[3])
    add_grads(1)
    add_grads(2)
    link.go(t_heads, s_ff[0], g_ff[5], during=[*turned[2:], *sent[1:]])
    hidden_part(g_ff[4], sizes[4])
    hidden_part(g_ff[5], sizes[5])
    t_back = row_sums(d_gate_ups, False)
    link.go(s_ff[1], s_ff[0], during=t_back.sums)
    add_grads(3)
    t_ffn = row_sums(hiddens, True)
    link.go(t_back, s_ff[2], s_ff[1], s_ff[0], during=[*t_ffn.sums, *sent[3:]])
    add_grads(4)
    link.go(t_back, t_ffn, s_ff[3], s_ff[2], s_ff[1], during=sent[4:])
    first_spec = pl.BlockSpec((1, sp_rows, width), lambda i: (0, 0, 0))
    back_terms = t_back.terms()
    d_mixed, d_attn_own, d_gain_two = pl.pallas_call(
        mixed_back_kernel,
        grid=(1,),
        in_specs=[square, square, whole((1, width)), whole((sp_rows, 1))]
        + [first_spec] * len(back_terms),
        out_specs=(square, square, whole((1, width))),
        out_shape=(
            jax.ShapeDtypeStruct((sp_rows, width), f32),
            jax.ShapeDtypeStruct((sp_rows, width), bf16),
            jax.ShapeDtypeStruct((1, width), f32),
        ),
        compiler_params=params(),
        cost_estimate=SMALL,
        name="mixed_back",
    )(mixed, cotangent, gain_two[None], live, *back_terms)

    d_heads = pl.pallas_call(
        heads_back_kernel,
        grid=(n_tensor,),
        in_specs=[whole((sp_rows, width)), both_spec],
        out_specs=part_spec,
        out_shape=jax.ShapeDtypeStruct(packed, bf16),
        compiler_params=params(),
        cost_estimate=SMALL,
        name="heads_back",
    )(d_attn_own, out_all)
    d_query, d_low, d_high = pl.pallas_call(
        attend_back_kernel,
        grid=(rows, HEADS_KV),
        in_specs=[q_spec, q_spec, limit_spec, pos_spec] + [kv_spec] * 2,
        out_specs=[q_spec] + [kv_spec] * 2,
        out_shape=[jax.ShapeDtypeStruct(packed, f32)]
        + [jax.ShapeDtypeStruct((n // 2,) + packed_kv, bf16)] * 2,
        scratch_shapes=[
            pltpu.VMEM((SLOTS, LANES), bf16),
            pltpu.VMEM((LANES, SLOTS), bf16),
            pltpu.VMEM((SLOTS, LANES), f32),
        ],
        compiler_params=params(2),
        cost_estimate=SMALL,
        name="attend_back",
    )(queries, d_heads, limit, key_pos, *kv_halves)

    def key_grads(begin, end, arrived, kind):
        if begin >= n // 2:
            return d_high
        return plus(d_low[begin:end].astype(f32), arrived, kind)

    s_keys = Scatter(key_grads)
    t_attn = TensorGather(d_attn_own)
    d_q_low, d_q_gain = pl.pallas_call(
        query_back_kernel,
        grid=(n_tensor,),
        in_specs=[part_spec, head_spec, whole(one_head), whole(one_head), whole((1, HEAD))],
        out_specs=(head_spec, whole((1, HEAD))),
        out_shape=(
            jax.ShapeDtypeStruct(heads_shape, bf16),
            jax.ShapeDtypeStruct((1, HEAD), f32),
        ),
        compiler_params=params(),
        cost_estimate=SMALL,
        name="query_back",
    )(d_query, q_raw, cos, sin, q_gain)

    def product(left, right):
        wide = right.shape[1]
        count = width // 256
        halves = pl.pallas_call(
            product_kernel,
            grid=(count,),
            in_specs=[pl.BlockSpec((rows_all, 256), lambda j: (0, j)), whole(right.shape)],
            out_specs=(
                pl.BlockSpec((1, wide, 256), lambda j: (jnp.minimum(j, count // 2 - 1), 0, 0)),
                pl.BlockSpec((1, wide, 256), lambda j: (jnp.maximum(j - count // 2, 0), 0, 0)),
            ),
            out_shape=[jax.ShapeDtypeStruct((count // 2, wide, 256), bf16)] * 2,
            scratch_shapes=[pltpu.VMEM((wide, rows_all), bf16)],
            compiler_params=params(),
            cost_estimate=SMALL,
            name="product",
        )(left, right)
        return split_places(halves, wide)

    def sum_of(halves):
        def make(begin, end, arrived, kind):
            if begin >= n // 2:
                return halves[1]
            return plus(halves[0][begin:end].astype(f32), arrived, kind)

        return Scatter(make)

    t_query_back = TensorExchange(d_q_low)
    link.go(t_ffn, s_ff[4], s_ff[3], s_ff[2], during=[d_query])
    add_grads(5)
    link.go(t_attn, t_query_back, s_keys, s_ff[4], s_ff[3], during=[d_q_low, sent[5]])
    ffn_terms = t_ffn.terms()
    outputs = pl.pallas_call(
        functools.partial(finish_kernel, tuple(order)),
        grid=(1,),
        in_specs=[smem, square, whole((sp_rows, 1))] + [first_spec] * len(ffn_terms),
        out_specs=square,
        out_shape=low_square,
        compiler_params=params(),
        cost_estimate=SMALL,
        name="finish",
    )(index, mixed, live, *ffn_terms)
    link.go(t_attn, t_query_back, s_keys, s_ff[5], s_ff[4], during=[outputs])
    d_attn = t_attn.stack.reshape(-1, width)
    s_out = sum_of(product(d_attn, t_heads.rows()))
    s_query = sum_of(product(h_one_all, t_query_back.rows()))
    link.go(s_keys, s_out, s_query, s_ff[5])
    d_kv = s_keys.result()
    d_kv_low, d_k_gain = pl.pallas_call(
        key_back_kernel,
        out_shape=(
            jax.ShapeDtypeStruct((sp_rows, kv_cols), bf16),
            jax.ShapeDtypeStruct((1, HEAD), f32),
        ),
        compiler_params=pltpu.CompilerParams(vmem_limit_bytes=VMEM_LIMIT),
        cost_estimate=SMALL,
        name="key_value_back",
    )(d_kv, kv_raw, cos, sin, k_gain)
    kv_part = kv_cols // n_tensor
    t_kv_back = Direct(
        [
            lax.dynamic_slice_in_dim(d_kv_low, (tensor ^ s) * kv_part, kv_part, axis=1)
            for s in tensor_order
        ]
    )
    grad_rel, d_gain_one = pl.pallas_call(
        back_kernel,
        grid=(n_tensor,),
        in_specs=[
            head_spec,
            both_spec,
            whole((sp_rows, kv_cols)),
            whole((width, kv_cols)),
            square,
            whole((1, width)),
            square,
        ],
        out_specs=(square, whole((1, width))),
        out_shape=(
            jax.ShapeDtypeStruct((sp_rows, width), bf16),
            jax.ShapeDtypeStruct((1, width), f32),
        ),
        scratch_shapes=[pltpu.VMEM((sp_rows, width), f32)],
        compiler_params=params(),
        cost_estimate=SMALL,
        name="h_one_back",
    )(d_q_low, query_all, d_kv_low, kv_all, inputs, gain_one[None], d_mixed)
    link.go(t_kv_back, s_out, during=[grad_rel])
    grad_inputs = call(
        functools.partial(leave_kernel, tuple(order)),
        low_square,
        "leave",
        index,
        grad_rel,
        specs=[smem, vmem],
    )

    gain_parts = jnp.concatenate([d_gain_one, d_gain_two]).reshape(2, n, cols).transpose(1, 0, 2)
    head_rows = max(2 * HEAD // cols, 1)
    head_parts = jnp.concatenate([d_q_gain, d_k_gain]).reshape(1, -1)
    head_parts = jnp.pad(head_parts, ((0, 0), (0, head_rows * cols - 2 * HEAD)))
    head_parts = jnp.broadcast_to(head_parts.reshape(1, head_rows, cols), (n, head_rows, cols))
    small_parts = jnp.concatenate([gain_parts, head_parts], axis=1)
    kv_halves_back = product(h_one_all, t_kv_back.rows())

    def kv_grads(begin, end, arrived, kind):
        side = begin // (n // 2)
        own = kv_halves_back[side][begin - side * n // 2 : end - side * n // 2]
        own = jnp.concatenate([own.astype(f32), small_parts[begin:end]], axis=1)
        return plus(own, arrived, kind)

    s_kv = Scatter(kv_grads)
    link.go(s_kv, s_query, s_out, s_ff[5])
    link.go(s_kv, s_query)
    link.go(s_kv)
    sum_kv = s_kv.result()
    t_small = TensorGather(sum_kv[kv_part:])
    t_sums = TensorGather(sum_kv[:kv_part].astype(bf16))
    link.go(t_small, t_sums)
    link.go(t_small, t_sums)
    small = jnp.sum(t_small.stack, axis=0)
    sum_gains = small[:2]
    sum_heads = small[2:].reshape(-1)[: 2 * HEAD].reshape(2, HEAD)
    stack = t_sums.stack
    places = jnp.argsort(tensor ^ jnp.array(tensor_order, jnp.int32))
    sum_kv = jnp.concatenate(
        [
            lax.dynamic_index_in_dim(stack, places[i], axis=0, keepdims=False)
            for i in range(n_tensor)
        ],
        axis=0,
    ).T
    sum_out = s_out.result()
    sum_query = s_query.result().T
    sums = [s.result() for s in s_ff]
    sum_in = jnp.concatenate(
        [x[: 2 * part].reshape(2, part, cols) for part, x in zip(sizes, sums)], axis=1
    ).transpose(2, 0, 1)
    sum_down = jnp.concatenate([x[2 * part :] for part, x in zip(sizes, sums)], axis=0)
    return (
        outputs,
        grad_inputs,
        sum_query,
        sum_kv.astype(f32),
        sum_out,
        sum_in,
        sum_down,
        sum_gains,
        sum_heads,
    )


def solution(mesh):
    in_specs = (
        P(("dp", "tensor"), None),
        P(("dp", "tensor"), None),
        P("dp", "tensor"),
        P("dp", None),
        P("tensor", "dp"),
        P("dp", None, "tensor"),
        P("tensor", "dp"),
        P(None, "dp"),
        P(),
        P(),
        P(),
    )
    out_specs = (
        P(("dp", "tensor"), None),
        P(("dp", "tensor"), None),
        P("dp", "tensor"),
        P("dp", None),
        P("tensor", "dp"),
        P("dp", None, "tensor"),
        P("tensor", "dp"),
        P(None, "dp"),
        P(),
    )
    return jax.shard_map(local, mesh=mesh, in_specs=in_specs, out_specs=out_specs, check_vma=False)
```

```python
import functools

import jax
import jax.numpy as jnp
from jax import lax
from jax.experimental import layout
from jax.experimental import pallas as pl
from jax.experimental.pallas import tpu as pltpu
from jax.sharding import PartitionSpec as P

HEADS_KV = 5
HEAD = 64
SLOTS = 2048
STRETCH = 64
LANES = 128
FF_PARTS = (1, 1, 1, 1, 1, 1)
FF_LAST = len(FF_PARTS) - 1
VMEM_LIMIT = 48 * 1024 * 1024
SMALL = pl.CostEstimate(flops=1000, bytes_accessed=1000, transcendentals=0)

eps_norm = 1e-06
rope_base = 10000.0
neg_large = -1e30
f32 = jnp.float32
bf16 = jnp.bfloat16
contract_rows = (((0,), (0,)), ((), ()))
contract_cols = (((1,), (1,)), ((), ()))


def dot(a, b, dims=(((1,), (0,)), ((), ()))):
    return lax.dot_general(a, b, dims, preferred_element_type=f32)


def after(value, *deps):
    return lax.optimization_barrier((value, *deps))[0]


def masks_of(axis):
    size = lax.axis_size(axis)
    bits = [1 << i for i in range(1, size.bit_length() - 1)]
    return bits + [1]


def order_of(axis):
    order = [0]
    for mask in masks_of(axis):
        order = order + [r ^ mask for r in order]
    return order


def swap(value, axis, mask):
    size = lax.axis_size(axis)
    return lax.ppermute(value, axis, [(i, i ^ mask) for i in range(size)])


def join(first, second):
    both = jnp.concatenate([first, second], axis=0)
    return layout.with_layout_constraint(both, layout.Layout(tuple(range(both.ndim))))


def gather(value, axis):
    stack = value[None]
    for mask in masks_of(axis):
        stack = join(stack, swap(stack, axis, mask))
    return stack


def gather_rows(value, axis):
    index = lax.axis_index(axis)
    stack = value
    size = lax.axis_size(axis)
    bit = size // 2
    at = value.ndim - 2
    while bit:
        other = swap(stack, axis, bit)
        upper = (index & bit) != 0
        stack = jnp.stack(
            [jnp.where(upper, other, stack), jnp.where(upper, stack, other)], axis=at
        )
        bit //= 2
        at += 1
    return stack.reshape(value.shape[:-2] + (size,) + value.shape[-2:])


def scatter(make, axis):
    half = lax.axis_size(axis)
    arrived = []
    for mask in reversed(masks_of(axis)):
        half //= 2
        sent = make(half, 2 * half, [x[half : 2 * half] for x in arrived], bf16)
        arrived = [x[:half] for x in arrived] + [swap(sent, axis, mask)]
    return make(0, 1, arrived, f32)[0]


def phases():
    masks = masks_of("dp")
    return [masks[:1], masks[1:-1], masks[-1:]]


class Item:
    late = ()

    def bring(self, value, axis, mask):
        got = swap(value, axis, mask)
        return after(got, *self.late) if self.late else got


class Gather(Item):
    def __init__(self, value):
        self.stack, self.halves, self.phase = value[None], None, 0

    def value(self):
        return self.stack

    def advance(self, value):
        for mask in phases()[self.phase]:
            got = self.bring(value, "dp", mask)
            self.halves = (value, got)
            value = join(value, got)
        self.stack = value
        self.phase += 1
        return got

    def pieces(self):
        half = order_of("dp")[: lax.axis_size("dp") // 2]
        return [(x, [r ^ m for r in half]) for x, m in zip(self.halves, (0, masks_of("dp")[-1]))]


class GatherSoon(Item):
    def __init__(self, value):
        self.stack, self.phase = value[None], 0

    def value(self):
        return self.stack

    def advance(self, value):
        order = order_of("dp")
        if self.phase:
            got = [self.bring(value, "dp", masks_of("dp")[-1])]
        else:
            got = [self.bring(value, "dp", r) for r in order[1 : len(order) // 2]]
        both = jnp.concatenate([value, *got], axis=0)
        self.stack = layout.with_layout_constraint(both, layout.Layout(tuple(range(both.ndim))))
        self.phase += 1
        return got


class ScatterSoon(Item):
    def __init__(self, low, high):
        self.low, self.high, self.phase = low, high, 0

    def value(self):
        if self.phase == 0:
            return self.high
        self.total = self.low.astype(f32) + self.first.astype(f32)
        return self.total[1:].astype(bf16)

    def advance(self, value):
        order = order_of("dp")
        self.phase += 1
        if self.phase == 1:
            self.first = self.bring(value, "dp", order[len(order) // 2])
            return self.first
        self.rest = [
            self.bring(value[p - 1], "dp", order[p]) for p in range(1, len(order) // 2)
        ]
        return self.rest

    def result(self):
        return self.total[0] + sum(x.astype(f32) for x in self.rest)


class TensorAll(Item):
    def __init__(self, value):
        self.own = value

    def value(self):
        return self.own

    def advance(self, value):
        got = [self.bring(value, "tensor", r) for r in order_of("tensor")[1:]]
        self.stack = jnp.stack([value, *got])
        return got


class GatherLate(Item):
    def __init__(self, value):
        self.parts, self.phase = [(value[None], [0])], 0

    def value(self):
        return self.parts[max(self.phase - 2, 0)][0]

    def advance(self, value):
        masks = masks_of("dp")
        masks = [masks[-1:], masks[:1], masks[1:-1], masks[1:-1]][self.phase]
        at = max(self.phase - 2, 0)
        places = self.parts[at][1]
        for mask in masks:
            got = self.bring(value, "dp", mask)
            halves = [(value, places), (got, [r ^ mask for r in places])]
            places = places + halves[1][1]
            if mask != masks[-1] or self.phase == 0:
                value = join(value, got)
        if self.phase == 0:
            self.parts = [(value, places)]
        elif self.phase == 1:
            self.parts = halves
        elif self.phase == 2:
            self.parts, self.first = [None, self.parts[1]], halves
        else:
            self.parts = self.first + halves
        self.phase += 1
        return got

    def pieces(self):
        return self.parts


class Scatter(Item):
    def __init__(self, make):
        self.make, self.half, self.arrived, self.phase = make, lax.axis_size("dp"), [], 2
        self.raw = []

    def value(self):
        half = self.half // 2
        return self.make(half, 2 * half, [x[half : 2 * half] for x in self.arrived], bf16)

    def advance(self, value):
        for k, mask in enumerate(reversed(phases()[self.phase])):
            if k:
                value = self.value()
            self.half //= 2
            got = self.bring(value, "dp", mask)
            self.arrived = [x[: self.half] for x in self.arrived] + [got]
            self.raw.append(got)
        self.phase -= 1
        return got

    def result(self):
        return self.make(0, 1, self.arrived, f32)[0]


class TensorGather(Item):
    def __init__(self, value):
        self.stack, self.masks = value[None], masks_of("tensor")

    def value(self):
        return self.stack

    def advance(self, value):
        got = self.bring(value, "tensor", self.masks[0])
        self.halves = (value, got)
        self.stack, self.masks = join(value, got), self.masks[1:]
        return got

    def rows(self):
        return [x.reshape(-1, x.shape[-1]) for x in self.halves]


class PairRows(Item):
    def __init__(self, value):
        self.stack = value

    def value(self):
        return self.stack

    def advance(self, value):
        got = self.bring(value, "tensor", 1)
        upper = (lax.axis_index("tensor") & 1) != 0
        self.stack = jnp.stack(
            [jnp.where(upper, got, value), jnp.where(upper, value, got)], axis=value.ndim - 2
        )
        return got


class TensorScatter(Item):
    def __init__(self, sums):
        self.sums, self.masks, self.arrived = sums, masks_of("tensor")[::-1], []

    def value(self):
        half = 1 << (len(self.masks) - 1)
        if half == self.sums[1].shape[0]:
            return self.sums[1]
        return plus(
            self.sums[0][half : 2 * half].astype(f32),
            [x[half : 2 * half] for x in self.arrived],
            bf16,
        )

    def advance(self, value):
        self.arrived.append(self.bring(value, "tensor", self.masks[0]))
        self.masks = self.masks[1:]
        return self.arrived[-1]

    def terms(self):
        return [self.sums[0], *self.arrived]


class TensorDirect(Item):
    def __init__(self, parts):
        self.parts = list(parts)

    def value(self):
        return self.parts

    def advance(self, value):
        order = order_of("tensor")
        self.got = [self.bring(value[p], "tensor", order[p]) for p in range(1, len(order))]
        return self.got

    def terms(self):
        return [x[None] for x in [self.parts[0], *self.got]]


class TensorExchange(Item):
    def __init__(self, stack):
        self.stack, self.masks = stack[:, None], masks_of("tensor")

    def value(self):
        return self.stack[1::2]

    def advance(self, value):
        got = self.bring(value, "tensor", self.masks[0])
        self.stack = jnp.concatenate([self.stack[0::2], got], axis=1)
        self.masks = self.masks[1:]
        return got

    def rows(self):
        return self.stack.reshape((-1,) + self.stack.shape[3:])


class Direct(Item):
    def __init__(self, parts):
        self.parts = parts

    def value(self):
        return jnp.stack(self.parts)

    def advance(self, value):
        order = order_of("tensor")
        got = [value[0]] + [
            self.bring(value[p], "tensor", order[p]) for p in range(1, len(order))
        ]
        self.all = jnp.concatenate(got, axis=0)
        return self.all

    def rows(self):
        return self.all


class Rounds:
    def __init__(self):
        self.done = []

    def go(self, *items, ends=(), during=()):
        done = list(ends)
        for item in items:
            value = item.value()
            if self.done:
                value = after(value, *self.done)
            item.late = during
            got = item.advance(value)
            done += got if isinstance(got, list) else [got]
        self.done = done


def plus(total, arrived, kind):
    for other in arrived:
        total = total + other.astype(f32)
    return total.astype(kind)


def scaled_norm(value_in, gain_vec):
    return (
        value_in
        * lax.rsqrt(jnp.mean(value_in * value_in, axis=-1, keepdims=True) + eps_norm)
        * gain_vec
    )


def silu_product(gate, up_part):
    return gate * jax.nn.sigmoid(gate) * up_part


def params(steps=1):
    return pltpu.CompilerParams(
        dimension_semantics=("arbitrary",) * steps, vmem_limit_bytes=VMEM_LIMIT
    )


def swap_halves(value):
    half = HEAD // 2
    return jnp.concatenate([value[:, half:], value[:, :half]], axis=1)


def rope_one(raw, gain, cos, sin, factor):
    scale = lax.rsqrt(jnp.mean(raw * raw, axis=-1, keepdims=True) + eps_norm)
    normed = raw * scale * gain
    return (normed * cos + swap_halves(normed) * sin) * factor


def rope_back(raw, gain, cos, sin, factor, grad):
    grad = grad * factor
    grad = grad * cos - swap_halves(grad) * sin
    scale = lax.rsqrt(jnp.mean(raw * raw, axis=-1, keepdims=True) + eps_norm)
    weighted = grad * gain
    back = scale * weighted - raw * (
        scale * scale * scale * jnp.mean(raw * weighted, axis=-1, keepdims=True)
    )
    return back, jnp.sum(grad * raw * scale, axis=0, keepdims=True)


def query_kernel(h_ref, w_ref, cos_ref, sin_ref, gain_ref, raw_ref, out_ref):
    cols = w_ref.shape[3]
    raw = sum(
        dot(h_ref[:, r * cols : (r + 1) * cols], w_ref[0, r], contract_cols)
        for r in range(w_ref.shape[1])
    )
    raw_ref[0] = raw
    rows, blocks = out_ref.shape[0], out_ref.shape[2]
    for h in range(HEADS_KV):
        turned = rope_one(
            raw[:, h * HEAD : (h + 1) * HEAD], gain_ref[...], cos_ref[...], sin_ref[...], 0.125
        )
        wide = jnp.concatenate([turned, jnp.zeros_like(turned)], axis=1).astype(bf16)
        out_ref[:, h, :, 0] = wide.reshape(rows, blocks, STRETCH, LANES)


def key_kernel(h_ref, w_ref, cos_ref, sin_ref, gain_ref, raw_ref, out_ref):
    raw = dot(h_ref[...], w_ref[...])
    raw_ref[...] = raw
    rows, blocks = out_ref.shape[0], out_ref.shape[2]
    for h in range(HEADS_KV):
        turned = rope_one(
            raw[:, h * HEAD : (h + 1) * HEAD], gain_ref[...], cos_ref[...], sin_ref[...], 1.0
        )
        start = (HEADS_KV + h) * HEAD
        wide = jnp.concatenate([turned, raw[:, start : start + HEAD]], axis=1).astype(bf16)
        out_ref[:, h] = wide.reshape(rows, blocks, STRETCH, LANES)


def load_keys(halves, kv, kvt):
    places = [(half, i) for half in halves for i in range(half.shape[0])]
    group = len(places) * STRETCH
    for g in range(halves[0].shape[3]):
        for r, (half, i) in enumerate(places):
            start = g * group + r * STRETCH
            kv[start : start + STRETCH, :] = half[i, 0, 0, g]
    kvt[...] = kv[...].T
    return group


def attend_kernel(q_ref, limit_ref, keypos_ref, low_ref, high_ref, out_ref, kv, kvt):
    blocks = q_ref.shape[2]
    group = load_keys((low_ref, high_ref), kv, kvt)
    for b in range(blocks):
        span = (b + 1) * group
        q = q_ref[0, 0, b].reshape(-1, LANES)
        scores = dot(kv[:span], q, contract_cols)
        scores = jnp.where(keypos_ref[0, :span] <= limit_ref[0, b], scores, neg_large)
        top = jnp.max(scores, axis=0, keepdims=True)
        weights = jnp.exp(scores - top)
        total = jnp.sum(weights, axis=0, keepdims=True)
        heads = dot(kvt[:, :span], weights.astype(bf16)) / total
        out_ref[0, 0, b] = heads.T.astype(bf16).reshape(q_ref.shape[3:])


def attend_back_kernel(q_ref, g_ref, limit_ref, keypos_ref, low_ref, high_ref, *rest):
    dq_ref, dlow_ref, dhigh_ref, kv, kvt, acc = rest[-6:]
    blocks = q_ref.shape[2]
    group = load_keys((low_ref, high_ref), kv, kvt)
    acc[...] = jnp.zeros_like(acc)
    for b in range(blocks):
        span = (b + 1) * group
        q = q_ref[0, 0, b].reshape(-1, LANES)
        grad = g_ref[0, 0, b].reshape(-1, LANES)
        scores = dot(kv[:span], q, contract_cols)
        scores = jnp.where(keypos_ref[0, :span] <= limit_ref[0, b], scores, neg_large)
        top = jnp.max(scores, axis=0, keepdims=True)
        weights = jnp.exp(scores - top)
        probs = weights * (1.0 / jnp.sum(weights, axis=0, keepdims=True))
        d_probs = dot(kv[:span], grad, contract_cols)
        delta = jnp.sum(probs * d_probs, axis=0, keepdims=True)
        d_scores = (probs * (d_probs - delta)).astype(bf16)
        dq = dot(kvt[:, :span], d_scores)
        dq_ref[0, 0, b] = dq.T.reshape(q_ref.shape[3:])
        acc[:span] += dot(d_scores, q) + dot(probs.astype(bf16), grad)
    count = dlow_ref.shape[0]
    for out, first in ((dlow_ref, 0), (dhigh_ref, count)):
        for r in range(count):
            for g in range(blocks):
                start = g * group + (first + r) * STRETCH
                out[r, 0, 0, g] = acc[start : start + STRETCH].astype(bf16)


def out_kernel(o_ref, w_low, w_high, x_ref, live_ref, gain_ref, mixed_ref, h_ref, heads_ref):
    rows = heads_ref.shape[1]
    heads = jnp.concatenate(
        [o_ref[:, h, :, 0].reshape(rows, LANES)[:, HEAD:] for h in range(HEADS_KV)], axis=1
    )
    heads_ref[0] = heads
    cols = w_low.shape[3]
    low = pl.program_id(0) < pl.num_programs(0) // 2

    @pl.when(pl.program_id(0) == 0)
    def _():
        mixed_ref[...] = jnp.zeros_like(mixed_ref)

    for r in range(w_low.shape[1]):
        here = jnp.where(low, w_low[0, r], w_high[0, r])
        mixed_ref[:, r * cols : (r + 1) * cols] += dot(heads, here)

    @pl.when(pl.program_id(0) == pl.num_programs(0) - 1)
    def _():
        mixed = x_ref[...].astype(f32) + live_ref[...] * mixed_ref[...]
        mixed_ref[...] = mixed
        h_ref[...] = scaled_norm(mixed, gain_ref[...]).astype(bf16)


def norm_back(value, gain, grad):
    scale = lax.rsqrt(jnp.mean(value * value, axis=-1, keepdims=True) + eps_norm)
    weighted = grad * gain
    inner = jnp.mean(value * weighted, axis=-1, keepdims=True)
    back = scale * weighted - value * (scale * scale * scale * inner)
    return back, jnp.sum(grad * value * scale, axis=0, keepdims=True)


def mixed_back_kernel(mixed_ref, cot_ref, gain_ref, live_ref, *rest):
    terms, (d_mixed_ref, d_attn_ref, dgain_ref) = rest[:-3], rest[-3:]
    grad = sum(ref[0].astype(f32) for ref in terms)
    back, dgain_ref[...] = norm_back(mixed_ref[...], gain_ref[...], grad)
    d_mixed = cot_ref[...].astype(f32) + back
    d_mixed_ref[...] = d_mixed
    d_attn_ref[...] = (live_ref[...] * d_mixed).astype(bf16)


def heads_back_kernel(d_ref, w_low, w_high, out_ref):
    cols = w_low.shape[3]
    low = pl.program_id(0) < pl.num_programs(0) // 2
    grad = sum(
        dot(
            d_ref[:, r * cols : (r + 1) * cols],
            jnp.where(low, w_low[0, r], w_high[0, r]),
            contract_cols,
        )
        for r in range(w_low.shape[1])
    )
    rows, blocks = out_ref.shape[0], out_ref.shape[2]
    for h in range(HEADS_KV):
        part = grad[:, h * HEAD : (h + 1) * HEAD]
        wide = jnp.concatenate([jnp.zeros_like(part), part], axis=1).astype(bf16)
        out_ref[:, h, :, 0] = wide.reshape(rows, blocks, STRETCH, LANES)


def query_back_kernel(dq_ref, raw_ref, cos_ref, sin_ref, gain_ref, out_ref, dgain_ref):
    @pl.when(pl.program_id(0) == 0)
    def _():
        dgain_ref[...] = jnp.zeros_like(dgain_ref)

    raw = raw_ref[0]
    parts = []
    for h in range(HEADS_KV):
        grad = dq_ref[:, h, :, 0].reshape(raw.shape[0], LANES)[:, :HEAD]
        back, dgain = rope_back(
            raw[:, h * HEAD : (h + 1) * HEAD],
            gain_ref[...],
            cos_ref[...],
            sin_ref[...],
            0.125,
            grad,
        )
        parts.append(back)
        dgain_ref[...] += dgain
    out_ref[0] = jnp.concatenate(parts, axis=1).astype(bf16)


def key_back_kernel(sum_ref, raw_ref, cos_ref, sin_ref, gain_ref, out_ref, dgain_ref):
    raw = raw_ref[...]
    keys, values = [], []
    total = jnp.zeros_like(dgain_ref)
    for h in range(HEADS_KV):
        both = sum_ref[:, h].reshape(raw.shape[0], LANES)
        back, dgain = rope_back(
            raw[:, h * HEAD : (h + 1) * HEAD],
            gain_ref[...],
            cos_ref[...],
            sin_ref[...],
            1.0,
            both[:, :HEAD],
        )
        keys.append(back)
        values.append(both[:, HEAD:])
        total = total + dgain
    dgain_ref[...] = total
    out_ref[...] = jnp.concatenate(keys + values, axis=1).astype(bf16)


def back_kernel(
    dq_ref, wq_ref, dkv_ref, wkv_ref, x_ref, gain_ref, d_mixed_ref, out_ref, dgain_ref, acc
):
    @pl.when(pl.program_id(0) == 0)
    def _():
        acc[...] = dot(dkv_ref[...], wkv_ref[...], contract_cols)

    cols = wq_ref.shape[3]
    for r in range(wq_ref.shape[1]):
        acc[:, r * cols : (r + 1) * cols] += dot(dq_ref[0], wq_ref[0, r])

    @pl.when(pl.program_id(0) == pl.num_programs(0) - 1)
    def _():
        back, dgain_ref[...] = norm_back(x_ref[...].astype(f32), gain_ref[...], acc[...])
        out_ref[...] = (d_mixed_ref[...] + back).astype(bf16)


def turn_kernel(x_ref, out_ref):
    out_ref[...] = x_ref[...].T


def shards_kernel(in_ref, down_ref, *parts):
    ff = down_ref.shape[0]
    start = 0
    for ref in parts:
        part = ref.shape[1] // 3
        ref[:, :part] = in_ref[:, start : start + part]
        ref[:, part : 2 * part] = in_ref[:, ff + start : ff + start + part]
        ref[:, 2 * part :] = down_ref[start : start + part, :].T
        start += part


def turn_columns(order, back, index, value):
    size = len(order)
    cols = value.shape[1] // size

    def pick(value, places):
        return jnp.concatenate([value[:, p * cols : (p + 1) * cols] for p in places], axis=1)

    if back:
        value = pick(value, [order.index(i) for i in range(size)])
    bit = 1
    while bit < size:
        value = jnp.where((index & bit) != 0, pick(value, [i ^ bit for i in range(size)]), value)
        bit *= 2
    return value if back else pick(value, order)


def enter_kernel(order, index_ref, x_ref, cot_ref, live_ref, x_out, cot_out, d_ffn_out):
    x_out[...] = turn_columns(order, False, index_ref[0], x_ref[...].astype(f32)).astype(bf16)
    cot = turn_columns(order, False, index_ref[0], cot_ref[...].astype(f32))
    cot_out[...] = cot.astype(bf16)
    d_ffn_out[...] = (cot * live_ref[...]).astype(bf16)


def leave_kernel(order, index_ref, x_ref, out_ref):
    value = x_ref[...].astype(f32)
    out_ref[...] = turn_columns(order, True, index_ref[0], value).astype(bf16)


def finish_kernel(order, index_ref, mixed_ref, live_ref, *rest):
    terms, out_ref = rest[:-1], rest[-1]
    ffn = sum(ref[0].astype(f32) for ref in terms)
    value = mixed_ref[...] + live_ref[...] * ffn
    out_ref[...] = turn_columns(order, True, index_ref[0], value).astype(bf16)


def product_kernel(left_low, left_high, right_ref, low_ref, high_ref, turned):
    @pl.when(pl.program_id(0) == 0)
    def _():
        turned[...] = right_ref[...].T

    out = halves_product(turned[...], left_low, left_high).astype(bf16)
    low = pl.program_id(0) < pl.num_programs(0) // 2
    span = low_ref.shape[2]
    for out_ref, here in ((low_ref, low), (high_ref, jnp.logical_not(low))):

        @pl.when(here)
        def _(out_ref=out_ref):
            for p in range(out_ref.shape[0]):
                out_ref[p] = out[:, p * span : (p + 1) * span]


def pick_columns(value, places, cols):
    if places == list(range(places[0], places[0] + len(places))):
        return value[:, places[0] * cols : (places[-1] + 1) * cols]
    return jnp.concatenate([value[:, p * cols : (p + 1) * cols] for p in places], axis=1)


def hidden_kernel(all_places, h_low, h_high, d_low, d_high, *refs):
    pieces, (hidden_ref, d_gate_up_ref, turned_ref) = refs[:-3], refs[-3:]
    part = hidden_ref.shape[1]
    low = pl.program_id(0) < pl.num_programs(0) // 2
    h = jnp.where(low, h_low[...], h_high[...])
    d = jnp.where(low, d_low[...], d_high[...])
    gate_up = d_hidden = None
    for places, ref in zip(all_places, pieces):
        cols = ref.shape[0] // len(places)
        first = dot(pick_columns(h, places, cols), ref[:, : 2 * part])
        second = dot(pick_columns(d, places, cols), ref[:, 2 * part :])
        gate_up = first if gate_up is None else gate_up + first
        d_hidden = second if d_hidden is None else d_hidden + second
    gate, up = gate_up[:, :part], gate_up[:, part:]
    sig = jax.nn.sigmoid(gate)
    swish = gate * sig
    hidden = (swish * up).astype(bf16)
    d_gate = (d_hidden * up * (sig + swish * (1.0 - sig))).astype(bf16)
    d_up = (d_hidden * swish).astype(bf16)
    hidden_ref[...] = hidden
    d_gate_up_ref[:, :part] = d_gate
    d_gate_up_ref[:, part:] = d_up
    turned_ref[:part] = d_gate.T
    turned_ref[part : 2 * part] = d_up.T
    turned_ref[2 * part :] = hidden.T


def halves_product(left, low_ref, high_ref):
    middle = low_ref.shape[0]
    return dot(left[:, :middle], low_ref[...]) + dot(left[:, middle:], high_ref[...])


def grads_kernel(h_low, h_high, d_low, d_high, turned_ref, low_ref, high_ref):
    split = turned_ref.shape[0] // 3 * 2
    first = halves_product(turned_ref[:split], h_low, h_high).astype(bf16)
    second = halves_product(turned_ref[split:], d_low, d_high).astype(bf16)
    low = pl.program_id(0) < pl.num_programs(0) // 2
    span = low_ref.shape[2]
    for out_ref, here in ((low_ref, low), (high_ref, jnp.logical_not(low))):

        @pl.when(here)
        def _(out_ref=out_ref):
            for p in range(out_ref.shape[0]):
                out_ref[p, :split] = first[:, p * span : (p + 1) * span]
                out_ref[p, split:] = second[:, p * span : (p + 1) * span]


def collect_kernel(count, each, *refs):
    in_ref, down_ref = refs[-2:]
    part = down_ref.shape[0]
    for c in range(count):

        @pl.when(pl.program_id(0) == c)
        def _(c=c):
            total = sum(ref[0].astype(f32) for ref in refs[c * each : (c + 1) * each])
            in_ref[:, 0, :] = total[:part].T
            in_ref[:, 1, :] = total[part : 2 * part].T
            down_ref[...] = total[2 * part :]


def back_sum_kernel(all_places, *refs):
    count = len(all_places)
    half = refs[-1].shape[1] // 2
    totals = [None, None]
    at = count
    for c, pieces in enumerate(all_places):
        terms = [dot(refs[c][...], refs[at + i][...], contract_cols) for i in range(len(pieces))]
        at += len(pieces)
        if len(pieces) > 2:
            blocks = {}
            for places, term in zip(pieces, terms):
                cols = term.shape[1] // len(places)
                for i, p in enumerate(places):
                    blocks[p] = term[:, i * cols : (i + 1) * cols]
            middle = len(blocks) // 2
            terms = [
                jnp.concatenate([blocks[side * middle + i] for i in range(middle)], axis=1)
                for side in range(2)
            ]
        totals = [t if old is None else old + t for old, t in zip(totals, terms)]
    outs = refs[at:]
    span = outs[0].shape[0]
    rows = totals[0].shape[0]
    each = max(rows // span, 1)
    for step in range(len(outs) // each):

        @pl.when(pl.program_id(0) == step)
        def _(step=step):
            for i in range(each):
                for side in range(2):
                    block = totals[side][i * span : (i + 1) * span].astype(bf16)
                    outs[step * each + i][:, side * half : (side + 1) * half] = block


def whole(shape):
    return pl.BlockSpec(shape, lambda *_: (0,) * len(shape))


def local(
    inputs,
    cotangent,
    w_query,
    w_kv,
    w_out,
    w_in,
    w_down,
    norm_gains,
    head_gains,
    lengths,
    slot_blocks,
):
    sp_rows, width = inputs.shape
    n = lax.axis_size("dp")
    n_tensor = lax.axis_size("tensor")
    dp = lax.axis_index("dp")
    tensor = lax.axis_index("tensor")
    seq_count = lengths.shape[0]
    row_span = sp_rows * n_tensor // seq_count
    blocks = row_span // STRETCH
    rows = sp_rows // row_span
    per_row = SLOTS // STRETCH
    cols = width // n
    q_cols = w_query.shape[1]
    kv_cols = w_kv.shape[1]
    ff = w_down.shape[0]
    order = order_of("dp")
    tensor_order = order_of("tensor")
    rels = jnp.array(order, jnp.int32)

    smem = pl.BlockSpec(memory_space=pltpu.SMEM)

    def call(kernel, out_shape, name, *args, specs=None):
        return pl.pallas_call(
            kernel,
            in_specs=specs,
            out_shape=out_shape,
            compiler_params=pltpu.CompilerParams(vmem_limit_bytes=VMEM_LIMIT),
            cost_estimate=SMALL,
            name=name,
        )(*args)

    table = slot_blocks.reshape(n, n_tensor, rows, blocks)
    mine = lax.dynamic_index_in_dim(table, tensor, axis=1, keepdims=False)[dp ^ rels]
    inside = jnp.arange(STRETCH, dtype=jnp.int32)
    key_pos = (mine % per_row * STRETCH)[..., None] + inside
    own_pos = key_pos[0]
    own_len = lengths[mine[0] // per_row][..., None]
    live = (own_pos < own_len).astype(f32).reshape(sp_rows, 1)
    limit = jnp.minimum(own_pos, own_len - 1)
    limit = jnp.broadcast_to(limit[:, :, None, None, :], (rows, blocks, 1, n_tensor, STRETCH))
    limit = limit.reshape(rows, blocks, 1, n_tensor * STRETCH)
    key_pos = key_pos.transpose(1, 2, 0, 3).reshape(rows, SLOTS, 1)
    half = HEAD // 2
    frequency = rope_base ** (-2.0 * jnp.arange(half, dtype=f32) / HEAD)
    angles = own_pos.reshape(sp_rows, 1).astype(f32) * frequency
    cosine, sine = jnp.cos(angles), jnp.sin(angles)
    cos = jnp.concatenate([cosine, cosine], axis=1)
    sin = jnp.concatenate([-sine, sine], axis=1)
    head_float = head_gains.astype(f32)
    q_gain, k_gain = head_float[0:1], head_float[1:2]

    vmem = pl.BlockSpec(memory_space=pltpu.VMEM)
    index = dp.reshape(1)
    low_square = jax.ShapeDtypeStruct((sp_rows, width), bf16)
    inputs, cotangent, d_ffn_own = call(
        functools.partial(enter_kernel, tuple(order)),
        [low_square] * 3,
        "enter",
        index,
        inputs,
        cotangent,
        live,
        specs=[smem, vmem, vmem, vmem],
    )
    inputs_f = inputs.astype(f32)
    part = w_kv.shape[0] // 2
    kv_shard = lax.dynamic_slice_in_dim(w_kv, (tensor & 1) * part, part, axis=0)
    unit = ff // sum(FF_PARTS)
    sizes = [size * unit for size in FF_PARTS]
    query_shard = call(
        turn_kernel, jax.ShapeDtypeStruct((q_cols, cols), bf16), "turn", w_query, specs=[vmem]
    )
    shards = call(
        shards_kernel,
        [jax.ShapeDtypeStruct((cols, 3 * part), bf16) for part in sizes],
        "shards",
        w_in.reshape(cols, 2 * ff),
        w_down,
        specs=[vmem, vmem],
    )
    link = Rounds()
    g_kv, g_gains = GatherSoon(kv_shard), Gather(norm_gains)
    g_query, g_out = Gather(query_shard), Gather(w_out)
    g_ff = [Gather(x) for x in shards[:-1]] + [GatherLate(shards[-1])]
    link.go(g_kv, g_gains, g_query)
    link.go(g_kv, g_gains, g_query, g_out, g_ff[0])
    t_kv = PairRows(g_kv.stack)
    link.go(t_kv, g_gains, g_query, g_out)
    gains = g_gains.stack.transpose(1, 0, 2).reshape(2, width).astype(f32)
    gain_one, gain_two = gains[0], gains[1]
    h_one = scaled_norm(inputs_f, gain_one).astype(bf16)
    t_query = TensorGather(g_query.stack)
    kv_all = t_kv.stack.reshape(width, kv_cols)
    t_d_ffn = TensorGather(d_ffn_own)

    packed = (rows, HEADS_KV, blocks, n_tensor, STRETCH, LANES)
    packed_kv = (rows, HEADS_KV, blocks, STRETCH, LANES)
    both_spec = pl.BlockSpec((1, n, q_cols, cols), lambda s: (s, 0, 0, 0))
    half_specs = [
        pl.BlockSpec(
            (1, n, q_cols, cols), lambda s: (jnp.minimum(s, n_tensor // 2 - 1), 0, 0, 0)
        ),
        pl.BlockSpec(
            (1, n, q_cols, cols), lambda s: (jnp.maximum(s - n_tensor // 2, 0), 0, 0, 0)
        ),
    ]
    kv_raw, kv_own = pl.pallas_call(
        key_kernel,
        out_shape=(
            jax.ShapeDtypeStruct((sp_rows, kv_cols), f32),
            jax.ShapeDtypeStruct(packed_kv, bf16),
        ),
        compiler_params=pltpu.CompilerParams(vmem_limit_bytes=VMEM_LIMIT),
        cost_estimate=SMALL,
        name="key_value",
    )(h_one, kv_all, cos, sin, k_gain)
    g_keys = Gather(kv_own)
    link.go(t_query, g_out, g_ff[5], g_ff[0], g_keys)
    t_out = TensorGather(g_out.stack)
    link.go(t_query, t_out, g_keys, g_ff[0], g_ff[1])
    query_all = t_query.stack
    one_head = (sp_rows, HEAD)
    part_spec = pl.BlockSpec(
        (rows, HEADS_KV, blocks, 1, STRETCH, LANES), lambda s: (0, 0, 0, s, 0, 0)
    )
    q_raw, queries = pl.pallas_call(
        query_kernel,
        grid=(n_tensor,),
        in_specs=[
            whole((sp_rows, width)),
            both_spec,
            whole(one_head),
            whole(one_head),
            whole((1, HEAD)),
        ],
        out_specs=(pl.BlockSpec((1, sp_rows, q_cols), lambda s: (s, 0, 0)), part_spec),
        out_shape=(
            jax.ShapeDtypeStruct((n_tensor, sp_rows, q_cols), f32),
            jax.ShapeDtypeStruct(packed, bf16),
        ),
        compiler_params=params(),
        cost_estimate=SMALL,
        name="query",
    )(h_one, query_all, cos, sin, q_gain)
    link.go(t_out, t_d_ffn, g_keys, g_ff[1], g_ff[2], during=[queries, key_pos])
    kv_halves = g_keys.halves
    q_spec = pl.BlockSpec(
        (1, 1, blocks, n_tensor, STRETCH, LANES), lambda i, h: (i, h, 0, 0, 0, 0)
    )
    kv_spec = pl.BlockSpec(
        (n // 2, 1, 1, blocks, STRETCH, LANES), lambda i, h: (0, i, h, 0, 0, 0)
    )
    limit_spec = pl.BlockSpec(
        (1, blocks, 1, n_tensor * STRETCH), lambda i, h: (i, 0, 0, 0)
    )
    pos_spec = pl.BlockSpec((1, SLOTS, 1), lambda i, h: (i, 0, 0))
    heads_packed = pl.pallas_call(
        attend_kernel,
        grid=(rows, HEADS_KV),
        in_specs=[q_spec, limit_spec, pos_spec] + [kv_spec] * 2,
        out_specs=q_spec,
        out_shape=jax.ShapeDtypeStruct(packed, bf16),
        scratch_shapes=[pltpu.VMEM((SLOTS, LANES), bf16), pltpu.VMEM((LANES, SLOTS), bf16)],
        compiler_params=params(2),
        cost_estimate=SMALL,
        name="attend",
    )(queries, limit, key_pos, *kv_halves)

    heads_shape = (n_tensor, sp_rows, q_cols)
    head_spec = pl.BlockSpec((1, sp_rows, q_cols), lambda s: (s, 0, 0))
    square = whole((sp_rows, width))
    mixed, h_two_own, attn_heads = pl.pallas_call(
        out_kernel,
        grid=(n_tensor,),
        in_specs=[
            part_spec,
            *half_specs,
            square,
            whole((sp_rows, 1)),
            whole((1, width)),
        ],
        out_specs=(square, square, head_spec),
        out_shape=(
            jax.ShapeDtypeStruct((sp_rows, width), f32),
            jax.ShapeDtypeStruct((sp_rows, width), bf16),
            jax.ShapeDtypeStruct(heads_shape, bf16),
        ),
        compiler_params=params(),
        cost_estimate=SMALL,
        name="out",
    )(heads_packed, *t_out.halves, inputs, live, gain_two[None])
    t_heads = TensorExchange(attn_heads)

    t_h_two = TensorGather(h_two_own)
    t_h_one = TensorGather(h_one)
    rows_all = sp_rows * n_tensor
    link.go(t_d_ffn, g_ff[1], g_ff[2], g_ff[3], during=[h_two_own])
    d_ffn = t_d_ffn.rows()
    link.go(t_h_two, g_ff[2], g_ff[3], g_ff[4])
    link.go(t_h_two, t_h_one, g_ff[3], g_ff[4], g_ff[5])
    h_two = t_h_two.rows()
    steps = n_tensor // 2
    row_block = lambda span: pl.BlockSpec((rows_all // steps, span), lambda i: (i, 0))
    low_rows = pl.BlockSpec((sp_rows, width), lambda i: (jnp.minimum(i, n_tensor // 2 - 1), 0))
    high_rows = pl.BlockSpec((sp_rows, width), lambda i: (jnp.maximum(i - n_tensor // 2, 0), 0))
    weights, hiddens, d_gate_ups, turned = [], [], [], []

    def hidden_part(g, part):
        pieces = [
            (x.reshape(len(rs) * cols, 3 * part), [order.index(r) for r in rs])
            for x, rs in g.pieces()
        ]
        weights.append(pieces)
        hidden, d_gate_up, flipped = pl.pallas_call(
            functools.partial(hidden_kernel, [places for _, places in pieces]),
            grid=(n_tensor,),
            in_specs=[low_rows, high_rows] * 2 + [whole(x.shape) for x, _ in pieces],
            out_specs=(
                pl.BlockSpec((sp_rows, part), lambda i: (i, 0)),
                pl.BlockSpec((sp_rows, 2 * part), lambda i: (i, 0)),
                pl.BlockSpec((3 * part, sp_rows), lambda i: (0, i)),
            ),
            out_shape=(
                jax.ShapeDtypeStruct((rows_all, part), bf16),
                jax.ShapeDtypeStruct((rows_all, 2 * part), bf16),
                jax.ShapeDtypeStruct((3 * part, rows_all), bf16),
            ),
            compiler_params=params(),
            cost_estimate=SMALL,
        name="hidden",
        )(*h_two, *d_ffn, *[x for x, _ in pieces])
        hiddens.append(hidden)
        d_gate_ups.append(d_gate_up)
        turned.append(flipped)

    def split_places(halves, wide):
        if cols == 256:
            return halves
        return [
            x.reshape(-1, wide, 256 // cols, cols).transpose(0, 2, 1, 3).reshape(n // 2, wide, cols)
            for x in halves
        ]

    def grads_of(flipped):
        wide = flipped.shape[0]
        count = width // 256
        grid = width // 512
        low_spec = pl.BlockSpec((2, wide, 256), lambda j: (jnp.minimum(j, grid // 2 - 1), 0, 0))
        high_spec = pl.BlockSpec((2, wide, 256), lambda j: (jnp.maximum(j - grid // 2, 0), 0, 0))
        block = pl.BlockSpec((rows_all // 2, 512), lambda j: (0, j))
        halves = pl.pallas_call(
            grads_kernel,
            grid=(grid,),
            in_specs=[block] * 4 + [whole(flipped.shape)],
            out_specs=(low_spec, high_spec),
            out_shape=[jax.ShapeDtypeStruct((count // 2, wide, 256), bf16)] * 2,
            compiler_params=params(),
            cost_estimate=SMALL,
            name="weight_grads",
        )(*h_two, *d_ffn, flipped)
        halves = split_places(halves, wide)

        def make(begin, end, arrived, kind):
            if begin >= n // 2:
                return halves[1]
            return plus(halves[0][begin:end].astype(f32), arrived, kind)

        lows.append(halves[0])
        return Scatter(make), halves[1]

    s_ff, sent, lows = [], [], []

    def add_grads(c):
        item, first = grads_of(after(turned[c], *link.done) if c > 2 else turned[c])
        s_ff.append(item)
        sent.append(first)

    def back_sum(parts, down, pieces):
        span = rows_all // pieces
        def weight_spec(x, w):
            span = x.shape[1]
            at = (w.shape[1] - span) // span if down else 0
            return pl.BlockSpec(
                (w.shape[0], span), lambda i: (0, at), pipeline_mode=pl.Buffered(1)
            )

        return pl.pallas_call(
            functools.partial(
                back_sum_kernel, [[places for _, places in pieces] for pieces in weights]
            ),
            grid=(steps,),
            in_specs=[row_block(x.shape[1]) for x in parts]
            + [weight_spec(x, w) for x, pieces in zip(parts, weights) for w, _ in pieces],
            out_specs=[whole((span, width))] * pieces,
            out_shape=[jax.ShapeDtypeStruct((span, width), bf16)] * pieces,
            compiler_params=params(),
            cost_estimate=SMALL,
            name="back_sum",
        )(*parts, *[w for pieces in weights for w, _ in pieces])

    hidden_part(g_ff[0], sizes[0])
    hidden_part(g_ff[1], sizes[1])
    hidden_part(g_ff[2], sizes[2])
    add_grads(0)
    link.go(t_h_one, t_heads, g_ff[4], g_ff[5], during=[*turned, *sent])
    h_one_all = t_h_one.rows()
    hidden_part(g_ff[3], sizes[3])
    hidden_part(g_ff[4], sizes[4])
    add_grads(1)
    add_grads(2)
    link.go(t_heads, s_ff[0], g_ff[5], during=[*turned[3:], *sent[1:]])
    hidden_part(g_ff[5], sizes[5])
    t_back = TensorDirect(back_sum(d_gate_ups, False, n_tensor))
    link.go(s_ff[1], s_ff[0], during=t_back.parts)
    add_grads(3)
    add_grads(4)
    t_ffn = TensorScatter(
        [x.reshape(n_tensor // 2, sp_rows, width) for x in back_sum(hiddens, True, 2)]
    )
    link.go(t_back, s_ff[2], s_ff[1], during=[*t_ffn.sums, *sent[3:]])
    first_spec = pl.BlockSpec((1, sp_rows, width), lambda i: (0, 0, 0))
    back_terms = t_back.terms()
    d_mixed, d_attn_own, d_gain_two = pl.pallas_call(
        mixed_back_kernel,
        grid=(1,),
        in_specs=[square, square, whole((1, width)), whole((sp_rows, 1))]
        + [first_spec] * len(back_terms),
        out_specs=(square, square, whole((1, width))),
        out_shape=(
            jax.ShapeDtypeStruct((sp_rows, width), f32),
            jax.ShapeDtypeStruct((sp_rows, width), bf16),
            jax.ShapeDtypeStruct((1, width), f32),
        ),
        compiler_params=params(),
        cost_estimate=SMALL,
        name="mixed_back",
    )(mixed, cotangent, gain_two[None], live, *back_terms)

    d_heads = pl.pallas_call(
        heads_back_kernel,
        grid=(n_tensor,),
        in_specs=[whole((sp_rows, width)), *half_specs],
        out_specs=part_spec,
        out_shape=jax.ShapeDtypeStruct(packed, bf16),
        compiler_params=params(),
        cost_estimate=SMALL,
        name="heads_back",
    )(d_attn_own, *t_out.halves)
    def attend_back(first, count, grads, *held):
        shift = lambda spec: pl.BlockSpec(
            spec.block_shape, lambda i, h: spec.index_map(i, h + first)
        )
        q_part, kv_part = shift(q_spec), shift(kv_spec)
        return pl.pallas_call(
            attend_back_kernel,
            grid=(rows, count),
            in_specs=[q_part, q_part, limit_spec, pos_spec]
            + [kv_part] * 2
            + [pl.BlockSpec(memory_space=pl.ANY)] * len(held),
            out_specs=[q_part] + [kv_part] * 2,
            out_shape=[jax.ShapeDtypeStruct(packed, f32)]
            + [jax.ShapeDtypeStruct((n // 2,) + packed_kv, bf16)] * 2,
            scratch_shapes=[
                pltpu.VMEM((SLOTS, LANES), bf16),
                pltpu.VMEM((LANES, SLOTS), bf16),
                pltpu.VMEM((SLOTS, LANES), f32),
            ],
            input_output_aliases={6 + i: i for i in range(len(held))},
            compiler_params=params(2),
            cost_estimate=SMALL,
            name="attend_back",
        )(queries, grads, limit, key_pos, *kv_halves, *held)

    held = attend_back(0, 3, d_heads)
    t_attn = TensorGather(d_attn_own)
    link.go(t_ffn, s_ff[3], s_ff[2], s_ff[0], s_ff[1], during=held)
    d_query, d_low, d_high = attend_back(3, HEADS_KV - 3, after(d_heads, *link.done), *held)

    def key_grads(begin, end, arrived, kind):
        if begin >= n // 2:
            return d_high
        return plus(d_low[begin:end].astype(f32), arrived, kind)

    s_keys = Scatter(key_grads)
    d_q_low, d_q_gain = pl.pallas_call(
        query_back_kernel,
        grid=(n_tensor,),
        in_specs=[part_spec, head_spec, whole(one_head), whole(one_head), whole((1, HEAD))],
        out_specs=(head_spec, whole((1, HEAD))),
        out_shape=(
            jax.ShapeDtypeStruct(heads_shape, bf16),
            jax.ShapeDtypeStruct((1, HEAD), f32),
        ),
        compiler_params=params(),
        cost_estimate=SMALL,
        name="query_back",
    )(d_query, q_raw, cos, sin, q_gain)

    def product(left, right):
        wide = right.shape[1]
        count = width // 256
        grid = width // 512
        halves = pl.pallas_call(
            product_kernel,
            grid=(grid,),
            in_specs=[pl.BlockSpec((rows_all // 2, 512), lambda j: (0, j))] * 2
            + [whole(right.shape)],
            out_specs=(
                pl.BlockSpec((2, wide, 256), lambda j: (jnp.minimum(j, grid // 2 - 1), 0, 0)),
                pl.BlockSpec((2, wide, 256), lambda j: (jnp.maximum(j - grid // 2, 0), 0, 0)),
            ),
            out_shape=[jax.ShapeDtypeStruct((count // 2, wide, 256), bf16)] * 2,
            scratch_shapes=[pltpu.VMEM((wide, rows_all), bf16)],
            compiler_params=params(),
            cost_estimate=SMALL,
            name="product",
        )(*left, right)
        return split_places(halves, wide)

    def sum_of(halves):
        def make(begin, end, arrived, kind):
            if begin >= n // 2:
                return halves[1]
            return plus(halves[0][begin:end].astype(f32), arrived, kind)

        return Scatter(make)

    t_query_back = TensorExchange(d_q_low)
    link.go(t_attn, s_ff[4], s_ff[3], s_ff[2], during=[d_q_low])
    add_grads(5)
    link.go(t_attn, t_query_back, s_keys, s_ff[4], t_ffn, during=[sent[5]])
    ffn_terms = t_ffn.terms()
    outputs = pl.pallas_call(
        functools.partial(finish_kernel, tuple(order)),
        grid=(1,),
        in_specs=[smem, square, whole((sp_rows, 1))] + [first_spec] * len(ffn_terms),
        out_specs=square,
        out_shape=low_square,
        compiler_params=params(),
        cost_estimate=SMALL,
        name="finish",
    )(index, mixed, live, *ffn_terms)
    d_attn = t_attn.rows()
    out_halves = product(d_attn, t_heads.rows())
    link.go(t_query_back, s_keys, s_ff[5], s_ff[3], s_ff[4], during=[*out_halves, outputs])
    s_out = sum_of(out_halves)
    s_query = sum_of(product(h_one_all, t_query_back.rows()))
    link.go(s_keys, s_out, s_ff[5], during=[s_query.value()])
    d_kv = s_keys.result()
    d_kv_low, d_k_gain = pl.pallas_call(
        key_back_kernel,
        out_shape=(
            jax.ShapeDtypeStruct((sp_rows, kv_cols), bf16),
            jax.ShapeDtypeStruct((1, HEAD), f32),
        ),
        compiler_params=pltpu.CompilerParams(vmem_limit_bytes=VMEM_LIMIT),
        cost_estimate=SMALL,
        name="key_value_back",
    )(d_kv, kv_raw, cos, sin, k_gain)
    kv_part = kv_cols // n_tensor
    t_kv_back = Direct(
        [
            lax.dynamic_slice_in_dim(d_kv_low, (tensor ^ s) * kv_part, kv_part, axis=1)
            for s in tensor_order
        ]
    )
    grad_rel, d_gain_one = pl.pallas_call(
        back_kernel,
        grid=(n_tensor,),
        in_specs=[
            head_spec,
            both_spec,
            whole((sp_rows, kv_cols)),
            whole((width, kv_cols)),
            square,
            whole((1, width)),
            square,
        ],
        out_specs=(square, whole((1, width))),
        out_shape=(
            jax.ShapeDtypeStruct((sp_rows, width), bf16),
            jax.ShapeDtypeStruct((1, width), f32),
        ),
        scratch_shapes=[pltpu.VMEM((sp_rows, width), f32)],
        compiler_params=params(),
        cost_estimate=SMALL,
        name="h_one_back",
    )(d_q_low, query_all, d_kv_low, kv_all, inputs, gain_one[None], d_mixed)
    def collect(first, last, *held):
        terms = [[lows[c], *s_ff[c].raw] for c in range(first, last)]
        flat = [x for group in terms for x in group]
        if not held:
            flat[0] = after(flat[0], *link.done)
        return pl.pallas_call(
            functools.partial(collect_kernel, len(terms), len(terms[0])),
            grid=(len(terms),),
            in_specs=[pl.BlockSpec((1,) + x.shape[1:], lambda i: (0, 0, 0)) for x in flat]
            + [pl.BlockSpec(memory_space=pl.ANY)] * len(held),
            out_specs=(
                pl.BlockSpec((cols, 2, unit), lambda i: (0, 0, first + i)),
                pl.BlockSpec((unit, cols), lambda i: (first + i, 0)),
            ),
            out_shape=(
                jax.ShapeDtypeStruct((cols, 2, ff), f32),
                jax.ShapeDtypeStruct((ff, cols), f32),
            ),
            input_output_aliases={len(flat) + i: i for i in range(len(held))},
            compiler_params=params(),
            cost_estimate=SMALL,
            name="collect",
        )(*flat, *held)

    early_sums = collect(0, FF_LAST)
    link.go(t_kv_back, s_out, s_query, during=[grad_rel, *early_sums])
    grad_inputs = call(
        functools.partial(leave_kernel, tuple(order)),
        low_square,
        "leave",
        index,
        grad_rel,
        specs=[smem, vmem],
    )

    gain_parts = jnp.concatenate([d_gain_one, d_gain_two]).reshape(2, n, cols).transpose(1, 0, 2)
    head_rows = max(2 * HEAD // cols, 1)
    head_parts = jnp.concatenate([d_q_gain, d_k_gain]).reshape(1, -1)
    head_parts = jnp.pad(head_parts, ((0, 0), (0, head_rows * cols - 2 * HEAD)))
    head_parts = jnp.broadcast_to(head_parts.reshape(1, head_rows, cols), (n, head_rows, cols))
    small_parts = jnp.concatenate([gain_parts, head_parts], axis=1)
    kv_halves_back = product(h_one_all, t_kv_back.rows())

    def with_small(side):
        begin = side * n // 2
        small_here = small_parts[begin : begin + n // 2].astype(bf16)
        return jnp.concatenate([kv_halves_back[side], small_here], axis=1)

    s_kv = ScatterSoon(with_small(0), with_small(1))
    link.go(s_kv, s_query, s_out, s_ff[5])
    sum_in, sum_down = collect(FF_LAST, len(sizes), *early_sums)
    link.go(s_kv, s_query, during=[sum_in, sum_down])
    t_sums = TensorAll(s_kv.result().astype(bf16))
    link.go(t_sums)
    stack = t_sums.stack
    small = jnp.sum(stack[:, kv_part:].astype(f32), axis=0)
    stack = stack[:, :kv_part]
    sum_gains = small[:2]
    sum_heads = small[2:].reshape(-1)[: 2 * HEAD].reshape(2, HEAD)
    inverse = jnp.array([tensor_order.index(i) for i in range(n_tensor)], jnp.int32)
    places = [
        lax.dynamic_index_in_dim(inverse, tensor ^ i, axis=0, keepdims=False)
        for i in range(n_tensor)
    ]
    sum_kv = jnp.concatenate(
        [
            lax.dynamic_index_in_dim(stack, places[i], axis=0, keepdims=False)
            for i in range(n_tensor)
        ],
        axis=0,
    ).T.astype(f32)
    sum_out = s_out.result()
    sum_query = s_query.result().T
    return (
        outputs,
        grad_inputs,
        sum_query,
        sum_kv.astype(f32),
        sum_out,
        sum_in,
        sum_down,
        sum_gains,
        sum_heads,
    )


def solution(mesh):
    in_specs = (
        P(("dp", "tensor"), None),
        P(("dp", "tensor"), None),
        P("dp", "tensor"),
        P("dp", None),
        P("tensor", "dp"),
        P("dp", None, "tensor"),
        P("tensor", "dp"),
        P(None, "dp"),
        P(),
        P(),
        P(),
    )
    out_specs = (
        P(("dp", "tensor"), None),
        P(("dp", "tensor"), None),
        P("dp", "tensor"),
        P("dp", None),
        P("tensor", "dp"),
        P("dp", None, "tensor"),
        P("tensor", "dp"),
        P(None, "dp"),
        P(),
    )
    return jax.shard_map(local, mesh=mesh, in_specs=in_specs, out_specs=out_specs, check_vma=False)
```

```python
import functools

import jax
import jax.numpy as jnp
from jax import lax
from jax.experimental import layout
from jax.experimental import pallas as pl
from jax.experimental.pallas import tpu as pltpu
from jax.sharding import PartitionSpec as P

HEADS_KV = 5
HEAD = 64
SLOTS = 2048
STRETCH = 64
LANES = 128
FF_PARTS = (1, 1, 1, 1, 1, 1)
FF_LAST = len(FF_PARTS) - 1
VMEM_LIMIT = 48 * 1024 * 1024
SMALL = pl.CostEstimate(flops=1000, bytes_accessed=1000, transcendentals=0)

eps_norm = 1e-06
rope_base = 10000.0
neg_large = -1e30
f32 = jnp.float32
bf16 = jnp.bfloat16
contract_rows = (((0,), (0,)), ((), ()))
contract_cols = (((1,), (1,)), ((), ()))


def dot(a, b, dims=(((1,), (0,)), ((), ()))):
    return lax.dot_general(a, b, dims, preferred_element_type=f32)


def after(value, *deps):
    return lax.optimization_barrier((value, *deps))[0]


def masks_of(axis):
    size = lax.axis_size(axis)
    bits = [1 << i for i in range(1, size.bit_length() - 1)]
    return bits + [1]


def order_of(axis):
    order = [0]
    for mask in masks_of(axis):
        order = order + [r ^ mask for r in order]
    return order


def swap(value, axis, mask):
    size = lax.axis_size(axis)
    return lax.ppermute(value, axis, [(i, i ^ mask) for i in range(size)])


def join(first, second):
    both = jnp.concatenate([first, second], axis=0)
    return layout.with_layout_constraint(both, layout.Layout(tuple(range(both.ndim))))


def gather(value, axis):
    stack = value[None]
    for mask in masks_of(axis):
        stack = join(stack, swap(stack, axis, mask))
    return stack


def gather_rows(value, axis):
    index = lax.axis_index(axis)
    stack = value
    size = lax.axis_size(axis)
    bit = size // 2
    at = value.ndim - 2
    while bit:
        other = swap(stack, axis, bit)
        upper = (index & bit) != 0
        stack = jnp.stack(
            [jnp.where(upper, other, stack), jnp.where(upper, stack, other)], axis=at
        )
        bit //= 2
        at += 1
    return stack.reshape(value.shape[:-2] + (size,) + value.shape[-2:])


def scatter(make, axis):
    half = lax.axis_size(axis)
    arrived = []
    for mask in reversed(masks_of(axis)):
        half //= 2
        sent = make(half, 2 * half, [x[half : 2 * half] for x in arrived], bf16)
        arrived = [x[:half] for x in arrived] + [swap(sent, axis, mask)]
    return make(0, 1, arrived, f32)[0]


def phases():
    masks = masks_of("dp")
    return [masks[:1], masks[1:-1], masks[-1:]]


class Item:
    late = ()

    def bring(self, value, axis, mask):
        got = swap(value, axis, mask)
        return after(got, *self.late) if self.late else got


class Gather(Item):
    def __init__(self, value):
        self.stack, self.halves, self.phase = value[None], None, 0

    def value(self):
        return self.stack

    def advance(self, value):
        for mask in phases()[self.phase]:
            got = self.bring(value, "dp", mask)
            self.halves = (value, got)
            value = join(value, got)
        self.stack = value
        self.phase += 1
        return got

    def pieces(self):
        half = order_of("dp")[: lax.axis_size("dp") // 2]
        return [(x, [r ^ m for r in half]) for x, m in zip(self.halves, (0, masks_of("dp")[-1]))]


class GatherSoon(Item):
    def __init__(self, value):
        self.stack, self.phase = value[None], 0

    def value(self):
        return self.stack

    def advance(self, value):
        order = order_of("dp")
        if self.phase:
            got = [self.bring(value, "dp", masks_of("dp")[-1])]
        else:
            got = [self.bring(value, "dp", r) for r in order[1 : len(order) // 2]]
        both = jnp.concatenate([value, *got], axis=0)
        self.stack = layout.with_layout_constraint(both, layout.Layout(tuple(range(both.ndim))))
        self.phase += 1
        return got


class ScatterSoon(Item):
    def __init__(self, low, high):
        self.low, self.high, self.phase = low, high, 0

    def value(self):
        if self.phase == 0:
            return self.high
        self.total = self.low.astype(f32) + self.first.astype(f32)
        return self.total[1:].astype(bf16)

    def advance(self, value):
        order = order_of("dp")
        self.phase += 1
        if self.phase == 1:
            self.first = self.bring(value, "dp", order[len(order) // 2])
            return self.first
        self.rest = [
            self.bring(value[p - 1], "dp", order[p]) for p in range(1, len(order) // 2)
        ]
        return self.rest

    def result(self):
        return self.total[0] + sum(x.astype(f32) for x in self.rest)


class TensorAll(Item):
    def __init__(self, value):
        self.own = value

    def value(self):
        return self.own

    def advance(self, value):
        got = [self.bring(value, "tensor", r) for r in order_of("tensor")[1:]]
        self.stack = jnp.stack([value, *got])
        return got


class GatherLate(Item):
    def __init__(self, value):
        self.parts, self.phase = [(value[None], [0])], 0

    def value(self):
        return self.parts[max(self.phase - 2, 0)][0]

    def advance(self, value):
        masks = masks_of("dp")
        masks = [masks[-1:], masks[:1], masks[1:-1], masks[1:-1]][self.phase]
        at = max(self.phase - 2, 0)
        places = self.parts[at][1]
        for mask in masks:
            got = self.bring(value, "dp", mask)
            halves = [(value, places), (got, [r ^ mask for r in places])]
            places = places + halves[1][1]
            if mask != masks[-1] or self.phase == 0:
                value = join(value, got)
        if self.phase == 0:
            self.parts = [(value, places)]
        elif self.phase == 1:
            self.parts = halves
        elif self.phase == 2:
            self.parts, self.first = [None, self.parts[1]], halves
        else:
            self.parts = self.first + halves
        self.phase += 1
        return got

    def pieces(self):
        return self.parts


class Scatter(Item):
    def __init__(self, make):
        self.make, self.half, self.arrived, self.phase = make, lax.axis_size("dp"), [], 2
        self.raw = []

    def value(self):
        half = self.half // 2
        return self.make(half, 2 * half, [x[half : 2 * half] for x in self.arrived], bf16)

    def advance(self, value):
        for k, mask in enumerate(reversed(phases()[self.phase])):
            if k:
                value = self.value()
            self.half //= 2
            got = self.bring(value, "dp", mask)
            self.arrived = [x[: self.half] for x in self.arrived] + [got]
            self.raw.append(got)
        self.phase -= 1
        return got

    def result(self):
        return self.make(0, 1, self.arrived, f32)[0]


class TensorGather(Item):
    def __init__(self, value):
        self.stack, self.masks = value[None], masks_of("tensor")

    def value(self):
        return self.stack

    def advance(self, value):
        got = self.bring(value, "tensor", self.masks[0])
        self.halves = (value, got)
        self.stack, self.masks = join(value, got), self.masks[1:]
        return got

    def rows(self):
        return [x.reshape(-1, x.shape[-1]) for x in self.halves]


class PairRows(Item):
    def __init__(self, value):
        self.stack = value

    def value(self):
        return self.stack

    def advance(self, value):
        got = self.bring(value, "tensor", 1)
        upper = (lax.axis_index("tensor") & 1) != 0
        self.stack = jnp.stack(
            [jnp.where(upper, got, value), jnp.where(upper, value, got)], axis=value.ndim - 2
        )
        return got


class TensorScatter(Item):
    def __init__(self, sums):
        self.sums, self.masks, self.arrived = sums, masks_of("tensor")[::-1], []

    def value(self):
        half = 1 << (len(self.masks) - 1)
        if half == self.sums[1].shape[0]:
            return self.sums[1]
        return plus(
            self.sums[0][half : 2 * half].astype(f32),
            [x[half : 2 * half] for x in self.arrived],
            bf16,
        )

    def advance(self, value):
        self.arrived.append(self.bring(value, "tensor", self.masks[0]))
        self.masks = self.masks[1:]
        return self.arrived[-1]

    def terms(self):
        return [self.sums[0], *self.arrived]


class TensorDirect(Item):
    def __init__(self, parts):
        self.parts = list(parts)

    def value(self):
        return self.parts

    def advance(self, value):
        order = order_of("tensor")
        self.got = [self.bring(value[p], "tensor", order[p]) for p in range(1, len(order))]
        return self.got

    def terms(self):
        return [x[None] for x in [self.parts[0], *self.got]]


class TensorExchange(Item):
    def __init__(self, stack):
        self.stack, self.masks = stack[:, None], masks_of("tensor")

    def value(self):
        return self.stack[1::2]

    def advance(self, value):
        got = self.bring(value, "tensor", self.masks[0])
        self.stack = jnp.concatenate([self.stack[0::2], got], axis=1)
        self.masks = self.masks[1:]
        return got

    def rows(self):
        return self.stack.reshape((-1,) + self.stack.shape[3:])


class Direct(Item):
    def __init__(self, parts):
        self.parts = parts

    def value(self):
        return jnp.stack(self.parts)

    def advance(self, value):
        order = order_of("tensor")
        got = [value[0]] + [
            self.bring(value[p], "tensor", order[p]) for p in range(1, len(order))
        ]
        self.all = jnp.concatenate(got, axis=0)
        return self.all

    def rows(self):
        return self.all


class Rounds:
    def __init__(self):
        self.done = []

    def go(self, *items, ends=(), during=()):
        done = list(ends)
        for item in items:
            value = item.value()
            if self.done:
                value = after(value, *self.done)
            item.late = during
            got = item.advance(value)
            done += got if isinstance(got, list) else [got]
        self.done = done


def plus(total, arrived, kind):
    for other in arrived:
        total = total + other.astype(f32)
    return total.astype(kind)


def scaled_norm(value_in, gain_vec):
    return (
        value_in
        * lax.rsqrt(jnp.mean(value_in * value_in, axis=-1, keepdims=True) + eps_norm)
        * gain_vec
    )


def silu_product(gate, up_part):
    return gate * jax.nn.sigmoid(gate) * up_part


def params(steps=1):
    return pltpu.CompilerParams(
        dimension_semantics=("arbitrary",) * steps, vmem_limit_bytes=VMEM_LIMIT
    )


def swap_halves(value):
    half = HEAD // 2
    return jnp.concatenate([value[:, half:], value[:, :half]], axis=1)


def rope_one(raw, gain, cos, sin, factor):
    scale = lax.rsqrt(jnp.mean(raw * raw, axis=-1, keepdims=True) + eps_norm)
    normed = raw * scale * gain
    return (normed * cos + swap_halves(normed) * sin) * factor


def rope_back(raw, gain, cos, sin, factor, grad):
    grad = grad * factor
    grad = grad * cos - swap_halves(grad) * sin
    scale = lax.rsqrt(jnp.mean(raw * raw, axis=-1, keepdims=True) + eps_norm)
    weighted = grad * gain
    back = scale * weighted - raw * (
        scale * scale * scale * jnp.mean(raw * weighted, axis=-1, keepdims=True)
    )
    return back, jnp.sum(grad * raw * scale, axis=0, keepdims=True)


def query_kernel(h_ref, w_ref, cos_ref, sin_ref, gain_ref, raw_ref, out_ref):
    cols = w_ref.shape[3]
    raw = sum(
        dot(h_ref[:, r * cols : (r + 1) * cols], w_ref[0, r], contract_cols)
        for r in range(w_ref.shape[1])
    )
    raw_ref[0] = raw
    rows, blocks = out_ref.shape[0], out_ref.shape[2]
    for h in range(HEADS_KV):
        turned = rope_one(
            raw[:, h * HEAD : (h + 1) * HEAD], gain_ref[...], cos_ref[...], sin_ref[...], 0.125
        )
        wide = jnp.concatenate([turned, jnp.zeros_like(turned)], axis=1).astype(bf16)
        out_ref[:, h, :, 0] = wide.reshape(rows, blocks, STRETCH, LANES)


def key_kernel(h_ref, w_ref, cos_ref, sin_ref, gain_ref, raw_ref, out_ref):
    raw = dot(h_ref[...], w_ref[...])
    raw_ref[...] = raw
    rows, blocks = out_ref.shape[0], out_ref.shape[2]
    for h in range(HEADS_KV):
        turned = rope_one(
            raw[:, h * HEAD : (h + 1) * HEAD], gain_ref[...], cos_ref[...], sin_ref[...], 1.0
        )
        start = (HEADS_KV + h) * HEAD
        wide = jnp.concatenate([turned, raw[:, start : start + HEAD]], axis=1).astype(bf16)
        out_ref[:, h] = wide.reshape(rows, blocks, STRETCH, LANES)


def load_keys(halves, kv, kvt):
    places = [(half, i) for half in halves for i in range(half.shape[0])]
    group = len(places) * STRETCH
    for g in range(halves[0].shape[3]):
        for r, (half, i) in enumerate(places):
            start = g * group + r * STRETCH
            kv[start : start + STRETCH, :] = half[i, 0, 0, g]
    kvt[...] = kv[...].T
    return group


def attend_kernel(q_ref, limit_ref, keypos_ref, low_ref, high_ref, out_ref, kv, kvt):
    blocks = q_ref.shape[2]
    group = load_keys((low_ref, high_ref), kv, kvt)
    for b in range(blocks):
        span = (b + 1) * group
        q = q_ref[0, 0, b].reshape(-1, LANES)
        scores = dot(kv[:span], q, contract_cols)
        scores = jnp.where(keypos_ref[0, :span] <= limit_ref[0, b], scores, neg_large)
        top = jnp.max(scores, axis=0, keepdims=True)
        weights = jnp.exp(scores - top)
        total = jnp.sum(weights, axis=0, keepdims=True)
        heads = dot(kvt[:, :span], weights.astype(bf16)) / total
        out_ref[0, 0, b] = heads.T.astype(bf16).reshape(q_ref.shape[3:])


def attend_back_kernel(q_ref, g_ref, limit_ref, keypos_ref, low_ref, high_ref, *rest):
    dq_ref, dlow_ref, dhigh_ref, kv, kvt, acc = rest[-6:]
    blocks = q_ref.shape[2]
    group = load_keys((low_ref, high_ref), kv, kvt)
    acc[...] = jnp.zeros_like(acc)
    for b in range(blocks):
        span = (b + 1) * group
        q = q_ref[0, 0, b].reshape(-1, LANES)
        grad = g_ref[0, 0, b].reshape(-1, LANES)
        scores = dot(kv[:span], q, contract_cols)
        scores = jnp.where(keypos_ref[0, :span] <= limit_ref[0, b], scores, neg_large)
        top = jnp.max(scores, axis=0, keepdims=True)
        weights = jnp.exp(scores - top)
        probs = weights * (1.0 / jnp.sum(weights, axis=0, keepdims=True))
        d_probs = dot(kv[:span], grad, contract_cols)
        delta = jnp.sum(probs * d_probs, axis=0, keepdims=True)
        d_scores = (probs * (d_probs - delta)).astype(bf16)
        dq = dot(kvt[:, :span], d_scores)
        dq_ref[0, 0, b] = dq.T.reshape(q_ref.shape[3:])
        acc[:span] += dot(d_scores, q) + dot(probs.astype(bf16), grad)
    count = dlow_ref.shape[0]
    for out, first in ((dlow_ref, 0), (dhigh_ref, count)):
        for r in range(count):
            for g in range(blocks):
                start = g * group + (first + r) * STRETCH
                out[r, 0, 0, g] = acc[start : start + STRETCH].astype(bf16)


def out_kernel(o_ref, w_low, w_high, x_ref, live_ref, gain_ref, mixed_ref, h_ref, heads_ref):
    rows = heads_ref.shape[1]
    heads = jnp.concatenate(
        [o_ref[:, h, :, 0].reshape(rows, LANES)[:, HEAD:] for h in range(HEADS_KV)], axis=1
    )
    heads_ref[0] = heads
    cols = w_low.shape[3]
    low = pl.program_id(0) < pl.num_programs(0) // 2

    @pl.when(pl.program_id(0) == 0)
    def _():
        mixed_ref[...] = jnp.zeros_like(mixed_ref)

    for r in range(w_low.shape[1]):
        here = jnp.where(low, w_low[0, r], w_high[0, r])
        mixed_ref[:, r * cols : (r + 1) * cols] += dot(heads, here)

    @pl.when(pl.program_id(0) == pl.num_programs(0) - 1)
    def _():
        mixed = x_ref[...].astype(f32) + live_ref[...] * mixed_ref[...]
        mixed_ref[...] = mixed
        h_ref[...] = scaled_norm(mixed, gain_ref[...]).astype(bf16)


def norm_back(value, gain, grad):
    scale = lax.rsqrt(jnp.mean(value * value, axis=-1, keepdims=True) + eps_norm)
    weighted = grad * gain
    inner = jnp.mean(value * weighted, axis=-1, keepdims=True)
    back = scale * weighted - value * (scale * scale * scale * inner)
    return back, jnp.sum(grad * value * scale, axis=0, keepdims=True)


def mixed_back_kernel(mixed_ref, cot_ref, gain_ref, live_ref, *rest):
    terms, (d_mixed_ref, d_attn_ref, dgain_ref) = rest[:-3], rest[-3:]
    grad = sum(ref[0].astype(f32) for ref in terms)
    back, dgain_ref[...] = norm_back(mixed_ref[...], gain_ref[...], grad)
    d_mixed = cot_ref[...].astype(f32) + back
    d_mixed_ref[...] = d_mixed
    d_attn_ref[...] = (live_ref[...] * d_mixed).astype(bf16)


def heads_back_kernel(d_ref, w_low, w_high, out_ref):
    cols = w_low.shape[3]
    low = pl.program_id(0) < pl.num_programs(0) // 2
    grad = sum(
        dot(
            d_ref[:, r * cols : (r + 1) * cols],
            jnp.where(low, w_low[0, r], w_high[0, r]),
            contract_cols,
        )
        for r in range(w_low.shape[1])
    )
    rows, blocks = out_ref.shape[0], out_ref.shape[2]
    for h in range(HEADS_KV):
        part = grad[:, h * HEAD : (h + 1) * HEAD]
        wide = jnp.concatenate([jnp.zeros_like(part), part], axis=1).astype(bf16)
        out_ref[:, h, :, 0] = wide.reshape(rows, blocks, STRETCH, LANES)


def query_back_kernel(dq_ref, raw_ref, cos_ref, sin_ref, gain_ref, out_ref, dgain_ref):
    @pl.when(pl.program_id(0) == 0)
    def _():
        dgain_ref[...] = jnp.zeros_like(dgain_ref)

    raw = raw_ref[0]
    parts = []
    for h in range(HEADS_KV):
        grad = dq_ref[:, h, :, 0].reshape(raw.shape[0], LANES)[:, :HEAD]
        back, dgain = rope_back(
            raw[:, h * HEAD : (h + 1) * HEAD],
            gain_ref[...],
            cos_ref[...],
            sin_ref[...],
            0.125,
            grad,
        )
        parts.append(back)
        dgain_ref[...] += dgain
    out_ref[0] = jnp.concatenate(parts, axis=1).astype(bf16)


def key_back_kernel(sum_ref, raw_ref, cos_ref, sin_ref, gain_ref, out_ref, dgain_ref):
    raw = raw_ref[...]
    keys, values = [], []
    total = jnp.zeros_like(dgain_ref)
    for h in range(HEADS_KV):
        both = sum_ref[:, h].reshape(raw.shape[0], LANES)
        back, dgain = rope_back(
            raw[:, h * HEAD : (h + 1) * HEAD],
            gain_ref[...],
            cos_ref[...],
            sin_ref[...],
            1.0,
            both[:, :HEAD],
        )
        keys.append(back)
        values.append(both[:, HEAD:])
        total = total + dgain
    dgain_ref[...] = total
    out_ref[...] = jnp.concatenate(keys + values, axis=1).astype(bf16)


def back_kernel(
    dq_ref, wq_ref, dkv_ref, wkv_ref, x_ref, gain_ref, d_mixed_ref, out_ref, dgain_ref, acc
):
    @pl.when(pl.program_id(0) == 0)
    def _():
        acc[...] = dot(dkv_ref[...], wkv_ref[...], contract_cols)

    cols = wq_ref.shape[3]
    for r in range(wq_ref.shape[1]):
        acc[:, r * cols : (r + 1) * cols] += dot(dq_ref[0], wq_ref[0, r])

    @pl.when(pl.program_id(0) == pl.num_programs(0) - 1)
    def _():
        back, dgain_ref[...] = norm_back(x_ref[...].astype(f32), gain_ref[...], acc[...])
        out_ref[...] = (d_mixed_ref[...] + back).astype(bf16)


def turn_kernel(x_ref, out_ref):
    out_ref[...] = x_ref[...].T


def shards_kernel(in_ref, down_ref, *parts):
    ff = down_ref.shape[0]
    start = 0
    for ref in parts:
        part = ref.shape[1] // 3
        ref[:, :part] = in_ref[:, start : start + part]
        ref[:, part : 2 * part] = in_ref[:, ff + start : ff + start + part]
        ref[:, 2 * part :] = down_ref[start : start + part, :].T
        start += part


def turn_columns(order, back, index, value):
    size = len(order)
    cols = value.shape[1] // size

    def pick(value, places):
        return jnp.concatenate([value[:, p * cols : (p + 1) * cols] for p in places], axis=1)

    if back:
        value = pick(value, [order.index(i) for i in range(size)])
    bit = 1
    while bit < size:
        value = jnp.where((index & bit) != 0, pick(value, [i ^ bit for i in range(size)]), value)
        bit *= 2
    return value if back else pick(value, order)


def enter_kernel(order, index_ref, x_ref, cot_ref, live_ref, x_out, cot_out, d_ffn_out):
    x_out[...] = turn_columns(order, False, index_ref[0], x_ref[...].astype(f32)).astype(bf16)
    cot = turn_columns(order, False, index_ref[0], cot_ref[...].astype(f32))
    cot_out[...] = cot.astype(bf16)
    d_ffn_out[...] = (cot * live_ref[...]).astype(bf16)


def leave_kernel(order, index_ref, x_ref, out_ref):
    value = x_ref[...].astype(f32)
    out_ref[...] = turn_columns(order, True, index_ref[0], value).astype(bf16)


def finish_kernel(order, index_ref, mixed_ref, live_ref, *rest):
    terms, out_ref = rest[:-1], rest[-1]
    ffn = sum(ref[0].astype(f32) for ref in terms)
    value = mixed_ref[...] + live_ref[...] * ffn
    out_ref[...] = turn_columns(order, True, index_ref[0], value).astype(bf16)


def product_kernel(left_low, left_high, right_ref, low_ref, high_ref, turned):
    @pl.when(pl.program_id(0) == 0)
    def _():
        turned[...] = right_ref[...].T

    out = halves_product(turned[...], left_low, left_high).astype(bf16)
    low = pl.program_id(0) < pl.num_programs(0) // 2
    span = low_ref.shape[2]
    for out_ref, here in ((low_ref, low), (high_ref, jnp.logical_not(low))):

        @pl.when(here)
        def _(out_ref=out_ref):
            for p in range(out_ref.shape[0]):
                out_ref[p] = out[:, p * span : (p + 1) * span]


def pick_columns(value, places, cols):
    if places == list(range(places[0], places[0] + len(places))):
        return value[:, places[0] * cols : (places[-1] + 1) * cols]
    return jnp.concatenate([value[:, p * cols : (p + 1) * cols] for p in places], axis=1)


def hidden_kernel(all_places, h_low, h_high, d_low, d_high, *refs):
    pieces, (hidden_ref, d_gate_up_ref, turned_ref) = refs[:-3], refs[-3:]
    part = hidden_ref.shape[1]
    low = pl.program_id(0) < pl.num_programs(0) // 2
    h = jnp.where(low, h_low[...], h_high[...])
    d = jnp.where(low, d_low[...], d_high[...])
    gate_up = d_hidden = None
    for places, ref in zip(all_places, pieces):
        cols = ref.shape[0] // len(places)
        first = dot(pick_columns(h, places, cols), ref[:, : 2 * part])
        second = dot(pick_columns(d, places, cols), ref[:, 2 * part :])
        gate_up = first if gate_up is None else gate_up + first
        d_hidden = second if d_hidden is None else d_hidden + second
    gate, up = gate_up[:, :part], gate_up[:, part:]
    sig = jax.nn.sigmoid(gate)
    swish = gate * sig
    hidden = (swish * up).astype(bf16)
    d_gate = (d_hidden * up * (sig + swish * (1.0 - sig))).astype(bf16)
    d_up = (d_hidden * swish).astype(bf16)
    hidden_ref[...] = hidden
    d_gate_up_ref[:, :part] = d_gate
    d_gate_up_ref[:, part:] = d_up
    turned_ref[:part] = d_gate.T
    turned_ref[part : 2 * part] = d_up.T
    turned_ref[2 * part :] = hidden.T


def halves_product(left, low_ref, high_ref):
    middle = low_ref.shape[0]
    return dot(left[:, :middle], low_ref[...]) + dot(left[:, middle:], high_ref[...])


def grads_kernel(h_low, h_high, d_low, d_high, turned_ref, low_ref, high_ref):
    split = turned_ref.shape[0] // 3 * 2
    first = halves_product(turned_ref[:split], h_low, h_high).astype(bf16)
    second = halves_product(turned_ref[split:], d_low, d_high).astype(bf16)
    low = pl.program_id(0) < pl.num_programs(0) // 2
    span = low_ref.shape[2]
    for out_ref, here in ((low_ref, low), (high_ref, jnp.logical_not(low))):

        @pl.when(here)
        def _(out_ref=out_ref):
            for p in range(out_ref.shape[0]):
                out_ref[p, :split] = first[:, p * span : (p + 1) * span]
                out_ref[p, split:] = second[:, p * span : (p + 1) * span]


def collect_kernel(count, each, *refs):
    in_ref, down_ref = refs[-2:]
    part = down_ref.shape[0]
    for c in range(count):

        @pl.when(pl.program_id(0) == c)
        def _(c=c):
            total = sum(ref[0].astype(f32) for ref in refs[c * each : (c + 1) * each])
            in_ref[:, 0, :] = total[:part].T
            in_ref[:, 1, :] = total[part : 2 * part].T
            down_ref[...] = total[2 * part :]


def back_sum_kernel(all_places, *refs):
    count = len(all_places)
    half = refs[-1].shape[1] // 2
    totals = [None, None]
    at = count
    for c, pieces in enumerate(all_places):
        terms = [dot(refs[c][...], refs[at + i][...], contract_cols) for i in range(len(pieces))]
        at += len(pieces)
        if len(pieces) > 2:
            blocks = {}
            for places, term in zip(pieces, terms):
                cols = term.shape[1] // len(places)
                for i, p in enumerate(places):
                    blocks[p] = term[:, i * cols : (i + 1) * cols]
            middle = len(blocks) // 2
            terms = [
                jnp.concatenate([blocks[side * middle + i] for i in range(middle)], axis=1)
                for side in range(2)
            ]
        totals = [t if old is None else old + t for old, t in zip(totals, terms)]
    outs = refs[at:]
    span = outs[0].shape[0]
    rows = totals[0].shape[0]
    each = max(rows // span, 1)
    for step in range(len(outs) // each):

        @pl.when(pl.program_id(0) == step)
        def _(step=step):
            for i in range(each):
                for side in range(2):
                    block = totals[side][i * span : (i + 1) * span].astype(bf16)
                    outs[step * each + i][:, side * half : (side + 1) * half] = block


def whole(shape):
    return pl.BlockSpec(shape, lambda *_: (0,) * len(shape))


def local(
    inputs,
    cotangent,
    w_query,
    w_kv,
    w_out,
    w_in,
    w_down,
    norm_gains,
    head_gains,
    lengths,
    slot_blocks,
):
    sp_rows, width = inputs.shape
    n = lax.axis_size("dp")
    n_tensor = lax.axis_size("tensor")
    dp = lax.axis_index("dp")
    tensor = lax.axis_index("tensor")
    seq_count = lengths.shape[0]
    row_span = sp_rows * n_tensor // seq_count
    blocks = row_span // STRETCH
    rows = sp_rows // row_span
    per_row = SLOTS // STRETCH
    cols = width // n
    q_cols = w_query.shape[1]
    kv_cols = w_kv.shape[1]
    ff = w_down.shape[0]
    order = order_of("dp")
    tensor_order = order_of("tensor")
    rels = jnp.array(order, jnp.int32)

    smem = pl.BlockSpec(memory_space=pltpu.SMEM)

    def call(kernel, out_shape, name, *args, specs=None):
        return pl.pallas_call(
            kernel,
            in_specs=specs,
            out_shape=out_shape,
            compiler_params=pltpu.CompilerParams(vmem_limit_bytes=VMEM_LIMIT),
            cost_estimate=SMALL,
            name=name,
        )(*args)

    table = slot_blocks.reshape(n, n_tensor, rows, blocks)
    mine = lax.dynamic_index_in_dim(table, tensor, axis=1, keepdims=False)[dp ^ rels]
    inside = jnp.arange(STRETCH, dtype=jnp.int32)
    key_pos = (mine % per_row * STRETCH)[..., None] + inside
    own_pos = key_pos[0]
    own_len = lengths[mine[0] // per_row][..., None]
    live = (own_pos < own_len).astype(f32).reshape(sp_rows, 1)
    limit = jnp.minimum(own_pos, own_len - 1)
    limit = jnp.broadcast_to(limit[:, :, None, None, :], (rows, blocks, 1, n_tensor, STRETCH))
    limit = limit.reshape(rows, blocks, 1, n_tensor * STRETCH)
    key_pos = key_pos.transpose(1, 2, 0, 3).reshape(rows, SLOTS, 1)
    half = HEAD // 2
    frequency = rope_base ** (-2.0 * jnp.arange(half, dtype=f32) / HEAD)
    angles = own_pos.reshape(sp_rows, 1).astype(f32) * frequency
    cosine, sine = jnp.cos(angles), jnp.sin(angles)
    cos = jnp.concatenate([cosine, cosine], axis=1)
    sin = jnp.concatenate([-sine, sine], axis=1)
    head_float = head_gains.astype(f32)
    q_gain, k_gain = head_float[0:1], head_float[1:2]

    vmem = pl.BlockSpec(memory_space=pltpu.VMEM)
    index = dp.reshape(1)
    low_square = jax.ShapeDtypeStruct((sp_rows, width), bf16)
    inputs, cotangent, d_ffn_own = call(
        functools.partial(enter_kernel, tuple(order)),
        [low_square] * 3,
        "enter",
        index,
        inputs,
        cotangent,
        live,
        specs=[smem, vmem, vmem, vmem],
    )
    inputs_f = inputs.astype(f32)
    part = w_kv.shape[0] // 2
    kv_shard = lax.dynamic_slice_in_dim(w_kv, (tensor & 1) * part, part, axis=0)
    unit = ff // sum(FF_PARTS)
    sizes = [size * unit for size in FF_PARTS]
    query_shard = call(
        turn_kernel, jax.ShapeDtypeStruct((q_cols, cols), bf16), "turn", w_query, specs=[vmem]
    )
    shards = call(
        shards_kernel,
        [jax.ShapeDtypeStruct((cols, 3 * part), bf16) for part in sizes],
        "shards",
        w_in.reshape(cols, 2 * ff),
        w_down,
        specs=[vmem, vmem],
    )
    link = Rounds()
    g_kv, g_gains = GatherSoon(kv_shard), Gather(norm_gains)
    g_query, g_out = Gather(query_shard), Gather(w_out)
    g_ff = [Gather(x) for x in shards[:-1]] + [GatherLate(shards[-1])]
    link.go(g_kv, g_gains, g_query, during=[d_ffn_own, cos, sin, limit, *shards])
    link.go(g_kv, g_gains, g_query, g_out)
    t_kv = PairRows(g_kv.stack)
    link.go(t_kv, g_gains, g_query, g_out, g_ff[0])
    gains = g_gains.stack.transpose(1, 0, 2).reshape(2, width).astype(f32)
    gain_one, gain_two = gains[0], gains[1]
    h_one = scaled_norm(inputs_f, gain_one).astype(bf16)
    t_query = TensorGather(g_query.stack)
    kv_all = t_kv.stack.reshape(width, kv_cols)
    t_d_ffn = TensorGather(d_ffn_own)

    packed = (rows, HEADS_KV, blocks, n_tensor, STRETCH, LANES)
    packed_kv = (rows, HEADS_KV, blocks, STRETCH, LANES)
    both_spec = pl.BlockSpec((1, n, q_cols, cols), lambda s: (s, 0, 0, 0))
    half_specs = [
        pl.BlockSpec(
            (1, n, q_cols, cols), lambda s: (jnp.minimum(s, n_tensor // 2 - 1), 0, 0, 0)
        ),
        pl.BlockSpec(
            (1, n, q_cols, cols), lambda s: (jnp.maximum(s - n_tensor // 2, 0), 0, 0, 0)
        ),
    ]
    kv_raw, kv_own = pl.pallas_call(
        key_kernel,
        out_shape=(
            jax.ShapeDtypeStruct((sp_rows, kv_cols), f32),
            jax.ShapeDtypeStruct(packed_kv, bf16),
        ),
        compiler_params=pltpu.CompilerParams(vmem_limit_bytes=VMEM_LIMIT),
        cost_estimate=SMALL,
        name="key_value",
    )(h_one, kv_all, cos, sin, k_gain)
    g_keys = Gather(kv_own)
    link.go(t_query, g_out, g_ff[5], g_ff[0], g_keys)
    t_out = TensorGather(g_out.stack)
    link.go(t_query, t_out, g_keys, g_ff[0], g_ff[1])
    query_all = t_query.stack
    one_head = (sp_rows, HEAD)
    part_spec = pl.BlockSpec(
        (rows, HEADS_KV, blocks, 1, STRETCH, LANES), lambda s: (0, 0, 0, s, 0, 0)
    )
    q_raw, queries = pl.pallas_call(
        query_kernel,
        grid=(n_tensor,),
        in_specs=[
            whole((sp_rows, width)),
            both_spec,
            whole(one_head),
            whole(one_head),
            whole((1, HEAD)),
        ],
        out_specs=(pl.BlockSpec((1, sp_rows, q_cols), lambda s: (s, 0, 0)), part_spec),
        out_shape=(
            jax.ShapeDtypeStruct((n_tensor, sp_rows, q_cols), f32),
            jax.ShapeDtypeStruct(packed, bf16),
        ),
        compiler_params=params(),
        cost_estimate=SMALL,
        name="query",
    )(h_one, query_all, cos, sin, q_gain)
    link.go(t_out, t_d_ffn, g_keys, g_ff[1], g_ff[2], during=[queries, key_pos])
    kv_halves = g_keys.halves
    q_spec = pl.BlockSpec(
        (1, 1, blocks, n_tensor, STRETCH, LANES), lambda i, h: (i, h, 0, 0, 0, 0)
    )
    kv_spec = pl.BlockSpec(
        (n // 2, 1, 1, blocks, STRETCH, LANES), lambda i, h: (0, i, h, 0, 0, 0)
    )
    limit_spec = pl.BlockSpec(
        (1, blocks, 1, n_tensor * STRETCH), lambda i, h: (i, 0, 0, 0)
    )
    pos_spec = pl.BlockSpec((1, SLOTS, 1), lambda i, h: (i, 0, 0))
    heads_packed = pl.pallas_call(
        attend_kernel,
        grid=(rows, HEADS_KV),
        in_specs=[q_spec, limit_spec, pos_spec] + [kv_spec] * 2,
        out_specs=q_spec,
        out_shape=jax.ShapeDtypeStruct(packed, bf16),
        scratch_shapes=[pltpu.VMEM((SLOTS, LANES), bf16), pltpu.VMEM((LANES, SLOTS), bf16)],
        compiler_params=params(2),
        cost_estimate=SMALL,
        name="attend",
    )(queries, limit, key_pos, *kv_halves)

    heads_shape = (n_tensor, sp_rows, q_cols)
    head_spec = pl.BlockSpec((1, sp_rows, q_cols), lambda s: (s, 0, 0))
    square = whole((sp_rows, width))
    mixed, h_two_own, attn_heads = pl.pallas_call(
        out_kernel,
        grid=(n_tensor,),
        in_specs=[
            part_spec,
            *half_specs,
            square,
            whole((sp_rows, 1)),
            whole((1, width)),
        ],
        out_specs=(square, square, head_spec),
        out_shape=(
            jax.ShapeDtypeStruct((sp_rows, width), f32),
            jax.ShapeDtypeStruct((sp_rows, width), bf16),
            jax.ShapeDtypeStruct(heads_shape, bf16),
        ),
        compiler_params=params(),
        cost_estimate=SMALL,
        name="out",
    )(heads_packed, *t_out.halves, inputs, live, gain_two[None])
    t_heads = TensorExchange(attn_heads)

    t_h_two = TensorGather(h_two_own)
    t_h_one = TensorGather(h_one)
    rows_all = sp_rows * n_tensor
    link.go(t_d_ffn, g_ff[1], g_ff[2], g_ff[3], during=[h_two_own])
    d_ffn = t_d_ffn.rows()
    link.go(t_h_two, g_ff[2], g_ff[3], g_ff[4])
    link.go(t_h_two, t_h_one, g_ff[3], g_ff[4], g_ff[5])
    h_two = t_h_two.rows()
    steps = n_tensor // 2
    row_block = lambda span: pl.BlockSpec((rows_all // steps, span), lambda i: (i, 0))
    low_rows = pl.BlockSpec((sp_rows, width), lambda i: (jnp.minimum(i, n_tensor // 2 - 1), 0))
    high_rows = pl.BlockSpec((sp_rows, width), lambda i: (jnp.maximum(i - n_tensor // 2, 0), 0))
    weights, hiddens, d_gate_ups, turned = [], [], [], []

    def hidden_part(g, part):
        pieces = [
            (x.reshape(len(rs) * cols, 3 * part), [order.index(r) for r in rs])
            for x, rs in g.pieces()
        ]
        weights.append(pieces)
        hidden, d_gate_up, flipped = pl.pallas_call(
            functools.partial(hidden_kernel, [places for _, places in pieces]),
            grid=(n_tensor,),
            in_specs=[low_rows, high_rows] * 2 + [whole(x.shape) for x, _ in pieces],
            out_specs=(
                pl.BlockSpec((sp_rows, part), lambda i: (i, 0)),
                pl.BlockSpec((sp_rows, 2 * part), lambda i: (i, 0)),
                pl.BlockSpec((3 * part, sp_rows), lambda i: (0, i)),
            ),
            out_shape=(
                jax.ShapeDtypeStruct((rows_all, part), bf16),
                jax.ShapeDtypeStruct((rows_all, 2 * part), bf16),
                jax.ShapeDtypeStruct((3 * part, rows_all), bf16),
            ),
            compiler_params=params(),
            cost_estimate=SMALL,
        name="hidden",
        )(*h_two, *d_ffn, *[x for x, _ in pieces])
        hiddens.append(hidden)
        d_gate_ups.append(d_gate_up)
        turned.append(flipped)

    def split_places(halves, wide):
        if cols == 256:
            return halves
        return [
            x.reshape(-1, wide, 256 // cols, cols).transpose(0, 2, 1, 3).reshape(n // 2, wide, cols)
            for x in halves
        ]

    def grads_of(flipped):
        wide = flipped.shape[0]
        count = width // 256
        grid = width // 512
        low_spec = pl.BlockSpec((2, wide, 256), lambda j: (jnp.minimum(j, grid // 2 - 1), 0, 0))
        high_spec = pl.BlockSpec((2, wide, 256), lambda j: (jnp.maximum(j - grid // 2, 0), 0, 0))
        block = pl.BlockSpec((rows_all // 2, 512), lambda j: (0, j))
        halves = pl.pallas_call(
            grads_kernel,
            grid=(grid,),
            in_specs=[block] * 4 + [whole(flipped.shape)],
            out_specs=(low_spec, high_spec),
            out_shape=[jax.ShapeDtypeStruct((count // 2, wide, 256), bf16)] * 2,
            compiler_params=params(),
            cost_estimate=SMALL,
            name="weight_grads",
        )(*h_two, *d_ffn, flipped)
        halves = split_places(halves, wide)

        def make(begin, end, arrived, kind):
            if begin >= n // 2:
                return halves[1]
            return plus(halves[0][begin:end].astype(f32), arrived, kind)

        lows.append(halves[0])
        return Scatter(make), halves[1]

    s_ff, sent, lows = [], [], []

    def add_grads(c):
        item, first = grads_of(after(turned[c], *link.done) if c > 2 else turned[c])
        s_ff.append(item)
        sent.append(first)

    def back_sum(parts, down, pieces):
        span = rows_all // pieces
        def weight_spec(x, w):
            span = x.shape[1]
            at = (w.shape[1] - span) // span if down else 0
            return pl.BlockSpec(
                (w.shape[0], span), lambda i: (0, at), pipeline_mode=pl.Buffered(1)
            )

        return pl.pallas_call(
            functools.partial(
                back_sum_kernel, [[places for _, places in pieces] for pieces in weights]
            ),
            grid=(steps,),
            in_specs=[row_block(x.shape[1]) for x in parts]
            + [weight_spec(x, w) for x, pieces in zip(parts, weights) for w, _ in pieces],
            out_specs=[whole((span, width))] * pieces,
            out_shape=[jax.ShapeDtypeStruct((span, width), bf16)] * pieces,
            compiler_params=params(),
            cost_estimate=SMALL,
            name="back_sum",
        )(*parts, *[w for pieces in weights for w, _ in pieces])

    hidden_part(g_ff[0], sizes[0])
    hidden_part(g_ff[1], sizes[1])
    hidden_part(g_ff[2], sizes[2])
    add_grads(0)
    link.go(t_h_one, t_heads, g_ff[4], g_ff[5], during=[*turned, *sent])
    h_one_all = t_h_one.rows()
    hidden_part(g_ff[3], sizes[3])
    hidden_part(g_ff[4], sizes[4])
    add_grads(1)
    add_grads(2)
    link.go(t_heads, s_ff[0], g_ff[5], during=[*turned[3:], *sent[1:]])
    hidden_part(g_ff[5], sizes[5])
    t_back = TensorDirect(back_sum(d_gate_ups, False, n_tensor))
    link.go(s_ff[1], s_ff[0], during=t_back.parts)
    add_grads(3)
    add_grads(4)
    t_ffn = TensorScatter(
        [x.reshape(n_tensor // 2, sp_rows, width) for x in back_sum(hiddens, True, 2)]
    )
    link.go(t_back, s_ff[2], s_ff[1], during=[*t_ffn.sums, *sent[3:]])
    first_spec = pl.BlockSpec((1, sp_rows, width), lambda i: (0, 0, 0))
    back_terms = t_back.terms()
    d_mixed, d_attn_own, d_gain_two = pl.pallas_call(
        mixed_back_kernel,
        grid=(1,),
        in_specs=[square, square, whole((1, width)), whole((sp_rows, 1))]
        + [first_spec] * len(back_terms),
        out_specs=(square, square, whole((1, width))),
        out_shape=(
            jax.ShapeDtypeStruct((sp_rows, width), f32),
            jax.ShapeDtypeStruct((sp_rows, width), bf16),
            jax.ShapeDtypeStruct((1, width), f32),
        ),
        compiler_params=params(),
        cost_estimate=SMALL,
        name="mixed_back",
    )(mixed, cotangent, gain_two[None], live, *back_terms)

    d_heads = pl.pallas_call(
        heads_back_kernel,
        grid=(n_tensor,),
        in_specs=[whole((sp_rows, width)), *half_specs],
        out_specs=part_spec,
        out_shape=jax.ShapeDtypeStruct(packed, bf16),
        compiler_params=params(),
        cost_estimate=SMALL,
        name="heads_back",
    )(d_attn_own, *t_out.halves)
    def attend_back(first, count, grads, *held):
        shift = lambda spec: pl.BlockSpec(
            spec.block_shape, lambda i, h: spec.index_map(i, h + first)
        )
        q_part, kv_part = shift(q_spec), shift(kv_spec)
        return pl.pallas_call(
            attend_back_kernel,
            grid=(rows, count),
            in_specs=[q_part, q_part, limit_spec, pos_spec]
            + [kv_part] * 2
            + [pl.BlockSpec(memory_space=pl.ANY)] * len(held),
            out_specs=[q_part] + [kv_part] * 2,
            out_shape=[jax.ShapeDtypeStruct(packed, f32)]
            + [jax.ShapeDtypeStruct((n // 2,) + packed_kv, bf16)] * 2,
            scratch_shapes=[
                pltpu.VMEM((SLOTS, LANES), bf16),
                pltpu.VMEM((LANES, SLOTS), bf16),
                pltpu.VMEM((SLOTS, LANES), f32),
            ],
            input_output_aliases={6 + i: i for i in range(len(held))},
            compiler_params=params(2),
            cost_estimate=SMALL,
            name="attend_back",
        )(queries, grads, limit, key_pos, *kv_halves, *held)

    held = attend_back(0, 3, d_heads)
    t_attn = TensorGather(d_attn_own)
    link.go(t_ffn, s_ff[3], s_ff[2], s_ff[0], s_ff[1], during=held)
    d_query, d_low, d_high = attend_back(3, HEADS_KV - 3, after(d_heads, *link.done), *held)

    def key_grads(begin, end, arrived, kind):
        if begin >= n // 2:
            return d_high
        return plus(d_low[begin:end].astype(f32), arrived, kind)

    s_keys = Scatter(key_grads)
    d_q_low, d_q_gain = pl.pallas_call(
        query_back_kernel,
        grid=(n_tensor,),
        in_specs=[part_spec, head_spec, whole(one_head), whole(one_head), whole((1, HEAD))],
        out_specs=(head_spec, whole((1, HEAD))),
        out_shape=(
            jax.ShapeDtypeStruct(heads_shape, bf16),
            jax.ShapeDtypeStruct((1, HEAD), f32),
        ),
        compiler_params=params(),
        cost_estimate=SMALL,
        name="query_back",
    )(d_query, q_raw, cos, sin, q_gain)

    def product(left, right):
        wide = right.shape[1]
        count = width // 256
        grid = width // 512
        halves = pl.pallas_call(
            product_kernel,
            grid=(grid,),
            in_specs=[pl.BlockSpec((rows_all // 2, 512), lambda j: (0, j))] * 2
            + [whole(right.shape)],
            out_specs=(
                pl.BlockSpec((2, wide, 256), lambda j: (jnp.minimum(j, grid // 2 - 1), 0, 0)),
                pl.BlockSpec((2, wide, 256), lambda j: (jnp.maximum(j - grid // 2, 0), 0, 0)),
            ),
            out_shape=[jax.ShapeDtypeStruct((count // 2, wide, 256), bf16)] * 2,
            scratch_shapes=[pltpu.VMEM((wide, rows_all), bf16)],
            compiler_params=params(),
            cost_estimate=SMALL,
            name="product",
        )(*left, right)
        return split_places(halves, wide)

    def sum_of(halves):
        def make(begin, end, arrived, kind):
            if begin >= n // 2:
                return halves[1]
            return plus(halves[0][begin:end].astype(f32), arrived, kind)

        return Scatter(make)

    t_query_back = TensorExchange(d_q_low)
    link.go(t_attn, s_ff[4], s_ff[3], s_ff[2], during=[d_q_low])
    add_grads(5)
    link.go(t_attn, t_query_back, s_keys, s_ff[4], t_ffn, during=[sent[5]])
    ffn_terms = t_ffn.terms()
    outputs = pl.pallas_call(
        functools.partial(finish_kernel, tuple(order)),
        grid=(1,),
        in_specs=[smem, square, whole((sp_rows, 1))] + [first_spec] * len(ffn_terms),
        out_specs=square,
        out_shape=low_square,
        compiler_params=params(),
        cost_estimate=SMALL,
        name="finish",
    )(index, mixed, live, *ffn_terms)
    d_attn = t_attn.rows()
    out_halves = product(d_attn, t_heads.rows())
    link.go(t_query_back, s_keys, s_ff[5], s_ff[3], s_ff[4], during=[*out_halves, outputs])
    s_out = sum_of(out_halves)
    link.go(s_keys, s_out, s_ff[5])
    d_kv = s_keys.result()
    query_halves = product(h_one_all, after(t_query_back.rows(), d_kv))
    s_query = sum_of(query_halves)
    d_kv_low, d_k_gain = pl.pallas_call(
        key_back_kernel,
        out_shape=(
            jax.ShapeDtypeStruct((sp_rows, kv_cols), bf16),
            jax.ShapeDtypeStruct((1, HEAD), f32),
        ),
        compiler_params=pltpu.CompilerParams(vmem_limit_bytes=VMEM_LIMIT),
        cost_estimate=SMALL,
        name="key_value_back",
    )(d_kv, kv_raw, cos, sin, k_gain)
    kv_part = kv_cols // n_tensor
    t_kv_back = Direct(
        [
            lax.dynamic_slice_in_dim(d_kv_low, (tensor ^ s) * kv_part, kv_part, axis=1)
            for s in tensor_order
        ]
    )
    grad_rel, d_gain_one = pl.pallas_call(
        back_kernel,
        grid=(n_tensor,),
        in_specs=[
            head_spec,
            both_spec,
            whole((sp_rows, kv_cols)),
            whole((width, kv_cols)),
            square,
            whole((1, width)),
            square,
        ],
        out_specs=(square, whole((1, width))),
        out_shape=(
            jax.ShapeDtypeStruct((sp_rows, width), bf16),
            jax.ShapeDtypeStruct((1, width), f32),
        ),
        scratch_shapes=[pltpu.VMEM((sp_rows, width), f32)],
        compiler_params=params(),
        cost_estimate=SMALL,
        name="h_one_back",
    )(d_q_low, query_all, d_kv_low, kv_all, inputs, gain_one[None], d_mixed)
    def collect(first, last, *held):
        terms = [[lows[c], *s_ff[c].raw] for c in range(first, last)]
        flat = [x for group in terms for x in group]
        if not held:
            flat[0] = after(flat[0], grad_rel)
        return pl.pallas_call(
            functools.partial(collect_kernel, len(terms), len(terms[0])),
            grid=(len(terms),),
            in_specs=[pl.BlockSpec((1,) + x.shape[1:], lambda i: (0, 0, 0)) for x in flat]
            + [pl.BlockSpec(memory_space=pl.ANY)] * len(held),
            out_specs=(
                pl.BlockSpec((cols, 2, unit), lambda i: (0, 0, first + i)),
                pl.BlockSpec((unit, cols), lambda i: (first + i, 0)),
            ),
            out_shape=(
                jax.ShapeDtypeStruct((cols, 2, ff), f32),
                jax.ShapeDtypeStruct((ff, cols), f32),
            ),
            input_output_aliases={len(flat) + i: i for i in range(len(held))},
            compiler_params=params(),
            cost_estimate=SMALL,
            name="collect",
        )(*flat, *held)

    early_sums = collect(0, FF_LAST)
    link.done += [*query_halves, *early_sums, grad_rel]
    link.go(t_kv_back, s_out, s_query)
    grad_inputs = call(
        functools.partial(leave_kernel, tuple(order)),
        low_square,
        "leave",
        index,
        grad_rel,
        specs=[smem, vmem],
    )

    gain_parts = jnp.concatenate([d_gain_one, d_gain_two]).reshape(2, n, cols).transpose(1, 0, 2)
    head_rows = max(2 * HEAD // cols, 1)
    head_parts = jnp.concatenate([d_q_gain, d_k_gain]).reshape(1, -1)
    head_parts = jnp.pad(head_parts, ((0, 0), (0, head_rows * cols - 2 * HEAD)))
    head_parts = jnp.broadcast_to(head_parts.reshape(1, head_rows, cols), (n, head_rows, cols))
    small_parts = jnp.concatenate([gain_parts, head_parts], axis=1)
    kv_halves_back = product(h_one_all, t_kv_back.rows())

    def with_small(side):
        begin = side * n // 2
        small_here = small_parts[begin : begin + n // 2].astype(bf16)
        return jnp.concatenate([kv_halves_back[side], small_here], axis=1)

    s_kv = ScatterSoon(with_small(0), with_small(1))
    link.go(s_kv, s_query, s_out, s_ff[5])
    sum_in, sum_down = collect(FF_LAST, len(sizes), *early_sums)
    link.go(s_kv, s_query, during=[sum_in, sum_down])
    t_sums = TensorAll(s_kv.result().astype(bf16))
    link.go(t_sums)
    stack = t_sums.stack
    small = jnp.sum(stack[:, kv_part:].astype(f32), axis=0)
    stack = stack[:, :kv_part]
    sum_gains = small[:2]
    sum_heads = small[2:].reshape(-1)[: 2 * HEAD].reshape(2, HEAD)
    places = [
        sum((((tensor ^ i) // mask) & 1) << k for k, mask in enumerate(masks_of("tensor")))
        for i in range(n_tensor)
    ]
    sum_kv = jnp.concatenate(
        [
            lax.dynamic_index_in_dim(stack, places[i], axis=0, keepdims=False)
            for i in range(n_tensor)
        ],
        axis=0,
    ).T.astype(f32)
    sum_out = s_out.result()
    sum_query = s_query.result().T
    return (
        outputs,
        grad_inputs,
        sum_query,
        sum_kv.astype(f32),
        sum_out,
        sum_in,
        sum_down,
        sum_gains,
        sum_heads,
    )


def solution(mesh):
    in_specs = (
        P(("dp", "tensor"), None),
        P(("dp", "tensor"), None),
        P("dp", "tensor"),
        P("dp", None),
        P("tensor", "dp"),
        P("dp", None, "tensor"),
        P("tensor", "dp"),
        P(None, "dp"),
        P(),
        P(),
        P(),
    )
    out_specs = (
        P(("dp", "tensor"), None),
        P(("dp", "tensor"), None),
        P("dp", "tensor"),
        P("dp", None),
        P("tensor", "dp"),
        P("dp", None, "tensor"),
        P("tensor", "dp"),
        P(None, "dp"),
        P(),
    )
    return jax.shard_map(local, mesh=mesh, in_specs=in_specs, out_specs=out_specs, check_vma=False)
```

```python
import functools

import jax
import jax.numpy as jnp
from jax import lax
from jax.experimental import layout
from jax.experimental import pallas as pl
from jax.experimental.pallas import tpu as pltpu
from jax.sharding import PartitionSpec as P

HEADS_KV = 5
HEAD = 64
SLOTS = 2048
STRETCH = 64
LANES = 128
FF_PARTS = (1, 1, 1, 1, 1, 1)
FF_LAST = len(FF_PARTS) - 1
VMEM_LIMIT = 48 * 1024 * 1024
SMALL = pl.CostEstimate(flops=1000, bytes_accessed=1000, transcendentals=0)

eps_norm = 1e-06
rope_base = 10000.0
neg_large = -1e30
f32 = jnp.float32
bf16 = jnp.bfloat16
contract_rows = (((0,), (0,)), ((), ()))
contract_cols = (((1,), (1,)), ((), ()))


def dot(a, b, dims=(((1,), (0,)), ((), ()))):
    return lax.dot_general(a, b, dims, preferred_element_type=f32)


def after(value, *deps):
    return lax.optimization_barrier((value, *deps))[0]


def masks_of(axis):
    size = lax.axis_size(axis)
    bits = [1 << i for i in range(1, size.bit_length() - 1)]
    return bits + [1]


def order_of(axis):
    order = [0]
    for mask in masks_of(axis):
        order = order + [r ^ mask for r in order]
    return order


def swap(value, axis, mask):
    size = lax.axis_size(axis)
    return lax.ppermute(value, axis, [(i, i ^ mask) for i in range(size)])


def join(first, second):
    both = jnp.concatenate([first, second], axis=0)
    return layout.with_layout_constraint(both, layout.Layout(tuple(range(both.ndim))))


def gather(value, axis):
    stack = value[None]
    for mask in masks_of(axis):
        stack = join(stack, swap(stack, axis, mask))
    return stack


def gather_rows(value, axis):
    index = lax.axis_index(axis)
    stack = value
    size = lax.axis_size(axis)
    bit = size // 2
    at = value.ndim - 2
    while bit:
        other = swap(stack, axis, bit)
        upper = (index & bit) != 0
        stack = jnp.stack(
            [jnp.where(upper, other, stack), jnp.where(upper, stack, other)], axis=at
        )
        bit //= 2
        at += 1
    return stack.reshape(value.shape[:-2] + (size,) + value.shape[-2:])


def scatter(make, axis):
    half = lax.axis_size(axis)
    arrived = []
    for mask in reversed(masks_of(axis)):
        half //= 2
        sent = make(half, 2 * half, [x[half : 2 * half] for x in arrived], bf16)
        arrived = [x[:half] for x in arrived] + [swap(sent, axis, mask)]
    return make(0, 1, arrived, f32)[0]


def phases():
    masks = masks_of("dp")
    return [masks[:1], masks[1:-1], masks[-1:]]


class Item:
    late = ()

    def bring(self, value, axis, mask):
        got = swap(value, axis, mask)
        return after(got, *self.late) if self.late else got


class Gather(Item):
    def __init__(self, value):
        self.stack, self.halves, self.phase = value[None], None, 0

    def value(self):
        return self.stack

    def advance(self, value):
        for mask in phases()[self.phase]:
            got = self.bring(value, "dp", mask)
            self.halves = (value, got)
            value = join(value, got)
        self.stack = value
        self.phase += 1
        return got

    def pieces(self):
        half = order_of("dp")[: lax.axis_size("dp") // 2]
        return [(x, [r ^ m for r in half]) for x, m in zip(self.halves, (0, masks_of("dp")[-1]))]


class GatherSoon(Item):
    def __init__(self, value):
        self.stack, self.phase = value[None], 0

    def value(self):
        return self.stack

    def advance(self, value):
        order = order_of("dp")
        if self.phase:
            got = [self.bring(value, "dp", masks_of("dp")[-1])]
        else:
            got = [self.bring(value, "dp", r) for r in order[1 : len(order) // 2]]
        both = jnp.concatenate([value, *got], axis=0)
        self.stack = layout.with_layout_constraint(both, layout.Layout(tuple(range(both.ndim))))
        self.phase += 1
        return got


class ScatterSoon(Item):
    def __init__(self, low, high):
        self.low, self.high, self.phase = low, high, 0

    def value(self):
        if self.phase == 0:
            return self.high
        self.total = self.low.astype(f32) + self.first.astype(f32)
        return self.total[1:].astype(bf16)

    def advance(self, value):
        order = order_of("dp")
        self.phase += 1
        if self.phase == 1:
            self.first = self.bring(value, "dp", order[len(order) // 2])
            return self.first
        self.rest = [
            self.bring(value[p - 1], "dp", order[p]) for p in range(1, len(order) // 2)
        ]
        return self.rest

    def result(self):
        return self.total[0] + sum(x.astype(f32) for x in self.rest)


class TensorAll(Item):
    def __init__(self, value):
        self.own = value

    def value(self):
        return self.own

    def advance(self, value):
        got = [self.bring(value, "tensor", r) for r in order_of("tensor")[1:]]
        self.stack = jnp.stack([value, *got])
        return got


class GatherLate(Item):
    def __init__(self, value):
        self.parts, self.phase = [(value[None], [0])], 0

    def value(self):
        return self.parts[max(self.phase - 2, 0)][0]

    def advance(self, value):
        masks = masks_of("dp")
        masks = [masks[-1:], masks[:1], masks[1:-1], masks[1:-1]][self.phase]
        at = max(self.phase - 2, 0)
        places = self.parts[at][1]
        for mask in masks:
            got = self.bring(value, "dp", mask)
            halves = [(value, places), (got, [r ^ mask for r in places])]
            places = places + halves[1][1]
            if mask != masks[-1] or self.phase == 0:
                value = join(value, got)
        if self.phase == 0:
            self.parts = [(value, places)]
        elif self.phase == 1:
            self.parts = halves
        elif self.phase == 2:
            self.parts, self.first = [None, self.parts[1]], halves
        else:
            self.parts = self.first + halves
        self.phase += 1
        return got

    def pieces(self):
        return self.parts


class Scatter(Item):
    def __init__(self, make):
        self.make, self.half, self.arrived, self.phase = make, lax.axis_size("dp"), [], 2
        self.raw = []

    def value(self):
        half = self.half // 2
        return self.make(half, 2 * half, [x[half : 2 * half] for x in self.arrived], bf16)

    def advance(self, value):
        for k, mask in enumerate(reversed(phases()[self.phase])):
            if k:
                value = self.value()
            self.half //= 2
            got = self.bring(value, "dp", mask)
            self.arrived = [x[: self.half] for x in self.arrived] + [got]
            self.raw.append(got)
        self.phase -= 1
        return got

    def result(self):
        return self.make(0, 1, self.arrived, f32)[0]


class TensorGather(Item):
    def __init__(self, value):
        self.stack, self.masks = value[None], masks_of("tensor")

    def value(self):
        return self.stack

    def advance(self, value):
        got = self.bring(value, "tensor", self.masks[0])
        self.halves = (value, got)
        self.stack, self.masks = join(value, got), self.masks[1:]
        return got

    def rows(self):
        return [x.reshape(-1, x.shape[-1]) for x in self.halves]


class PairRows(Item):
    def __init__(self, value):
        self.stack = value

    def value(self):
        return self.stack

    def advance(self, value):
        got = self.bring(value, "tensor", 1)
        upper = (lax.axis_index("tensor") & 1) != 0
        self.stack = jnp.stack(
            [jnp.where(upper, got, value), jnp.where(upper, value, got)], axis=value.ndim - 2
        )
        return got


class TensorScatter(Item):
    def __init__(self, sums):
        self.sums, self.masks, self.arrived = sums, masks_of("tensor")[::-1], []

    def value(self):
        half = 1 << (len(self.masks) - 1)
        if half == self.sums[1].shape[0]:
            return self.sums[1]
        return plus(
            self.sums[0][half : 2 * half].astype(f32),
            [x[half : 2 * half] for x in self.arrived],
            bf16,
        )

    def advance(self, value):
        self.arrived.append(self.bring(value, "tensor", self.masks[0]))
        self.masks = self.masks[1:]
        return self.arrived[-1]

    def terms(self):
        return [self.sums[0], *self.arrived]


class TensorDirect(Item):
    def __init__(self, parts):
        self.parts = list(parts)

    def value(self):
        return self.parts

    def advance(self, value):
        order = order_of("tensor")
        self.got = [self.bring(value[p], "tensor", order[p]) for p in range(1, len(order))]
        return self.got

    def terms(self):
        return [x[None] for x in [self.parts[0], *self.got]]


class TensorExchange(Item):
    def __init__(self, stack):
        self.stack, self.masks = stack[:, None], masks_of("tensor")

    def value(self):
        return self.stack[1::2]

    def advance(self, value):
        got = self.bring(value, "tensor", self.masks[0])
        self.stack = jnp.concatenate([self.stack[0::2], got], axis=1)
        self.masks = self.masks[1:]
        return got

    def rows(self):
        return self.stack.reshape((-1,) + self.stack.shape[3:])


class Direct(Item):
    def __init__(self, parts):
        self.parts = parts

    def value(self):
        return jnp.stack(self.parts)

    def advance(self, value):
        order = order_of("tensor")
        got = [value[0]] + [
            self.bring(value[p], "tensor", order[p]) for p in range(1, len(order))
        ]
        self.all = jnp.concatenate(got, axis=0)
        return self.all

    def rows(self):
        return self.all


class Rounds:
    def __init__(self):
        self.done = []

    def go(self, *items, ends=(), during=()):
        done = list(ends)
        for item in items:
            value = item.value()
            if self.done:
                value = after(value, *self.done)
            item.late = during
            got = item.advance(value)
            done += got if isinstance(got, list) else [got]
        self.done = done


def plus(total, arrived, kind):
    for other in arrived:
        total = total + other.astype(f32)
    return total.astype(kind)


def scaled_norm(value_in, gain_vec):
    return (
        value_in
        * lax.rsqrt(jnp.mean(value_in * value_in, axis=-1, keepdims=True) + eps_norm)
        * gain_vec
    )


def silu_product(gate, up_part):
    return gate * jax.nn.sigmoid(gate) * up_part


def params(steps=1):
    return pltpu.CompilerParams(
        dimension_semantics=("arbitrary",) * steps, vmem_limit_bytes=VMEM_LIMIT
    )


def swap_halves(value):
    half = HEAD // 2
    return jnp.concatenate([value[:, half:], value[:, :half]], axis=1)


def rope_one(raw, gain, cos, sin, factor):
    scale = lax.rsqrt(jnp.mean(raw * raw, axis=-1, keepdims=True) + eps_norm)
    normed = raw * scale * gain
    return (normed * cos + swap_halves(normed) * sin) * factor


def rope_back(raw, gain, cos, sin, factor, grad):
    grad = grad * factor
    grad = grad * cos - swap_halves(grad) * sin
    scale = lax.rsqrt(jnp.mean(raw * raw, axis=-1, keepdims=True) + eps_norm)
    weighted = grad * gain
    back = scale * weighted - raw * (
        scale * scale * scale * jnp.mean(raw * weighted, axis=-1, keepdims=True)
    )
    return back, jnp.sum(grad * raw * scale, axis=0, keepdims=True)


def query_kernel(h_ref, w_ref, cos_ref, sin_ref, gain_ref, raw_ref, out_ref):
    cols = w_ref.shape[3]
    raw = sum(
        dot(h_ref[:, r * cols : (r + 1) * cols], w_ref[0, r], contract_cols)
        for r in range(w_ref.shape[1])
    )
    raw_ref[0] = raw
    rows, blocks = out_ref.shape[0], out_ref.shape[2]
    for h in range(HEADS_KV):
        turned = rope_one(
            raw[:, h * HEAD : (h + 1) * HEAD], gain_ref[...], cos_ref[...], sin_ref[...], 0.125
        )
        wide = jnp.concatenate([turned, jnp.zeros_like(turned)], axis=1).astype(bf16)
        out_ref[:, h, :, 0] = wide.reshape(rows, blocks, STRETCH, LANES)


def key_kernel(h_ref, w_ref, cos_ref, sin_ref, gain_ref, raw_ref, out_ref):
    raw = dot(h_ref[...], w_ref[...])
    raw_ref[...] = raw
    rows, blocks = out_ref.shape[0], out_ref.shape[2]
    for h in range(HEADS_KV):
        turned = rope_one(
            raw[:, h * HEAD : (h + 1) * HEAD], gain_ref[...], cos_ref[...], sin_ref[...], 1.0
        )
        start = (HEADS_KV + h) * HEAD
        wide = jnp.concatenate([turned, raw[:, start : start + HEAD]], axis=1).astype(bf16)
        out_ref[:, h] = wide.reshape(rows, blocks, STRETCH, LANES)


def load_keys(halves, kv, kvt):
    places = [(half, i) for half in halves for i in range(half.shape[0])]
    group = len(places) * STRETCH
    for g in range(halves[0].shape[3]):
        for r, (half, i) in enumerate(places):
            start = g * group + r * STRETCH
            kv[start : start + STRETCH, :] = half[i, 0, 0, g]
    kvt[...] = kv[...].T
    return group


def attend_kernel(q_ref, limit_ref, keypos_ref, low_ref, high_ref, out_ref, kv, kvt):
    blocks = q_ref.shape[2]
    group = load_keys((low_ref, high_ref), kv, kvt)
    for b in range(blocks):
        span = (b + 1) * group
        q = q_ref[0, 0, b].reshape(-1, LANES)
        scores = dot(kv[:span], q, contract_cols)
        scores = jnp.where(keypos_ref[0, :span] <= limit_ref[0, b], scores, neg_large)
        top = jnp.max(scores, axis=0, keepdims=True)
        weights = jnp.exp(scores - top)
        total = jnp.sum(weights, axis=0, keepdims=True)
        heads = dot(kvt[:, :span], weights.astype(bf16)) / total
        out_ref[0, 0, b] = heads.T.astype(bf16).reshape(q_ref.shape[3:])


def attend_back_kernel(q_ref, g_ref, limit_ref, keypos_ref, low_ref, high_ref, *rest):
    dq_ref, dlow_ref, dhigh_ref, kv, kvt, acc = rest[-6:]
    blocks = q_ref.shape[2]
    group = load_keys((low_ref, high_ref), kv, kvt)
    acc[...] = jnp.zeros_like(acc)
    for b in range(blocks):
        span = (b + 1) * group
        q = q_ref[0, 0, b].reshape(-1, LANES)
        grad = g_ref[0, 0, b].reshape(-1, LANES)
        scores = dot(kv[:span], q, contract_cols)
        scores = jnp.where(keypos_ref[0, :span] <= limit_ref[0, b], scores, neg_large)
        top = jnp.max(scores, axis=0, keepdims=True)
        weights = jnp.exp(scores - top)
        probs = weights * (1.0 / jnp.sum(weights, axis=0, keepdims=True))
        d_probs = dot(kv[:span], grad, contract_cols)
        delta = jnp.sum(probs * d_probs, axis=0, keepdims=True)
        d_scores = (probs * (d_probs - delta)).astype(bf16)
        dq = dot(kvt[:, :span], d_scores)
        dq_ref[0, 0, b] = dq.T.reshape(q_ref.shape[3:])
        acc[:span] += dot(d_scores, q) + dot(probs.astype(bf16), grad)
    count = dlow_ref.shape[0]
    for out, first in ((dlow_ref, 0), (dhigh_ref, count)):
        for r in range(count):
            for g in range(blocks):
                start = g * group + (first + r) * STRETCH
                out[r, 0, 0, g] = acc[start : start + STRETCH].astype(bf16)


def out_kernel(o_ref, w_low, w_high, x_ref, live_ref, gain_ref, mixed_ref, h_ref, heads_ref):
    rows = heads_ref.shape[1]
    heads = jnp.concatenate(
        [o_ref[:, h, :, 0].reshape(rows, LANES)[:, HEAD:] for h in range(HEADS_KV)], axis=1
    )
    heads_ref[0] = heads
    cols = w_low.shape[3]
    low = pl.program_id(0) < pl.num_programs(0) // 2

    @pl.when(pl.program_id(0) == 0)
    def _():
        mixed_ref[...] = jnp.zeros_like(mixed_ref)

    for r in range(w_low.shape[1]):
        here = jnp.where(low, w_low[0, r], w_high[0, r])
        mixed_ref[:, r * cols : (r + 1) * cols] += dot(heads, here)

    @pl.when(pl.program_id(0) == pl.num_programs(0) - 1)
    def _():
        mixed = x_ref[...].astype(f32) + live_ref[...] * mixed_ref[...]
        mixed_ref[...] = mixed
        h_ref[...] = scaled_norm(mixed, gain_ref[...]).astype(bf16)


def norm_back(value, gain, grad):
    scale = lax.rsqrt(jnp.mean(value * value, axis=-1, keepdims=True) + eps_norm)
    weighted = grad * gain
    inner = jnp.mean(value * weighted, axis=-1, keepdims=True)
    back = scale * weighted - value * (scale * scale * scale * inner)
    return back, jnp.sum(grad * value * scale, axis=0, keepdims=True)


def mixed_back_kernel(mixed_ref, cot_ref, gain_ref, live_ref, *rest):
    terms, (d_mixed_ref, d_attn_ref, dgain_ref) = rest[:-3], rest[-3:]
    grad = sum(ref[0].astype(f32) for ref in terms)
    back, dgain_ref[...] = norm_back(mixed_ref[...], gain_ref[...], grad)
    d_mixed = cot_ref[...].astype(f32) + back
    d_mixed_ref[...] = d_mixed
    d_attn_ref[...] = (live_ref[...] * d_mixed).astype(bf16)


def heads_back_kernel(d_ref, w_low, w_high, out_ref):
    cols = w_low.shape[3]
    low = pl.program_id(0) < pl.num_programs(0) // 2
    grad = sum(
        dot(
            d_ref[:, r * cols : (r + 1) * cols],
            jnp.where(low, w_low[0, r], w_high[0, r]),
            contract_cols,
        )
        for r in range(w_low.shape[1])
    )
    rows, blocks = out_ref.shape[0], out_ref.shape[2]
    for h in range(HEADS_KV):
        part = grad[:, h * HEAD : (h + 1) * HEAD]
        wide = jnp.concatenate([jnp.zeros_like(part), part], axis=1).astype(bf16)
        out_ref[:, h, :, 0] = wide.reshape(rows, blocks, STRETCH, LANES)


def query_back_kernel(dq_ref, raw_ref, cos_ref, sin_ref, gain_ref, out_ref, dgain_ref):
    @pl.when(pl.program_id(0) == 0)
    def _():
        dgain_ref[...] = jnp.zeros_like(dgain_ref)

    raw = raw_ref[0]
    parts = []
    for h in range(HEADS_KV):
        grad = dq_ref[:, h, :, 0].reshape(raw.shape[0], LANES)[:, :HEAD]
        back, dgain = rope_back(
            raw[:, h * HEAD : (h + 1) * HEAD],
            gain_ref[...],
            cos_ref[...],
            sin_ref[...],
            0.125,
            grad,
        )
        parts.append(back)
        dgain_ref[...] += dgain
    out_ref[0] = jnp.concatenate(parts, axis=1).astype(bf16)


def key_back_kernel(sum_ref, raw_ref, cos_ref, sin_ref, gain_ref, out_ref, dgain_ref):
    raw = raw_ref[...]
    keys, values = [], []
    total = jnp.zeros_like(dgain_ref)
    for h in range(HEADS_KV):
        both = sum_ref[:, h].reshape(raw.shape[0], LANES)
        back, dgain = rope_back(
            raw[:, h * HEAD : (h + 1) * HEAD],
            gain_ref[...],
            cos_ref[...],
            sin_ref[...],
            1.0,
            both[:, :HEAD],
        )
        keys.append(back)
        values.append(both[:, HEAD:])
        total = total + dgain
    dgain_ref[...] = total
    out_ref[...] = jnp.concatenate(keys + values, axis=1).astype(bf16)


def back_kernel(
    dq_ref, wq_ref, dkv_ref, wkv_ref, x_ref, gain_ref, d_mixed_ref, out_ref, dgain_ref, acc
):
    @pl.when(pl.program_id(0) == 0)
    def _():
        acc[...] = dot(dkv_ref[...], wkv_ref[...], contract_cols)

    cols = wq_ref.shape[3]
    for r in range(wq_ref.shape[1]):
        acc[:, r * cols : (r + 1) * cols] += dot(dq_ref[0], wq_ref[0, r])

    @pl.when(pl.program_id(0) == pl.num_programs(0) - 1)
    def _():
        back, dgain_ref[...] = norm_back(x_ref[...].astype(f32), gain_ref[...], acc[...])
        out_ref[...] = (d_mixed_ref[...] + back).astype(bf16)


def turn_kernel(x_ref, out_ref):
    out_ref[...] = x_ref[...].T


def shards_kernel(in_ref, down_ref, *parts):
    ff = down_ref.shape[0]
    start = 0
    for ref in parts:
        part = ref.shape[1] // 3
        ref[:, :part] = in_ref[:, start : start + part]
        ref[:, part : 2 * part] = in_ref[:, ff + start : ff + start + part]
        ref[:, 2 * part :] = down_ref[start : start + part, :].T
        start += part


def turn_columns(order, back, index, value):
    size = len(order)
    cols = value.shape[1] // size

    def pick(value, places):
        return jnp.concatenate([value[:, p * cols : (p + 1) * cols] for p in places], axis=1)

    if back:
        value = pick(value, [order.index(i) for i in range(size)])
    bit = 1
    while bit < size:
        value = jnp.where((index & bit) != 0, pick(value, [i ^ bit for i in range(size)]), value)
        bit *= 2
    return value if back else pick(value, order)


def enter_kernel(order, index_ref, x_ref, cot_ref, live_ref, x_out, cot_out, d_ffn_out):
    x_out[...] = turn_columns(order, False, index_ref[0], x_ref[...].astype(f32)).astype(bf16)
    cot = turn_columns(order, False, index_ref[0], cot_ref[...].astype(f32))
    cot_out[...] = cot.astype(bf16)
    d_ffn_out[...] = (cot * live_ref[...]).astype(bf16)


def leave_kernel(order, index_ref, x_ref, out_ref):
    value = x_ref[...].astype(f32)
    out_ref[...] = turn_columns(order, True, index_ref[0], value).astype(bf16)


def finish_kernel(order, index_ref, mixed_ref, live_ref, *rest):
    terms, out_ref = rest[:-1], rest[-1]
    ffn = sum(ref[0].astype(f32) for ref in terms)
    value = mixed_ref[...] + live_ref[...] * ffn
    out_ref[...] = turn_columns(order, True, index_ref[0], value).astype(bf16)


def product_kernel(left_low, left_high, right_ref, low_ref, high_ref, turned):
    @pl.when(pl.program_id(0) == 0)
    def _():
        turned[...] = right_ref[...].T

    out = halves_product(turned[...], left_low, left_high).astype(bf16)
    low = pl.program_id(0) < pl.num_programs(0) // 2
    span = low_ref.shape[2]
    for out_ref, here in ((low_ref, low), (high_ref, jnp.logical_not(low))):

        @pl.when(here)
        def _(out_ref=out_ref):
            for p in range(out_ref.shape[0]):
                out_ref[p] = out[:, p * span : (p + 1) * span]


def pick_columns(value, places, cols):
    if places == list(range(places[0], places[0] + len(places))):
        return value[:, places[0] * cols : (places[-1] + 1) * cols]
    return jnp.concatenate([value[:, p * cols : (p + 1) * cols] for p in places], axis=1)


def hidden_kernel(all_places, h_low, h_high, d_low, d_high, *refs):
    pieces, (hidden_ref, d_gate_up_ref, turned_ref) = refs[:-3], refs[-3:]
    part = hidden_ref.shape[1]
    low = pl.program_id(0) < pl.num_programs(0) // 2
    h = jnp.where(low, h_low[...], h_high[...])
    d = jnp.where(low, d_low[...], d_high[...])
    gate_up = d_hidden = None
    for places, ref in zip(all_places, pieces):
        cols = ref.shape[0] // len(places)
        first = dot(pick_columns(h, places, cols), ref[:, : 2 * part])
        second = dot(pick_columns(d, places, cols), ref[:, 2 * part :])
        gate_up = first if gate_up is None else gate_up + first
        d_hidden = second if d_hidden is None else d_hidden + second
    gate, up = gate_up[:, :part], gate_up[:, part:]
    sig = jax.nn.sigmoid(gate)
    swish = gate * sig
    hidden = (swish * up).astype(bf16)
    d_gate = (d_hidden * up * (sig + swish * (1.0 - sig))).astype(bf16)
    d_up = (d_hidden * swish).astype(bf16)
    hidden_ref[...] = hidden
    d_gate_up_ref[:, :part] = d_gate
    d_gate_up_ref[:, part:] = d_up
    turned_ref[:part] = d_gate.T
    turned_ref[part : 2 * part] = d_up.T
    turned_ref[2 * part :] = hidden.T


def halves_product(left, low_ref, high_ref):
    middle = low_ref.shape[0]
    return dot(left[:, :middle], low_ref[...]) + dot(left[:, middle:], high_ref[...])


def grads_kernel(h_low, h_high, d_low, d_high, turned_ref, low_ref, high_ref):
    split = turned_ref.shape[0] // 3 * 2
    first = halves_product(turned_ref[:split], h_low, h_high).astype(bf16)
    second = halves_product(turned_ref[split:], d_low, d_high).astype(bf16)
    low = pl.program_id(0) < pl.num_programs(0) // 2
    span = low_ref.shape[2]
    for out_ref, here in ((low_ref, low), (high_ref, jnp.logical_not(low))):

        @pl.when(here)
        def _(out_ref=out_ref):
            for p in range(out_ref.shape[0]):
                out_ref[p, :split] = first[:, p * span : (p + 1) * span]
                out_ref[p, split:] = second[:, p * span : (p + 1) * span]


def collect_kernel(count, each, *refs):
    in_ref, down_ref = refs[-2:]
    part = down_ref.shape[0]
    for c in range(count):

        @pl.when(pl.program_id(0) == c)
        def _(c=c):
            total = sum(ref[0].astype(f32) for ref in refs[c * each : (c + 1) * each])
            in_ref[:, 0, :] = total[:part].T
            in_ref[:, 1, :] = total[part : 2 * part].T
            down_ref[...] = total[2 * part :]


def back_sum_kernel(all_places, *refs):
    count = len(all_places)
    half = refs[-1].shape[1] // 2
    totals = [None, None]
    at = count
    for c, pieces in enumerate(all_places):
        terms = [dot(refs[c][...], refs[at + i][...], contract_cols) for i in range(len(pieces))]
        at += len(pieces)
        if len(pieces) > 2:
            blocks = {}
            for places, term in zip(pieces, terms):
                cols = term.shape[1] // len(places)
                for i, p in enumerate(places):
                    blocks[p] = term[:, i * cols : (i + 1) * cols]
            middle = len(blocks) // 2
            terms = [
                jnp.concatenate([blocks[side * middle + i] for i in range(middle)], axis=1)
                for side in range(2)
            ]
        totals = [t if old is None else old + t for old, t in zip(totals, terms)]
    outs = refs[at:]
    span = outs[0].shape[0]
    rows = totals[0].shape[0]
    each = max(rows // span, 1)
    for step in range(len(outs) // each):

        @pl.when(pl.program_id(0) == step)
        def _(step=step):
            for i in range(each):
                for side in range(2):
                    block = totals[side][i * span : (i + 1) * span].astype(bf16)
                    outs[step * each + i][:, side * half : (side + 1) * half] = block


def whole(shape):
    return pl.BlockSpec(shape, lambda *_: (0,) * len(shape))


def local(
    inputs,
    cotangent,
    w_query,
    w_kv,
    w_out,
    w_in,
    w_down,
    norm_gains,
    head_gains,
    lengths,
    slot_blocks,
):
    sp_rows, width = inputs.shape
    n = lax.axis_size("dp")
    n_tensor = lax.axis_size("tensor")
    dp = lax.axis_index("dp")
    tensor = lax.axis_index("tensor")
    seq_count = lengths.shape[0]
    row_span = sp_rows * n_tensor // seq_count
    blocks = row_span // STRETCH
    rows = sp_rows // row_span
    per_row = SLOTS // STRETCH
    cols = width // n
    q_cols = w_query.shape[1]
    kv_cols = w_kv.shape[1]
    ff = w_down.shape[0]
    order = order_of("dp")
    tensor_order = order_of("tensor")
    rels = jnp.array(order, jnp.int32)

    smem = pl.BlockSpec(memory_space=pltpu.SMEM)

    def call(kernel, out_shape, name, *args, specs=None):
        return pl.pallas_call(
            kernel,
            in_specs=specs,
            out_shape=out_shape,
            compiler_params=pltpu.CompilerParams(vmem_limit_bytes=VMEM_LIMIT),
            cost_estimate=SMALL,
            name=name,
        )(*args)

    table = slot_blocks.reshape(n, n_tensor, rows, blocks)
    mine = lax.dynamic_index_in_dim(table, tensor, axis=1, keepdims=False)[dp ^ rels]
    inside = jnp.arange(STRETCH, dtype=jnp.int32)
    key_pos = (mine % per_row * STRETCH)[..., None] + inside
    own_pos = key_pos[0]
    own_len = lengths[mine[0] // per_row][..., None]
    live = (own_pos < own_len).astype(f32).reshape(sp_rows, 1)
    limit = jnp.minimum(own_pos, own_len - 1)
    limit = jnp.broadcast_to(limit[:, :, None, None, :], (rows, blocks, 1, n_tensor, STRETCH))
    limit = limit.reshape(rows, blocks, 1, n_tensor * STRETCH)
    key_pos = key_pos.transpose(1, 2, 0, 3).reshape(rows, SLOTS, 1)
    half = HEAD // 2
    frequency = rope_base ** (-2.0 * jnp.arange(half, dtype=f32) / HEAD)
    angles = own_pos.reshape(sp_rows, 1).astype(f32) * frequency
    cosine, sine = jnp.cos(angles), jnp.sin(angles)
    cos = jnp.concatenate([cosine, cosine], axis=1)
    sin = jnp.concatenate([-sine, sine], axis=1)
    head_float = head_gains.astype(f32)
    q_gain, k_gain = head_float[0:1], head_float[1:2]

    vmem = pl.BlockSpec(memory_space=pltpu.VMEM)
    index = dp.reshape(1)
    low_square = jax.ShapeDtypeStruct((sp_rows, width), bf16)
    inputs, cotangent, d_ffn_own = call(
        functools.partial(enter_kernel, tuple(order)),
        [low_square] * 3,
        "enter",
        index,
        inputs,
        cotangent,
        live,
        specs=[smem, vmem, vmem, vmem],
    )
    inputs_f = inputs.astype(f32)
    part = w_kv.shape[0] // 2
    kv_shard = lax.dynamic_slice_in_dim(w_kv, (tensor & 1) * part, part, axis=0)
    unit = ff // sum(FF_PARTS)
    sizes = [size * unit for size in FF_PARTS]
    query_shard = call(
        turn_kernel, jax.ShapeDtypeStruct((q_cols, cols), bf16), "turn", w_query, specs=[vmem]
    )
    shards = call(
        shards_kernel,
        [jax.ShapeDtypeStruct((cols, 3 * part), bf16) for part in sizes],
        "shards",
        w_in.reshape(cols, 2 * ff),
        w_down,
        specs=[vmem, vmem],
    )
    link = Rounds()
    g_kv, g_gains = GatherSoon(kv_shard), Gather(norm_gains)
    g_query, g_out = Gather(query_shard), Gather(w_out)
    g_ff = [Gather(x) for x in shards[:-1]] + [GatherLate(shards[-1])]
    link.go(g_kv, g_gains, g_query, during=[d_ffn_own, cos, sin, limit, *shards])
    link.go(g_kv, g_gains, g_query, g_out)
    t_kv = PairRows(g_kv.stack)
    link.go(t_kv, g_gains, g_query, g_out, g_ff[0])
    gains = g_gains.stack.transpose(1, 0, 2).reshape(2, width).astype(f32)
    gain_one, gain_two = gains[0], gains[1]
    h_one = scaled_norm(inputs_f, gain_one).astype(bf16)
    t_query = TensorGather(g_query.stack)
    kv_all = t_kv.stack.reshape(width, kv_cols)
    t_d_ffn = TensorGather(d_ffn_own)

    packed = (rows, HEADS_KV, blocks, n_tensor, STRETCH, LANES)
    packed_kv = (rows, HEADS_KV, blocks, STRETCH, LANES)
    both_spec = pl.BlockSpec((1, n, q_cols, cols), lambda s: (s, 0, 0, 0))
    half_specs = [
        pl.BlockSpec(
            (1, n, q_cols, cols), lambda s: (jnp.minimum(s, n_tensor // 2 - 1), 0, 0, 0)
        ),
        pl.BlockSpec(
            (1, n, q_cols, cols), lambda s: (jnp.maximum(s - n_tensor // 2, 0), 0, 0, 0)
        ),
    ]
    kv_raw, kv_own = pl.pallas_call(
        key_kernel,
        out_shape=(
            jax.ShapeDtypeStruct((sp_rows, kv_cols), f32),
            jax.ShapeDtypeStruct(packed_kv, bf16),
        ),
        compiler_params=pltpu.CompilerParams(vmem_limit_bytes=VMEM_LIMIT),
        cost_estimate=SMALL,
        name="key_value",
    )(h_one, kv_all, cos, sin, k_gain)
    g_keys = Gather(kv_own)
    link.go(t_query, g_out, g_ff[5], g_ff[0], g_keys)
    t_out = TensorGather(g_out.stack)
    link.go(t_query, t_out, g_keys, g_ff[0], g_ff[1])
    query_all = t_query.stack
    one_head = (sp_rows, HEAD)
    part_spec = pl.BlockSpec(
        (rows, HEADS_KV, blocks, 1, STRETCH, LANES), lambda s: (0, 0, 0, s, 0, 0)
    )
    q_raw, queries = pl.pallas_call(
        query_kernel,
        grid=(n_tensor,),
        in_specs=[
            whole((sp_rows, width)),
            both_spec,
            whole(one_head),
            whole(one_head),
            whole((1, HEAD)),
        ],
        out_specs=(pl.BlockSpec((1, sp_rows, q_cols), lambda s: (s, 0, 0)), part_spec),
        out_shape=(
            jax.ShapeDtypeStruct((n_tensor, sp_rows, q_cols), f32),
            jax.ShapeDtypeStruct(packed, bf16),
        ),
        compiler_params=params(),
        cost_estimate=SMALL,
        name="query",
    )(h_one, query_all, cos, sin, q_gain)
    link.go(t_out, t_d_ffn, g_keys, g_ff[1], g_ff[2], during=[queries, key_pos])
    kv_halves = g_keys.halves
    q_spec = pl.BlockSpec(
        (1, 1, blocks, n_tensor, STRETCH, LANES), lambda i, h: (i, h, 0, 0, 0, 0)
    )
    kv_spec = pl.BlockSpec(
        (n // 2, 1, 1, blocks, STRETCH, LANES), lambda i, h: (0, i, h, 0, 0, 0)
    )
    limit_spec = pl.BlockSpec(
        (1, blocks, 1, n_tensor * STRETCH), lambda i, h: (i, 0, 0, 0)
    )
    pos_spec = pl.BlockSpec((1, SLOTS, 1), lambda i, h: (i, 0, 0))
    heads_packed = pl.pallas_call(
        attend_kernel,
        grid=(rows, HEADS_KV),
        in_specs=[q_spec, limit_spec, pos_spec] + [kv_spec] * 2,
        out_specs=q_spec,
        out_shape=jax.ShapeDtypeStruct(packed, bf16),
        scratch_shapes=[pltpu.VMEM((SLOTS, LANES), bf16), pltpu.VMEM((LANES, SLOTS), bf16)],
        compiler_params=params(2),
        cost_estimate=SMALL,
        name="attend",
    )(queries, limit, key_pos, *kv_halves)

    heads_shape = (n_tensor, sp_rows, q_cols)
    head_spec = pl.BlockSpec((1, sp_rows, q_cols), lambda s: (s, 0, 0))
    square = whole((sp_rows, width))
    mixed, h_two_own, attn_heads = pl.pallas_call(
        out_kernel,
        grid=(n_tensor,),
        in_specs=[
            part_spec,
            *half_specs,
            square,
            whole((sp_rows, 1)),
            whole((1, width)),
        ],
        out_specs=(square, square, head_spec),
        out_shape=(
            jax.ShapeDtypeStruct((sp_rows, width), f32),
            jax.ShapeDtypeStruct((sp_rows, width), bf16),
            jax.ShapeDtypeStruct(heads_shape, bf16),
        ),
        compiler_params=params(),
        cost_estimate=SMALL,
        name="out",
    )(heads_packed, *t_out.halves, inputs, live, gain_two[None])
    t_heads = TensorExchange(attn_heads)

    t_h_two = TensorGather(h_two_own)
    t_h_one = TensorGather(h_one)
    rows_all = sp_rows * n_tensor
    link.go(g_ff[1], g_ff[2], g_ff[3], during=[h_two_own], ends=[t_d_ffn.stack])
    link.go(t_h_two, t_d_ffn, g_ff[2], g_ff[3], g_ff[4])
    d_ffn = t_d_ffn.rows()
    link.go(t_h_two, t_h_one, g_ff[3], g_ff[4], g_ff[5])
    h_two = t_h_two.rows()
    steps = n_tensor // 2
    row_block = lambda span: pl.BlockSpec((rows_all // steps, span), lambda i: (i, 0))
    low_rows = pl.BlockSpec((sp_rows, width), lambda i: (jnp.minimum(i, n_tensor // 2 - 1), 0))
    high_rows = pl.BlockSpec((sp_rows, width), lambda i: (jnp.maximum(i - n_tensor // 2, 0), 0))
    weights, hiddens, d_gate_ups, turned = [], [], [], []

    def hidden_part(g, part):
        pieces = [
            (x.reshape(len(rs) * cols, 3 * part), [order.index(r) for r in rs])
            for x, rs in g.pieces()
        ]
        weights.append(pieces)
        hidden, d_gate_up, flipped = pl.pallas_call(
            functools.partial(hidden_kernel, [places for _, places in pieces]),
            grid=(n_tensor,),
            in_specs=[low_rows, high_rows] * 2 + [whole(x.shape) for x, _ in pieces],
            out_specs=(
                pl.BlockSpec((sp_rows, part), lambda i: (i, 0)),
                pl.BlockSpec((sp_rows, 2 * part), lambda i: (i, 0)),
                pl.BlockSpec((3 * part, sp_rows), lambda i: (0, i)),
            ),
            out_shape=(
                jax.ShapeDtypeStruct((rows_all, part), bf16),
                jax.ShapeDtypeStruct((rows_all, 2 * part), bf16),
                jax.ShapeDtypeStruct((3 * part, rows_all), bf16),
            ),
            compiler_params=params(),
            cost_estimate=SMALL,
        name="hidden",
        )(*h_two, *d_ffn, *[x for x, _ in pieces])
        hiddens.append(hidden)
        d_gate_ups.append(d_gate_up)
        turned.append(flipped)

    def split_places(halves, wide):
        if cols == 256:
            return halves
        return [
            x.reshape(-1, wide, 256 // cols, cols).transpose(0, 2, 1, 3).reshape(n // 2, wide, cols)
            for x in halves
        ]

    def grads_of(flipped):
        wide = flipped.shape[0]
        count = width // 256
        grid = width // 512
        low_spec = pl.BlockSpec((2, wide, 256), lambda j: (jnp.minimum(j, grid // 2 - 1), 0, 0))
        high_spec = pl.BlockSpec((2, wide, 256), lambda j: (jnp.maximum(j - grid // 2, 0), 0, 0))
        block = pl.BlockSpec((rows_all // 2, 512), lambda j: (0, j))
        halves = pl.pallas_call(
            grads_kernel,
            grid=(grid,),
            in_specs=[block] * 4 + [whole(flipped.shape)],
            out_specs=(low_spec, high_spec),
            out_shape=[jax.ShapeDtypeStruct((count // 2, wide, 256), bf16)] * 2,
            compiler_params=params(),
            cost_estimate=SMALL,
            name="weight_grads",
        )(*h_two, *d_ffn, flipped)
        halves = split_places(halves, wide)

        def make(begin, end, arrived, kind):
            if begin >= n // 2:
                return halves[1]
            return plus(halves[0][begin:end].astype(f32), arrived, kind)

        lows.append(halves[0])
        return Scatter(make), halves[1]

    s_ff, sent, lows = [], [], []

    def add_grads(c):
        item, first = grads_of(after(turned[c], *link.done) if c > 2 else turned[c])
        s_ff.append(item)
        sent.append(first)

    def back_sum(parts, down, pieces):
        span = rows_all // pieces
        def weight_spec(x, w):
            span = x.shape[1]
            at = (w.shape[1] - span) // span if down else 0
            return pl.BlockSpec(
                (w.shape[0], span), lambda i: (0, at), pipeline_mode=pl.Buffered(1)
            )

        return pl.pallas_call(
            functools.partial(
                back_sum_kernel, [[places for _, places in pieces] for pieces in weights]
            ),
            grid=(steps,),
            in_specs=[row_block(x.shape[1]) for x in parts]
            + [weight_spec(x, w) for x, pieces in zip(parts, weights) for w, _ in pieces],
            out_specs=[whole((span, width))] * pieces,
            out_shape=[jax.ShapeDtypeStruct((span, width), bf16)] * pieces,
            compiler_params=params(),
            cost_estimate=SMALL,
            name="back_sum",
        )(*parts, *[w for pieces in weights for w, _ in pieces])

    hidden_part(g_ff[0], sizes[0])
    hidden_part(g_ff[1], sizes[1])
    hidden_part(g_ff[2], sizes[2])
    add_grads(0)
    link.go(t_h_one, t_heads, g_ff[4], g_ff[5], during=[*turned, *sent])
    h_one_all = t_h_one.rows()
    hidden_part(g_ff[3], sizes[3])
    hidden_part(g_ff[4], sizes[4])
    add_grads(1)
    add_grads(2)
    link.go(t_heads, s_ff[0], g_ff[5], during=[*turned[3:], *sent[1:]])
    hidden_part(g_ff[5], sizes[5])
    t_back = TensorDirect(back_sum(d_gate_ups, False, n_tensor))
    link.go(s_ff[1], s_ff[0], during=t_back.parts)
    add_grads(3)
    add_grads(4)
    t_ffn = TensorScatter(
        [x.reshape(n_tensor // 2, sp_rows, width) for x in back_sum(hiddens, True, 2)]
    )
    link.go(t_back, s_ff[2], s_ff[1], during=[*t_ffn.sums, *sent[3:]])
    first_spec = pl.BlockSpec((1, sp_rows, width), lambda i: (0, 0, 0))
    back_terms = t_back.terms()
    d_mixed, d_attn_own, d_gain_two = pl.pallas_call(
        mixed_back_kernel,
        grid=(1,),
        in_specs=[square, square, whole((1, width)), whole((sp_rows, 1))]
        + [first_spec] * len(back_terms),
        out_specs=(square, square, whole((1, width))),
        out_shape=(
            jax.ShapeDtypeStruct((sp_rows, width), f32),
            jax.ShapeDtypeStruct((sp_rows, width), bf16),
            jax.ShapeDtypeStruct((1, width), f32),
        ),
        compiler_params=params(),
        cost_estimate=SMALL,
        name="mixed_back",
    )(mixed, cotangent, gain_two[None], live, *back_terms)

    d_heads = pl.pallas_call(
        heads_back_kernel,
        grid=(n_tensor,),
        in_specs=[whole((sp_rows, width)), *half_specs],
        out_specs=part_spec,
        out_shape=jax.ShapeDtypeStruct(packed, bf16),
        compiler_params=params(),
        cost_estimate=SMALL,
        name="heads_back",
    )(d_attn_own, *t_out.halves)
    def attend_back(first, count, grads, *held):
        shift = lambda spec: pl.BlockSpec(
            spec.block_shape, lambda i, h: spec.index_map(i, h + first)
        )
        q_part, kv_part = shift(q_spec), shift(kv_spec)
        return pl.pallas_call(
            attend_back_kernel,
            grid=(rows, count),
            in_specs=[q_part, q_part, limit_spec, pos_spec]
            + [kv_part] * 2
            + [pl.BlockSpec(memory_space=pl.ANY)] * len(held),
            out_specs=[q_part] + [kv_part] * 2,
            out_shape=[jax.ShapeDtypeStruct(packed, f32)]
            + [jax.ShapeDtypeStruct((n // 2,) + packed_kv, bf16)] * 2,
            scratch_shapes=[
                pltpu.VMEM((SLOTS, LANES), bf16),
                pltpu.VMEM((LANES, SLOTS), bf16),
                pltpu.VMEM((SLOTS, LANES), f32),
            ],
            input_output_aliases={6 + i: i for i in range(len(held))},
            compiler_params=params(2),
            cost_estimate=SMALL,
            name="attend_back",
        )(queries, grads, limit, key_pos, *kv_halves, *held)

    held = attend_back(0, 3, d_heads)
    t_attn = TensorGather(d_attn_own)
    link.go(t_ffn, s_ff[3], s_ff[2], s_ff[0], s_ff[1], during=held)
    d_query, d_low, d_high = attend_back(3, HEADS_KV - 3, after(d_heads, *link.done), *held)

    def key_grads(begin, end, arrived, kind):
        if begin >= n // 2:
            return d_high
        return plus(d_low[begin:end].astype(f32), arrived, kind)

    s_keys = Scatter(key_grads)
    d_q_low, d_q_gain = pl.pallas_call(
        query_back_kernel,
        grid=(n_tensor,),
        in_specs=[part_spec, head_spec, whole(one_head), whole(one_head), whole((1, HEAD))],
        out_specs=(head_spec, whole((1, HEAD))),
        out_shape=(
            jax.ShapeDtypeStruct(heads_shape, bf16),
            jax.ShapeDtypeStruct((1, HEAD), f32),
        ),
        compiler_params=params(),
        cost_estimate=SMALL,
        name="query_back",
    )(d_query, q_raw, cos, sin, q_gain)

    def product(left, right):
        wide = right.shape[1]
        count = width // 256
        grid = width // 512
        halves = pl.pallas_call(
            product_kernel,
            grid=(grid,),
            in_specs=[pl.BlockSpec((rows_all // 2, 512), lambda j: (0, j))] * 2
            + [whole(right.shape)],
            out_specs=(
                pl.BlockSpec((2, wide, 256), lambda j: (jnp.minimum(j, grid // 2 - 1), 0, 0)),
                pl.BlockSpec((2, wide, 256), lambda j: (jnp.maximum(j - grid // 2, 0), 0, 0)),
            ),
            out_shape=[jax.ShapeDtypeStruct((count // 2, wide, 256), bf16)] * 2,
            scratch_shapes=[pltpu.VMEM((wide, rows_all), bf16)],
            compiler_params=params(),
            cost_estimate=SMALL,
            name="product",
        )(*left, right)
        return split_places(halves, wide)

    def sum_of(halves):
        def make(begin, end, arrived, kind):
            if begin >= n // 2:
                return halves[1]
            return plus(halves[0][begin:end].astype(f32), arrived, kind)

        return Scatter(make)

    t_query_back = TensorExchange(d_q_low)
    link.go(t_attn, s_ff[4], s_ff[3], s_ff[2], during=[d_q_low])
    add_grads(5)
    link.go(t_attn, t_query_back, s_keys, s_ff[4], s_ff[3], during=[sent[5]])
    d_attn = t_attn.rows()
    out_halves = product(d_attn, t_heads.rows())
    link.go(t_query_back, s_keys, s_ff[5], s_ff[4], during=out_halves)
    s_out = sum_of(out_halves)
    link.go(s_keys, s_out, s_ff[5], t_ffn)
    d_kv = s_keys.result()
    query_halves = product(h_one_all, after(t_query_back.rows(), d_kv))
    s_query = sum_of(query_halves)
    d_kv_low, d_k_gain = pl.pallas_call(
        key_back_kernel,
        out_shape=(
            jax.ShapeDtypeStruct((sp_rows, kv_cols), bf16),
            jax.ShapeDtypeStruct((1, HEAD), f32),
        ),
        compiler_params=pltpu.CompilerParams(vmem_limit_bytes=VMEM_LIMIT),
        cost_estimate=SMALL,
        name="key_value_back",
    )(d_kv, kv_raw, cos, sin, k_gain)
    kv_part = kv_cols // n_tensor
    t_kv_back = Direct(
        [
            lax.dynamic_slice_in_dim(d_kv_low, (tensor ^ s) * kv_part, kv_part, axis=1)
            for s in tensor_order
        ]
    )
    grad_rel, d_gain_one = pl.pallas_call(
        back_kernel,
        grid=(n_tensor,),
        in_specs=[
            head_spec,
            both_spec,
            whole((sp_rows, kv_cols)),
            whole((width, kv_cols)),
            square,
            whole((1, width)),
            square,
        ],
        out_specs=(square, whole((1, width))),
        out_shape=(
            jax.ShapeDtypeStruct((sp_rows, width), bf16),
            jax.ShapeDtypeStruct((1, width), f32),
        ),
        scratch_shapes=[pltpu.VMEM((sp_rows, width), f32)],
        compiler_params=params(),
        cost_estimate=SMALL,
        name="h_one_back",
    )(d_q_low, query_all, d_kv_low, kv_all, inputs, gain_one[None], d_mixed)
    def collect(first, last, *held):
        terms = [[lows[c], *s_ff[c].raw] for c in range(first, last)]
        flat = [x for group in terms for x in group]
        if not held:
            flat[0] = after(flat[0], grad_rel)
        return pl.pallas_call(
            functools.partial(collect_kernel, len(terms), len(terms[0])),
            grid=(len(terms),),
            in_specs=[pl.BlockSpec((1,) + x.shape[1:], lambda i: (0, 0, 0)) for x in flat]
            + [pl.BlockSpec(memory_space=pl.ANY)] * len(held),
            out_specs=(
                pl.BlockSpec((cols, 2, unit), lambda i: (0, 0, first + i)),
                pl.BlockSpec((unit, cols), lambda i: (first + i, 0)),
            ),
            out_shape=(
                jax.ShapeDtypeStruct((cols, 2, ff), f32),
                jax.ShapeDtypeStruct((ff, cols), f32),
            ),
            input_output_aliases={len(flat) + i: i for i in range(len(held))},
            compiler_params=params(),
            cost_estimate=SMALL,
            name="collect",
        )(*flat, *held)

    early_sums = collect(0, FF_LAST)
    link.done += [*query_halves, *early_sums, grad_rel]
    ffn_terms = t_ffn.terms()
    outputs = pl.pallas_call(
        functools.partial(finish_kernel, tuple(order)),
        grid=(1,),
        in_specs=[smem, square, whole((sp_rows, 1))] + [first_spec] * len(ffn_terms),
        out_specs=square,
        out_shape=low_square,
        compiler_params=params(),
        cost_estimate=SMALL,
        name="finish",
    )(index, mixed, live, *ffn_terms)
    link.go(t_kv_back, s_out, s_query, during=[outputs])
    grad_inputs = call(
        functools.partial(leave_kernel, tuple(order)),
        low_square,
        "leave",
        index,
        grad_rel,
        specs=[smem, vmem],
    )

    gain_parts = jnp.concatenate([d_gain_one, d_gain_two]).reshape(2, n, cols).transpose(1, 0, 2)
    head_rows = max(2 * HEAD // cols, 1)
    head_parts = jnp.concatenate([d_q_gain, d_k_gain]).reshape(1, -1)
    head_parts = jnp.pad(head_parts, ((0, 0), (0, head_rows * cols - 2 * HEAD)))
    head_parts = jnp.broadcast_to(head_parts.reshape(1, head_rows, cols), (n, head_rows, cols))
    small_parts = jnp.concatenate([gain_parts, head_parts], axis=1)
    kv_halves_back = product(h_one_all, t_kv_back.rows())

    def with_small(side):
        begin = side * n // 2
        small_here = small_parts[begin : begin + n // 2].astype(bf16)
        return jnp.concatenate([kv_halves_back[side], small_here], axis=1)

    s_kv = ScatterSoon(with_small(0), with_small(1))
    link.go(s_kv, s_query, s_out, s_ff[5])
    sum_in, sum_down = collect(FF_LAST, len(sizes), *early_sums)
    link.go(s_kv, s_query, during=[sum_in, sum_down])
    t_sums = TensorAll(s_kv.result().astype(bf16))
    link.go(t_sums)
    stack = t_sums.stack
    small = jnp.sum(stack[:, kv_part:].astype(f32), axis=0)
    stack = stack[:, :kv_part]
    sum_gains = small[:2]
    sum_heads = small[2:].reshape(-1)[: 2 * HEAD].reshape(2, HEAD)
    places = [
        sum((((tensor ^ i) // mask) & 1) << k for k, mask in enumerate(masks_of("tensor")))
        for i in range(n_tensor)
    ]
    sum_kv = jnp.concatenate(
        [
            lax.dynamic_index_in_dim(stack, places[i], axis=0, keepdims=False)
            for i in range(n_tensor)
        ],
        axis=0,
    ).T.astype(f32)
    sum_out = s_out.result()
    sum_query = s_query.result().T
    return (
        outputs,
        grad_inputs,
        sum_query,
        sum_kv.astype(f32),
        sum_out,
        sum_in,
        sum_down,
        sum_gains,
        sum_heads,
    )


def solution(mesh):
    in_specs = (
        P(("dp", "tensor"), None),
        P(("dp", "tensor"), None),
        P("dp", "tensor"),
        P("dp", None),
        P("tensor", "dp"),
        P("dp", None, "tensor"),
        P("tensor", "dp"),
        P(None, "dp"),
        P(),
        P(),
        P(),
    )
    out_specs = (
        P(("dp", "tensor"), None),
        P(("dp", "tensor"), None),
        P("dp", "tensor"),
        P("dp", None),
        P("tensor", "dp"),
        P("dp", None, "tensor"),
        P("tensor", "dp"),
        P(None, "dp"),
        P(),
    )
    return jax.shard_map(local, mesh=mesh, in_specs=in_specs, out_specs=out_specs, check_vma=False)
```

```python
import functools

import jax
import jax.numpy as jnp
from jax import lax
from jax.experimental import layout
from jax.experimental import pallas as pl
from jax.experimental.pallas import tpu as pltpu
from jax.sharding import PartitionSpec as P

HEADS_KV = 5
HEAD = 64
SLOTS = 2048
STRETCH = 64
LANES = 128
FF_PARTS = (1, 1, 1, 1, 1, 1)
FF_LAST = len(FF_PARTS) - 1
VMEM_LIMIT = 48 * 1024 * 1024
SMALL = pl.CostEstimate(flops=1000, bytes_accessed=1000, transcendentals=0)

eps_norm = 1e-06
rope_base = 10000.0
neg_large = -1e30
f32 = jnp.float32
bf16 = jnp.bfloat16
contract_rows = (((0,), (0,)), ((), ()))
contract_cols = (((1,), (1,)), ((), ()))


def dot(a, b, dims=(((1,), (0,)), ((), ()))):
    return lax.dot_general(a, b, dims, preferred_element_type=f32)


def after(value, *deps):
    return lax.optimization_barrier((value, *deps))[0]


def masks_of(axis):
    size = lax.axis_size(axis)
    bits = [1 << i for i in range(1, size.bit_length() - 1)]
    return bits + [1]


def order_of(axis):
    order = [0]
    for mask in masks_of(axis):
        order = order + [r ^ mask for r in order]
    return order


def swap(value, axis, mask):
    size = lax.axis_size(axis)
    return lax.ppermute(value, axis, [(i, i ^ mask) for i in range(size)])


def join(first, second):
    both = jnp.concatenate([first, second], axis=0)
    return layout.with_layout_constraint(both, layout.Layout(tuple(range(both.ndim))))


def gather(value, axis):
    stack = value[None]
    for mask in masks_of(axis):
        stack = join(stack, swap(stack, axis, mask))
    return stack


def gather_rows(value, axis):
    index = lax.axis_index(axis)
    stack = value
    size = lax.axis_size(axis)
    bit = size // 2
    at = value.ndim - 2
    while bit:
        other = swap(stack, axis, bit)
        upper = (index & bit) != 0
        stack = jnp.stack(
            [jnp.where(upper, other, stack), jnp.where(upper, stack, other)], axis=at
        )
        bit //= 2
        at += 1
    return stack.reshape(value.shape[:-2] + (size,) + value.shape[-2:])


def scatter(make, axis):
    half = lax.axis_size(axis)
    arrived = []
    for mask in reversed(masks_of(axis)):
        half //= 2
        sent = make(half, 2 * half, [x[half : 2 * half] for x in arrived], bf16)
        arrived = [x[:half] for x in arrived] + [swap(sent, axis, mask)]
    return make(0, 1, arrived, f32)[0]


def phases():
    masks = masks_of("dp")
    return [masks[:1], masks[1:-1], masks[-1:]]


class Item:
    late = ()

    def bring(self, value, axis, mask):
        got = swap(value, axis, mask)
        return after(got, *self.late) if self.late else got


class Gather(Item):
    def __init__(self, value):
        self.stack, self.halves, self.phase = value[None], None, 0

    def value(self):
        return self.stack

    def advance(self, value):
        for mask in phases()[self.phase]:
            got = self.bring(value, "dp", mask)
            self.halves = (value, got)
            value = join(value, got)
        self.stack = value
        self.phase += 1
        return got

    def pieces(self):
        half = order_of("dp")[: lax.axis_size("dp") // 2]
        return [(x, [r ^ m for r in half]) for x, m in zip(self.halves, (0, masks_of("dp")[-1]))]


class GatherSoon(Item):
    def __init__(self, value):
        self.stack, self.phase = value[None], 0

    def value(self):
        return self.stack

    def advance(self, value):
        order = order_of("dp")
        if self.phase:
            got = [self.bring(value, "dp", masks_of("dp")[-1])]
        else:
            got = [self.bring(value, "dp", r) for r in order[1 : len(order) // 2]]
        both = jnp.concatenate([value, *got], axis=0)
        self.stack = layout.with_layout_constraint(both, layout.Layout(tuple(range(both.ndim))))
        self.phase += 1
        return got


class ScatterSoon(Item):
    def __init__(self, low, high):
        self.low, self.high, self.phase = low, high, 0

    def value(self):
        if self.phase == 0:
            return self.high
        self.total = self.low.astype(f32) + self.first.astype(f32)
        return self.total[1:].astype(bf16)

    def advance(self, value):
        order = order_of("dp")
        self.phase += 1
        if self.phase == 1:
            self.first = self.bring(value, "dp", order[len(order) // 2])
            return self.first
        self.rest = [
            self.bring(value[p - 1], "dp", order[p]) for p in range(1, len(order) // 2)
        ]
        return self.rest

    def result(self):
        return self.total[0] + sum(x.astype(f32) for x in self.rest)


class TensorAll(Item):
    def __init__(self, value):
        self.own = value

    def value(self):
        return self.own

    def advance(self, value):
        got = [self.bring(value, "tensor", r) for r in order_of("tensor")[1:]]
        self.stack = jnp.stack([value, *got])
        return got


class GatherLate(Item):
    def __init__(self, value):
        self.parts, self.phase = [(value[None], [0])], 0

    def value(self):
        return self.parts[max(self.phase - 2, 0)][0]

    def advance(self, value):
        masks = masks_of("dp")
        masks = [masks[-1:], masks[:1], masks[1:-1], masks[1:-1]][self.phase]
        at = max(self.phase - 2, 0)
        places = self.parts[at][1]
        for mask in masks:
            got = self.bring(value, "dp", mask)
            halves = [(value, places), (got, [r ^ mask for r in places])]
            places = places + halves[1][1]
            if mask != masks[-1] or self.phase == 0:
                value = join(value, got)
        if self.phase == 0:
            self.parts = [(value, places)]
        elif self.phase == 1:
            self.parts = halves
        elif self.phase == 2:
            self.parts, self.first = [None, self.parts[1]], halves
        else:
            self.parts = self.first + halves
        self.phase += 1
        return got

    def pieces(self):
        return self.parts


class Scatter(Item):
    def __init__(self, make):
        self.make, self.half, self.arrived, self.phase = make, lax.axis_size("dp"), [], 2
        self.raw = []

    def value(self):
        half = self.half // 2
        return self.make(half, 2 * half, [x[half : 2 * half] for x in self.arrived], bf16)

    def advance(self, value):
        for k, mask in enumerate(reversed(phases()[self.phase])):
            if k:
                value = self.value()
            self.half //= 2
            got = self.bring(value, "dp", mask)
            self.arrived = [x[: self.half] for x in self.arrived] + [got]
            self.raw.append(got)
        self.phase -= 1
        return got

    def result(self):
        return self.make(0, 1, self.arrived, f32)[0]


class TensorGather(Item):
    def __init__(self, value):
        self.stack, self.masks = value[None], masks_of("tensor")

    def value(self):
        return self.stack

    def advance(self, value):
        got = self.bring(value, "tensor", self.masks[0])
        self.halves = (value, got)
        self.stack, self.masks = join(value, got), self.masks[1:]
        return got

    def rows(self):
        return [x.reshape(-1, x.shape[-1]) for x in self.halves]


class PairRows(Item):
    def __init__(self, value):
        self.stack = value

    def value(self):
        return self.stack

    def advance(self, value):
        got = self.bring(value, "tensor", 1)
        upper = (lax.axis_index("tensor") & 1) != 0
        self.stack = jnp.stack(
            [jnp.where(upper, got, value), jnp.where(upper, value, got)], axis=value.ndim - 2
        )
        return got


class TensorScatter(Item):
    def __init__(self, sums):
        self.sums, self.masks, self.arrived = sums, masks_of("tensor")[::-1], []

    def value(self):
        half = 1 << (len(self.masks) - 1)
        if half == self.sums[1].shape[0]:
            return self.sums[1]
        return plus(
            self.sums[0][half : 2 * half].astype(f32),
            [x[half : 2 * half] for x in self.arrived],
            bf16,
        )

    def advance(self, value):
        self.arrived.append(self.bring(value, "tensor", self.masks[0]))
        self.masks = self.masks[1:]
        return self.arrived[-1]

    def terms(self):
        return [self.sums[0], *self.arrived]


class TensorDirect(Item):
    def __init__(self, parts):
        self.parts = list(parts)

    def value(self):
        return self.parts

    def advance(self, value):
        order = order_of("tensor")
        self.got = [self.bring(value[p], "tensor", order[p]) for p in range(1, len(order))]
        return self.got

    def terms(self):
        return [x[None] for x in [self.parts[0], *self.got]]


class TensorExchange(Item):
    def __init__(self, stack):
        self.stack, self.masks = stack[:, None], masks_of("tensor")

    def value(self):
        return self.stack[1::2]

    def advance(self, value):
        got = self.bring(value, "tensor", self.masks[0])
        self.stack = jnp.concatenate([self.stack[0::2], got], axis=1)
        self.masks = self.masks[1:]
        return got

    def rows(self):
        return self.stack.reshape((-1,) + self.stack.shape[3:])


class Direct(Item):
    def __init__(self, parts):
        self.parts = parts

    def value(self):
        return jnp.stack(self.parts)

    def advance(self, value):
        order = order_of("tensor")
        got = [value[0]] + [
            self.bring(value[p], "tensor", order[p]) for p in range(1, len(order))
        ]
        self.all = jnp.concatenate(got, axis=0)
        return self.all

    def rows(self):
        return self.all


class Rounds:
    def __init__(self):
        self.done = []

    def go(self, *items, ends=(), during=()):
        done = list(ends)
        for item in items:
            value = item.value()
            if self.done:
                value = after(value, *self.done)
            item.late = during
            got = item.advance(value)
            done += got if isinstance(got, list) else [got]
        self.done = done


def plus(total, arrived, kind):
    for other in arrived:
        total = total + other.astype(f32)
    return total.astype(kind)


def scaled_norm(value_in, gain_vec):
    return (
        value_in
        * lax.rsqrt(jnp.mean(value_in * value_in, axis=-1, keepdims=True) + eps_norm)
        * gain_vec
    )


def silu_product(gate, up_part):
    return gate * jax.nn.sigmoid(gate) * up_part


def params(steps=1):
    return pltpu.CompilerParams(
        dimension_semantics=("arbitrary",) * steps, vmem_limit_bytes=VMEM_LIMIT
    )


def swap_halves(value):
    half = HEAD // 2
    return jnp.concatenate([value[:, half:], value[:, :half]], axis=1)


def rope_one(raw, gain, cos, sin, factor):
    scale = lax.rsqrt(jnp.mean(raw * raw, axis=-1, keepdims=True) + eps_norm)
    normed = raw * scale * gain
    return (normed * cos + swap_halves(normed) * sin) * factor


def rope_back(raw, gain, cos, sin, factor, grad):
    grad = grad * factor
    grad = grad * cos - swap_halves(grad) * sin
    scale = lax.rsqrt(jnp.mean(raw * raw, axis=-1, keepdims=True) + eps_norm)
    weighted = grad * gain
    back = scale * weighted - raw * (
        scale * scale * scale * jnp.mean(raw * weighted, axis=-1, keepdims=True)
    )
    return back, jnp.sum(grad * raw * scale, axis=0, keepdims=True)


def query_kernel(h_ref, w_ref, cos_ref, sin_ref, gain_ref, raw_ref, out_ref):
    cols = w_ref.shape[3]
    raw = sum(
        dot(h_ref[:, r * cols : (r + 1) * cols], w_ref[0, r], contract_cols)
        for r in range(w_ref.shape[1])
    )
    raw_ref[0] = raw
    rows, blocks = out_ref.shape[0], out_ref.shape[2]
    for h in range(HEADS_KV):
        turned = rope_one(
            raw[:, h * HEAD : (h + 1) * HEAD], gain_ref[...], cos_ref[...], sin_ref[...], 0.125
        )
        wide = jnp.concatenate([turned, jnp.zeros_like(turned)], axis=1).astype(bf16)
        out_ref[:, h, :, 0] = wide.reshape(rows, blocks, STRETCH, LANES)


def key_kernel(h_ref, w_ref, cos_ref, sin_ref, gain_ref, raw_ref, out_ref):
    raw = dot(h_ref[...], w_ref[...])
    raw_ref[...] = raw
    rows, blocks = out_ref.shape[0], out_ref.shape[2]
    for h in range(HEADS_KV):
        turned = rope_one(
            raw[:, h * HEAD : (h + 1) * HEAD], gain_ref[...], cos_ref[...], sin_ref[...], 1.0
        )
        start = (HEADS_KV + h) * HEAD
        wide = jnp.concatenate([turned, raw[:, start : start + HEAD]], axis=1).astype(bf16)
        out_ref[:, h] = wide.reshape(rows, blocks, STRETCH, LANES)


def load_keys(halves, kv, kvt):
    places = [(half, i) for half in halves for i in range(half.shape[0])]
    group = len(places) * STRETCH
    for g in range(halves[0].shape[3]):
        for r, (half, i) in enumerate(places):
            start = g * group + r * STRETCH
            kv[start : start + STRETCH, :] = half[i, 0, 0, g]
    kvt[...] = kv[...].T
    return group


def attend_kernel(q_ref, limit_ref, keypos_ref, low_ref, high_ref, out_ref, kv, kvt):
    blocks = q_ref.shape[2]
    group = load_keys((low_ref, high_ref), kv, kvt)
    for b in range(blocks):
        span = (b + 1) * group
        q = q_ref[0, 0, b].reshape(-1, LANES)
        scores = dot(kv[:span], q, contract_cols)
        scores = jnp.where(keypos_ref[0, :span] <= limit_ref[0, b], scores, neg_large)
        top = jnp.max(scores, axis=0, keepdims=True)
        weights = jnp.exp(scores - top)
        total = jnp.sum(weights, axis=0, keepdims=True)
        heads = dot(kvt[:, :span], weights.astype(bf16)) / total
        out_ref[0, 0, b] = heads.T.astype(bf16).reshape(q_ref.shape[3:])


def attend_back_kernel(q_ref, g_ref, limit_ref, keypos_ref, low_ref, high_ref, *rest):
    dq_ref, dlow_ref, dhigh_ref, kv, kvt, acc = rest[-6:]
    blocks = q_ref.shape[2]
    group = load_keys((low_ref, high_ref), kv, kvt)
    acc[...] = jnp.zeros_like(acc)
    for b in range(blocks):
        span = (b + 1) * group
        q = q_ref[0, 0, b].reshape(-1, LANES)
        grad = g_ref[0, 0, b].reshape(-1, LANES)
        scores = dot(kv[:span], q, contract_cols)
        scores = jnp.where(keypos_ref[0, :span] <= limit_ref[0, b], scores, neg_large)
        top = jnp.max(scores, axis=0, keepdims=True)
        weights = jnp.exp(scores - top)
        probs = weights * (1.0 / jnp.sum(weights, axis=0, keepdims=True))
        d_probs = dot(kv[:span], grad, contract_cols)
        delta = jnp.sum(probs * d_probs, axis=0, keepdims=True)
        d_scores = (probs * (d_probs - delta)).astype(bf16)
        dq = dot(kvt[:, :span], d_scores)
        dq_ref[0, 0, b] = dq.T.reshape(q_ref.shape[3:])
        acc[:span] += dot(d_scores, q) + dot(probs.astype(bf16), grad)
    count = dlow_ref.shape[0]
    for out, first in ((dlow_ref, 0), (dhigh_ref, count)):
        for r in range(count):
            for g in range(blocks):
                start = g * group + (first + r) * STRETCH
                out[r, 0, 0, g] = acc[start : start + STRETCH].astype(bf16)


def out_kernel(o_ref, w_low, w_high, x_ref, live_ref, gain_ref, mixed_ref, h_ref, heads_ref):
    rows = heads_ref.shape[1]
    heads = jnp.concatenate(
        [o_ref[:, h, :, 0].reshape(rows, LANES)[:, HEAD:] for h in range(HEADS_KV)], axis=1
    )
    heads_ref[0] = heads
    cols = w_low.shape[3]
    low = pl.program_id(0) < pl.num_programs(0) // 2

    @pl.when(pl.program_id(0) == 0)
    def _():
        mixed_ref[...] = jnp.zeros_like(mixed_ref)

    for r in range(w_low.shape[1]):
        here = jnp.where(low, w_low[0, r], w_high[0, r])
        mixed_ref[:, r * cols : (r + 1) * cols] += dot(heads, here)

    @pl.when(pl.program_id(0) == pl.num_programs(0) - 1)
    def _():
        mixed = x_ref[...].astype(f32) + live_ref[...] * mixed_ref[...]
        mixed_ref[...] = mixed
        h_ref[...] = scaled_norm(mixed, gain_ref[...]).astype(bf16)


def norm_back(value, gain, grad):
    scale = lax.rsqrt(jnp.mean(value * value, axis=-1, keepdims=True) + eps_norm)
    weighted = grad * gain
    inner = jnp.mean(value * weighted, axis=-1, keepdims=True)
    back = scale * weighted - value * (scale * scale * scale * inner)
    return back, jnp.sum(grad * value * scale, axis=0, keepdims=True)


def mixed_back_kernel(mixed_ref, cot_ref, gain_ref, live_ref, *rest):
    terms, (d_mixed_ref, d_attn_ref, dgain_ref) = rest[:-3], rest[-3:]
    grad = sum(ref[0].astype(f32) for ref in terms)
    back, dgain_ref[...] = norm_back(mixed_ref[...], gain_ref[...], grad)
    d_mixed = cot_ref[...].astype(f32) + back
    d_mixed_ref[...] = d_mixed
    d_attn_ref[...] = (live_ref[...] * d_mixed).astype(bf16)


def heads_back_kernel(d_ref, w_low, w_high, out_ref):
    cols = w_low.shape[3]
    low = pl.program_id(0) < pl.num_programs(0) // 2
    grad = sum(
        dot(
            d_ref[:, r * cols : (r + 1) * cols],
            jnp.where(low, w_low[0, r], w_high[0, r]),
            contract_cols,
        )
        for r in range(w_low.shape[1])
    )
    rows, blocks = out_ref.shape[0], out_ref.shape[2]
    for h in range(HEADS_KV):
        part = grad[:, h * HEAD : (h + 1) * HEAD]
        wide = jnp.concatenate([jnp.zeros_like(part), part], axis=1).astype(bf16)
        out_ref[:, h, :, 0] = wide.reshape(rows, blocks, STRETCH, LANES)


def query_back_kernel(dq_ref, raw_ref, cos_ref, sin_ref, gain_ref, out_ref, dgain_ref):
    @pl.when(pl.program_id(0) == 0)
    def _():
        dgain_ref[...] = jnp.zeros_like(dgain_ref)

    raw = raw_ref[0]
    parts = []
    for h in range(HEADS_KV):
        grad = dq_ref[:, h, :, 0].reshape(raw.shape[0], LANES)[:, :HEAD]
        back, dgain = rope_back(
            raw[:, h * HEAD : (h + 1) * HEAD],
            gain_ref[...],
            cos_ref[...],
            sin_ref[...],
            0.125,
            grad,
        )
        parts.append(back)
        dgain_ref[...] += dgain
    out_ref[0] = jnp.concatenate(parts, axis=1).astype(bf16)


def key_back_kernel(sum_ref, raw_ref, cos_ref, sin_ref, gain_ref, out_ref, dgain_ref):
    raw = raw_ref[...]
    keys, values = [], []
    total = jnp.zeros_like(dgain_ref)
    for h in range(HEADS_KV):
        both = sum_ref[:, h].reshape(raw.shape[0], LANES)
        back, dgain = rope_back(
            raw[:, h * HEAD : (h + 1) * HEAD],
            gain_ref[...],
            cos_ref[...],
            sin_ref[...],
            1.0,
            both[:, :HEAD],
        )
        keys.append(back)
        values.append(both[:, HEAD:])
        total = total + dgain
    dgain_ref[...] = total
    out_ref[...] = jnp.concatenate(keys + values, axis=1).astype(bf16)


def back_kernel(
    dq_ref, wq_ref, dkv_ref, wkv_ref, x_ref, gain_ref, d_mixed_ref, out_ref, dgain_ref, acc
):
    @pl.when(pl.program_id(0) == 0)
    def _():
        acc[...] = dot(dkv_ref[...], wkv_ref[...], contract_cols)

    cols = wq_ref.shape[3]
    for r in range(wq_ref.shape[1]):
        acc[:, r * cols : (r + 1) * cols] += dot(dq_ref[0], wq_ref[0, r])

    @pl.when(pl.program_id(0) == pl.num_programs(0) - 1)
    def _():
        back, dgain_ref[...] = norm_back(x_ref[...].astype(f32), gain_ref[...], acc[...])
        out_ref[...] = (d_mixed_ref[...] + back).astype(bf16)


def turn_kernel(x_ref, out_ref):
    out_ref[...] = x_ref[...].T


def shards_kernel(in_ref, down_ref, *parts):
    ff = down_ref.shape[0]
    start = 0
    for ref in parts:
        part = ref.shape[1] // 3
        ref[:, :part] = in_ref[:, start : start + part]
        ref[:, part : 2 * part] = in_ref[:, ff + start : ff + start + part]
        ref[:, 2 * part :] = down_ref[start : start + part, :].T
        start += part


def turn_columns(order, back, index, value):
    size = len(order)
    cols = value.shape[1] // size

    def pick(value, places):
        return jnp.concatenate([value[:, p * cols : (p + 1) * cols] for p in places], axis=1)

    if back:
        value = pick(value, [order.index(i) for i in range(size)])
    bit = 1
    while bit < size:
        value = jnp.where((index & bit) != 0, pick(value, [i ^ bit for i in range(size)]), value)
        bit *= 2
    return value if back else pick(value, order)


def enter_kernel(order, index_ref, x_ref, cot_ref, live_ref, x_out, cot_out, d_ffn_out):
    x_out[...] = turn_columns(order, False, index_ref[0], x_ref[...].astype(f32)).astype(bf16)
    cot = turn_columns(order, False, index_ref[0], cot_ref[...].astype(f32))
    cot_out[...] = cot.astype(bf16)
    d_ffn_out[...] = (cot * live_ref[...]).astype(bf16)


def leave_kernel(order, index_ref, x_ref, out_ref):
    value = x_ref[...].astype(f32)
    out_ref[...] = turn_columns(order, True, index_ref[0], value).astype(bf16)


def finish_kernel(order, index_ref, mixed_ref, live_ref, *rest):
    terms, out_ref = rest[:-1], rest[-1]
    ffn = sum(ref[0].astype(f32) for ref in terms)
    value = mixed_ref[...] + live_ref[...] * ffn
    out_ref[...] = turn_columns(order, True, index_ref[0], value).astype(bf16)


def product_kernel(left_low, left_high, right_ref, low_ref, high_ref, turned):
    @pl.when(pl.program_id(0) == 0)
    def _():
        turned[...] = right_ref[...].T

    out = halves_product(turned[...], left_low, left_high).astype(bf16)
    low = pl.program_id(0) < pl.num_programs(0) // 2
    span = low_ref.shape[2]
    for out_ref, here in ((low_ref, low), (high_ref, jnp.logical_not(low))):

        @pl.when(here)
        def _(out_ref=out_ref):
            for p in range(out_ref.shape[0]):
                out_ref[p] = out[:, p * span : (p + 1) * span]


def pick_columns(value, places, cols):
    if places == list(range(places[0], places[0] + len(places))):
        return value[:, places[0] * cols : (places[-1] + 1) * cols]
    return jnp.concatenate([value[:, p * cols : (p + 1) * cols] for p in places], axis=1)


def hidden_kernel(all_places, h_low, h_high, d_low, d_high, *refs):
    pieces, (hidden_ref, d_gate_up_ref, turned_ref) = refs[:-3], refs[-3:]
    part = hidden_ref.shape[1]
    low = pl.program_id(0) < pl.num_programs(0) // 2
    h = jnp.where(low, h_low[...], h_high[...])
    d = jnp.where(low, d_low[...], d_high[...])
    gate_up = d_hidden = None
    for places, ref in zip(all_places, pieces):
        cols = ref.shape[0] // len(places)
        first = dot(pick_columns(h, places, cols), ref[:, : 2 * part])
        second = dot(pick_columns(d, places, cols), ref[:, 2 * part :])
        gate_up = first if gate_up is None else gate_up + first
        d_hidden = second if d_hidden is None else d_hidden + second
    gate, up = gate_up[:, :part], gate_up[:, part:]
    sig = jax.nn.sigmoid(gate)
    swish = gate * sig
    hidden = (swish * up).astype(bf16)
    d_gate = (d_hidden * up * (sig + swish * (1.0 - sig))).astype(bf16)
    d_up = (d_hidden * swish).astype(bf16)
    hidden_ref[...] = hidden
    d_gate_up_ref[:, :part] = d_gate
    d_gate_up_ref[:, part:] = d_up
    turned_ref[:part] = d_gate.T
    turned_ref[part : 2 * part] = d_up.T
    turned_ref[2 * part :] = hidden.T


def halves_product(left, low_ref, high_ref):
    middle = low_ref.shape[0]
    return dot(left[:, :middle], low_ref[...]) + dot(left[:, middle:], high_ref[...])


def grads_kernel(h_low, h_high, d_low, d_high, turned_ref, low_ref, high_ref):
    split = turned_ref.shape[0] // 3 * 2
    first = halves_product(turned_ref[:split], h_low, h_high).astype(bf16)
    second = halves_product(turned_ref[split:], d_low, d_high).astype(bf16)
    low = pl.program_id(0) < pl.num_programs(0) // 2
    span = low_ref.shape[2]
    for out_ref, here in ((low_ref, low), (high_ref, jnp.logical_not(low))):

        @pl.when(here)
        def _(out_ref=out_ref):
            for p in range(out_ref.shape[0]):
                out_ref[p, :split] = first[:, p * span : (p + 1) * span]
                out_ref[p, split:] = second[:, p * span : (p + 1) * span]


def collect_kernel(count, each, *refs):
    in_ref, down_ref = refs[-2:]
    part = down_ref.shape[0]
    for c in range(count):

        @pl.when(pl.program_id(0) == c)
        def _(c=c):
            total = sum(ref[0].astype(f32) for ref in refs[c * each : (c + 1) * each])
            in_ref[:, 0, :] = total[:part].T
            in_ref[:, 1, :] = total[part : 2 * part].T
            down_ref[...] = total[2 * part :]


def back_sum_kernel(all_places, *refs):
    count = len(all_places)
    half = refs[-1].shape[1] // 2
    totals = [None, None]
    at = count
    for c, pieces in enumerate(all_places):
        terms = [dot(refs[c][...], refs[at + i][...], contract_cols) for i in range(len(pieces))]
        at += len(pieces)
        if len(pieces) > 2:
            blocks = {}
            for places, term in zip(pieces, terms):
                cols = term.shape[1] // len(places)
                for i, p in enumerate(places):
                    blocks[p] = term[:, i * cols : (i + 1) * cols]
            middle = len(blocks) // 2
            terms = [
                jnp.concatenate([blocks[side * middle + i] for i in range(middle)], axis=1)
                for side in range(2)
            ]
        totals = [t if old is None else old + t for old, t in zip(totals, terms)]
    outs = refs[at:]
    span = outs[0].shape[0]
    rows = totals[0].shape[0]
    each = max(rows // span, 1)
    for step in range(len(outs) // each):

        @pl.when(pl.program_id(0) == step)
        def _(step=step):
            for i in range(each):
                for side in range(2):
                    block = totals[side][i * span : (i + 1) * span].astype(bf16)
                    outs[step * each + i][:, side * half : (side + 1) * half] = block


def whole(shape):
    return pl.BlockSpec(shape, lambda *_: (0,) * len(shape))


def local(
    inputs,
    cotangent,
    w_query,
    w_kv,
    w_out,
    w_in,
    w_down,
    norm_gains,
    head_gains,
    lengths,
    slot_blocks,
):
    sp_rows, width = inputs.shape
    n = lax.axis_size("dp")
    n_tensor = lax.axis_size("tensor")
    dp = lax.axis_index("dp")
    tensor = lax.axis_index("tensor")
    seq_count = lengths.shape[0]
    row_span = sp_rows * n_tensor // seq_count
    blocks = row_span // STRETCH
    rows = sp_rows // row_span
    per_row = SLOTS // STRETCH
    cols = width // n
    q_cols = w_query.shape[1]
    kv_cols = w_kv.shape[1]
    ff = w_down.shape[0]
    order = order_of("dp")
    tensor_order = order_of("tensor")
    rels = jnp.array(order, jnp.int32)

    smem = pl.BlockSpec(memory_space=pltpu.SMEM)

    def call(kernel, out_shape, name, *args, specs=None):
        return pl.pallas_call(
            kernel,
            in_specs=specs,
            out_shape=out_shape,
            compiler_params=pltpu.CompilerParams(vmem_limit_bytes=VMEM_LIMIT),
            cost_estimate=SMALL,
            name=name,
        )(*args)

    table = slot_blocks.reshape(n, n_tensor, rows, blocks)
    mine = lax.dynamic_index_in_dim(table, tensor, axis=1, keepdims=False)[dp ^ rels]
    inside = jnp.arange(STRETCH, dtype=jnp.int32)
    key_pos = (mine % per_row * STRETCH)[..., None] + inside
    own_pos = key_pos[0]
    own_len = lengths[mine[0] // per_row][..., None]
    live = (own_pos < own_len).astype(f32).reshape(sp_rows, 1)
    limit = jnp.minimum(own_pos, own_len - 1)
    limit = jnp.broadcast_to(limit[:, :, None, None, :], (rows, blocks, 1, n_tensor, STRETCH))
    limit = limit.reshape(rows, blocks, 1, n_tensor * STRETCH)
    key_pos = key_pos.transpose(1, 2, 0, 3).reshape(rows, SLOTS, 1)
    half = HEAD // 2
    frequency = rope_base ** (-2.0 * jnp.arange(half, dtype=f32) / HEAD)
    angles = own_pos.reshape(sp_rows, 1).astype(f32) * frequency
    cosine, sine = jnp.cos(angles), jnp.sin(angles)
    cos = jnp.concatenate([cosine, cosine], axis=1)
    sin = jnp.concatenate([-sine, sine], axis=1)
    head_float = head_gains.astype(f32)
    q_gain, k_gain = head_float[0:1], head_float[1:2]

    vmem = pl.BlockSpec(memory_space=pltpu.VMEM)
    index = dp.reshape(1)
    low_square = jax.ShapeDtypeStruct((sp_rows, width), bf16)
    inputs, cotangent, d_ffn_own = call(
        functools.partial(enter_kernel, tuple(order)),
        [low_square] * 3,
        "enter",
        index,
        inputs,
        cotangent,
        live,
        specs=[smem, vmem, vmem, vmem],
    )
    inputs_f = inputs.astype(f32)
    part = w_kv.shape[0] // 2
    kv_shard = lax.dynamic_slice_in_dim(w_kv, (tensor & 1) * part, part, axis=0)
    unit = ff // sum(FF_PARTS)
    sizes = [size * unit for size in FF_PARTS]
    query_shard = call(
        turn_kernel, jax.ShapeDtypeStruct((q_cols, cols), bf16), "turn", w_query, specs=[vmem]
    )
    shards = call(
        shards_kernel,
        [jax.ShapeDtypeStruct((cols, 3 * part), bf16) for part in sizes],
        "shards",
        w_in.reshape(cols, 2 * ff),
        w_down,
        specs=[vmem, vmem],
    )
    link = Rounds()
    g_kv, g_gains = GatherSoon(kv_shard), Gather(norm_gains)
    g_query, g_out = Gather(query_shard), Gather(w_out)
    g_ff = [Gather(x) for x in shards[:-1]] + [GatherLate(shards[-1])]
    link.go(g_kv, g_gains, g_query, during=[d_ffn_own, cos, sin, limit, *shards])
    link.go(g_kv, g_gains, g_query, g_out)
    t_kv = PairRows(g_kv.stack)
    link.go(t_kv, g_gains, g_query, g_out, g_ff[0])
    gains = g_gains.stack.transpose(1, 0, 2).reshape(2, width).astype(f32)
    gain_one, gain_two = gains[0], gains[1]
    h_one = scaled_norm(inputs_f, gain_one).astype(bf16)
    t_query = TensorGather(g_query.stack)
    kv_all = t_kv.stack.reshape(width, kv_cols)
    t_d_ffn = TensorGather(d_ffn_own)

    packed = (rows, HEADS_KV, blocks, n_tensor, STRETCH, LANES)
    packed_kv = (rows, HEADS_KV, blocks, STRETCH, LANES)
    both_spec = pl.BlockSpec((1, n, q_cols, cols), lambda s: (s, 0, 0, 0))
    half_specs = [
        pl.BlockSpec(
            (1, n, q_cols, cols), lambda s: (jnp.minimum(s, n_tensor // 2 - 1), 0, 0, 0)
        ),
        pl.BlockSpec(
            (1, n, q_cols, cols), lambda s: (jnp.maximum(s - n_tensor // 2, 0), 0, 0, 0)
        ),
    ]
    kv_raw, kv_own = pl.pallas_call(
        key_kernel,
        out_shape=(
            jax.ShapeDtypeStruct((sp_rows, kv_cols), f32),
            jax.ShapeDtypeStruct(packed_kv, bf16),
        ),
        compiler_params=pltpu.CompilerParams(vmem_limit_bytes=VMEM_LIMIT),
        cost_estimate=SMALL,
        name="key_value",
    )(h_one, kv_all, cos, sin, k_gain)
    g_keys = Gather(kv_own)
    link.go(t_query, g_out, g_ff[5], g_ff[0], g_keys)
    t_out = TensorGather(g_out.stack)
    link.go(t_query, t_out, g_keys, g_ff[0], g_ff[1])
    query_all = t_query.stack
    one_head = (sp_rows, HEAD)
    part_spec = pl.BlockSpec(
        (rows, HEADS_KV, blocks, 1, STRETCH, LANES), lambda s: (0, 0, 0, s, 0, 0)
    )
    q_raw, queries = pl.pallas_call(
        query_kernel,
        grid=(n_tensor,),
        in_specs=[
            whole((sp_rows, width)),
            both_spec,
            whole(one_head),
            whole(one_head),
            whole((1, HEAD)),
        ],
        out_specs=(pl.BlockSpec((1, sp_rows, q_cols), lambda s: (s, 0, 0)), part_spec),
        out_shape=(
            jax.ShapeDtypeStruct((n_tensor, sp_rows, q_cols), f32),
            jax.ShapeDtypeStruct(packed, bf16),
        ),
        compiler_params=params(),
        cost_estimate=SMALL,
        name="query",
    )(h_one, query_all, cos, sin, q_gain)
    link.go(t_out, t_d_ffn, g_keys, g_ff[1], g_ff[2], during=[queries, key_pos])
    kv_halves = g_keys.halves
    q_spec = pl.BlockSpec(
        (1, 1, blocks, n_tensor, STRETCH, LANES), lambda i, h: (i, h, 0, 0, 0, 0)
    )
    kv_spec = pl.BlockSpec(
        (n // 2, 1, 1, blocks, STRETCH, LANES), lambda i, h: (0, i, h, 0, 0, 0)
    )
    limit_spec = pl.BlockSpec(
        (1, blocks, 1, n_tensor * STRETCH), lambda i, h: (i, 0, 0, 0)
    )
    pos_spec = pl.BlockSpec((1, SLOTS, 1), lambda i, h: (i, 0, 0))
    heads_packed = pl.pallas_call(
        attend_kernel,
        grid=(rows, HEADS_KV),
        in_specs=[q_spec, limit_spec, pos_spec] + [kv_spec] * 2,
        out_specs=q_spec,
        out_shape=jax.ShapeDtypeStruct(packed, bf16),
        scratch_shapes=[pltpu.VMEM((SLOTS, LANES), bf16), pltpu.VMEM((LANES, SLOTS), bf16)],
        compiler_params=params(2),
        cost_estimate=SMALL,
        name="attend",
    )(queries, limit, key_pos, *kv_halves)

    heads_shape = (n_tensor, sp_rows, q_cols)
    head_spec = pl.BlockSpec((1, sp_rows, q_cols), lambda s: (s, 0, 0))
    square = whole((sp_rows, width))
    mixed, h_two_own, attn_heads = pl.pallas_call(
        out_kernel,
        grid=(n_tensor,),
        in_specs=[
            part_spec,
            *half_specs,
            square,
            whole((sp_rows, 1)),
            whole((1, width)),
        ],
        out_specs=(square, square, head_spec),
        out_shape=(
            jax.ShapeDtypeStruct((sp_rows, width), f32),
            jax.ShapeDtypeStruct((sp_rows, width), bf16),
            jax.ShapeDtypeStruct(heads_shape, bf16),
        ),
        compiler_params=params(),
        cost_estimate=SMALL,
        name="out",
    )(heads_packed, *t_out.halves, inputs, live, gain_two[None])
    t_heads = TensorExchange(attn_heads)

    t_h_two = TensorGather(h_two_own)
    t_h_one = TensorGather(h_one)
    rows_all = sp_rows * n_tensor
    link.go(g_ff[1], g_ff[2], g_ff[3], during=[h_two_own], ends=[t_d_ffn.stack])
    link.go(t_h_two, t_d_ffn, g_ff[2], g_ff[3], g_ff[4])
    d_ffn = t_d_ffn.rows()
    link.go(t_h_two, t_h_one, g_ff[3], g_ff[4], g_ff[5])
    h_two = t_h_two.rows()
    steps = n_tensor // 2
    row_block = lambda span: pl.BlockSpec((rows_all // steps, span), lambda i: (i, 0))
    low_rows = pl.BlockSpec((sp_rows, width), lambda i: (jnp.minimum(i, n_tensor // 2 - 1), 0))
    high_rows = pl.BlockSpec((sp_rows, width), lambda i: (jnp.maximum(i - n_tensor // 2, 0), 0))
    weights, hiddens, d_gate_ups, turned = [], [], [], []

    def hidden_part(g, part):
        pieces = [
            (x.reshape(len(rs) * cols, 3 * part), [order.index(r) for r in rs])
            for x, rs in g.pieces()
        ]
        weights.append(pieces)
        hidden, d_gate_up, flipped = pl.pallas_call(
            functools.partial(hidden_kernel, [places for _, places in pieces]),
            grid=(n_tensor,),
            in_specs=[low_rows, high_rows] * 2 + [whole(x.shape) for x, _ in pieces],
            out_specs=(
                pl.BlockSpec((sp_rows, part), lambda i: (i, 0)),
                pl.BlockSpec((sp_rows, 2 * part), lambda i: (i, 0)),
                pl.BlockSpec((3 * part, sp_rows), lambda i: (0, i)),
            ),
            out_shape=(
                jax.ShapeDtypeStruct((rows_all, part), bf16),
                jax.ShapeDtypeStruct((rows_all, 2 * part), bf16),
                jax.ShapeDtypeStruct((3 * part, rows_all), bf16),
            ),
            compiler_params=params(),
            cost_estimate=SMALL,
        name="hidden",
        )(*h_two, *d_ffn, *[x for x, _ in pieces])
        hiddens.append(hidden)
        d_gate_ups.append(d_gate_up)
        turned.append(flipped)

    def split_places(halves, wide):
        if cols == 256:
            return halves
        return [
            x.reshape(-1, wide, 256 // cols, cols).transpose(0, 2, 1, 3).reshape(n // 2, wide, cols)
            for x in halves
        ]

    def grads_of(flipped):
        wide = flipped.shape[0]
        count = width // 256
        grid = width // 512
        low_spec = pl.BlockSpec((2, wide, 256), lambda j: (jnp.minimum(j, grid // 2 - 1), 0, 0))
        high_spec = pl.BlockSpec((2, wide, 256), lambda j: (jnp.maximum(j - grid // 2, 0), 0, 0))
        block = pl.BlockSpec((rows_all // 2, 512), lambda j: (0, j))
        halves = pl.pallas_call(
            grads_kernel,
            grid=(grid,),
            in_specs=[block] * 4 + [whole(flipped.shape)],
            out_specs=(low_spec, high_spec),
            out_shape=[jax.ShapeDtypeStruct((count // 2, wide, 256), bf16)] * 2,
            compiler_params=params(),
            cost_estimate=SMALL,
            name="weight_grads",
        )(*h_two, *d_ffn, flipped)
        halves = split_places(halves, wide)

        def make(begin, end, arrived, kind):
            if begin >= n // 2:
                return halves[1]
            return plus(halves[0][begin:end].astype(f32), arrived, kind)

        lows.append(halves[0])
        return Scatter(make), halves[1]

    s_ff, sent, lows = [], [], []

    def add_grads(c):
        item, first = grads_of(after(turned[c], *link.done) if c > 2 else turned[c])
        s_ff.append(item)
        sent.append(first)

    def back_sum(parts, down, pieces):
        span = rows_all // pieces
        def weight_spec(x, w):
            span = x.shape[1]
            at = (w.shape[1] - span) // span if down else 0
            return pl.BlockSpec(
                (w.shape[0], span), lambda i: (0, at), pipeline_mode=pl.Buffered(1)
            )

        return pl.pallas_call(
            functools.partial(
                back_sum_kernel, [[places for _, places in pieces] for pieces in weights]
            ),
            grid=(steps,),
            in_specs=[row_block(x.shape[1]) for x in parts]
            + [weight_spec(x, w) for x, pieces in zip(parts, weights) for w, _ in pieces],
            out_specs=[whole((span, width))] * pieces,
            out_shape=[jax.ShapeDtypeStruct((span, width), bf16)] * pieces,
            compiler_params=params(),
            cost_estimate=SMALL,
            name="back_sum",
        )(*parts, *[w for pieces in weights for w, _ in pieces])

    hidden_part(g_ff[0], sizes[0])
    hidden_part(g_ff[1], sizes[1])
    hidden_part(g_ff[2], sizes[2])
    add_grads(0)
    link.go(t_h_one, t_heads, g_ff[4], g_ff[5], during=[*turned, *sent])
    h_one_all = t_h_one.rows()
    hidden_part(g_ff[3], sizes[3])
    hidden_part(g_ff[4], sizes[4])
    add_grads(1)
    add_grads(2)
    link.go(t_heads, s_ff[0], g_ff[5], during=[*turned[3:], *sent[1:]])
    hidden_part(g_ff[5], sizes[5])
    t_back = TensorDirect(back_sum(d_gate_ups, False, n_tensor))
    link.go(s_ff[1], s_ff[0], during=t_back.parts)
    add_grads(3)
    add_grads(4)
    t_ffn = TensorScatter(
        [x.reshape(n_tensor // 2, sp_rows, width) for x in back_sum(hiddens, True, 2)]
    )
    back_got = t_back.advance(t_back.value())
    link.go(s_ff[2], s_ff[1], during=[*t_ffn.sums, *sent[3:]], ends=back_got)
    first_spec = pl.BlockSpec((1, sp_rows, width), lambda i: (0, 0, 0))
    back_terms = t_back.terms()
    d_mixed, d_attn_own, d_gain_two = pl.pallas_call(
        mixed_back_kernel,
        grid=(1,),
        in_specs=[square, square, whole((1, width)), whole((sp_rows, 1))]
        + [first_spec] * len(back_terms),
        out_specs=(square, square, whole((1, width))),
        out_shape=(
            jax.ShapeDtypeStruct((sp_rows, width), f32),
            jax.ShapeDtypeStruct((sp_rows, width), bf16),
            jax.ShapeDtypeStruct((1, width), f32),
        ),
        compiler_params=params(),
        cost_estimate=SMALL,
        name="mixed_back",
    )(mixed, cotangent, gain_two[None], live, *back_terms)

    d_heads = pl.pallas_call(
        heads_back_kernel,
        grid=(n_tensor,),
        in_specs=[whole((sp_rows, width)), *half_specs],
        out_specs=part_spec,
        out_shape=jax.ShapeDtypeStruct(packed, bf16),
        compiler_params=params(),
        cost_estimate=SMALL,
        name="heads_back",
    )(d_attn_own, *t_out.halves)
    def attend_back(first, count, grads, *held):
        shift = lambda spec: pl.BlockSpec(
            spec.block_shape, lambda i, h: spec.index_map(i, h + first)
        )
        q_part, kv_part = shift(q_spec), shift(kv_spec)
        return pl.pallas_call(
            attend_back_kernel,
            grid=(rows, count),
            in_specs=[q_part, q_part, limit_spec, pos_spec]
            + [kv_part] * 2
            + [pl.BlockSpec(memory_space=pl.ANY)] * len(held),
            out_specs=[q_part] + [kv_part] * 2,
            out_shape=[jax.ShapeDtypeStruct(packed, f32)]
            + [jax.ShapeDtypeStruct((n // 2,) + packed_kv, bf16)] * 2,
            scratch_shapes=[
                pltpu.VMEM((SLOTS, LANES), bf16),
                pltpu.VMEM((LANES, SLOTS), bf16),
                pltpu.VMEM((SLOTS, LANES), f32),
            ],
            input_output_aliases={6 + i: i for i in range(len(held))},
            compiler_params=params(2),
            cost_estimate=SMALL,
            name="attend_back",
        )(queries, grads, limit, key_pos, *kv_halves, *held)

    held = attend_back(0, 3, d_heads)
    t_attn = TensorGather(d_attn_own)
    link.go(t_ffn, s_ff[3], s_ff[2], s_ff[0], s_ff[1], during=held)
    d_query, d_low, d_high = attend_back(3, HEADS_KV - 3, after(d_heads, *link.done), *held)

    def key_grads(begin, end, arrived, kind):
        if begin >= n // 2:
            return d_high
        return plus(d_low[begin:end].astype(f32), arrived, kind)

    s_keys = Scatter(key_grads)
    d_q_low, d_q_gain = pl.pallas_call(
        query_back_kernel,
        grid=(n_tensor,),
        in_specs=[part_spec, head_spec, whole(one_head), whole(one_head), whole((1, HEAD))],
        out_specs=(head_spec, whole((1, HEAD))),
        out_shape=(
            jax.ShapeDtypeStruct(heads_shape, bf16),
            jax.ShapeDtypeStruct((1, HEAD), f32),
        ),
        compiler_params=params(),
        cost_estimate=SMALL,
        name="query_back",
    )(d_query, q_raw, cos, sin, q_gain)

    def product(left, right):
        wide = right.shape[1]
        count = width // 256
        grid = width // 512
        halves = pl.pallas_call(
            product_kernel,
            grid=(grid,),
            in_specs=[pl.BlockSpec((rows_all // 2, 512), lambda j: (0, j))] * 2
            + [whole(right.shape)],
            out_specs=(
                pl.BlockSpec((2, wide, 256), lambda j: (jnp.minimum(j, grid // 2 - 1), 0, 0)),
                pl.BlockSpec((2, wide, 256), lambda j: (jnp.maximum(j - grid // 2, 0), 0, 0)),
            ),
            out_shape=[jax.ShapeDtypeStruct((count // 2, wide, 256), bf16)] * 2,
            scratch_shapes=[pltpu.VMEM((wide, rows_all), bf16)],
            compiler_params=params(),
            cost_estimate=SMALL,
            name="product",
        )(*left, right)
        return split_places(halves, wide)

    def sum_of(halves):
        def make(begin, end, arrived, kind):
            if begin >= n // 2:
                return halves[1]
            return plus(halves[0][begin:end].astype(f32), arrived, kind)

        return Scatter(make)

    t_query_back = TensorExchange(d_q_low)
    link.go(t_attn, s_ff[4], s_ff[3], s_ff[2], during=[d_q_low])
    add_grads(5)
    link.go(t_attn, t_query_back, s_keys, s_ff[4], s_ff[3], during=[sent[5]])
    d_attn = t_attn.rows()
    out_halves = product(d_attn, t_heads.rows())
    link.go(t_query_back, s_keys, s_ff[5], s_ff[4], during=out_halves)
    s_out = sum_of(out_halves)
    link.go(s_keys, s_out, s_ff[5], t_ffn)
    d_kv = s_keys.result()
    query_halves = product(h_one_all, after(t_query_back.rows(), d_kv))
    s_query = sum_of(query_halves)
    d_kv_low, d_k_gain = pl.pallas_call(
        key_back_kernel,
        out_shape=(
            jax.ShapeDtypeStruct((sp_rows, kv_cols), bf16),
            jax.ShapeDtypeStruct((1, HEAD), f32),
        ),
        compiler_params=pltpu.CompilerParams(vmem_limit_bytes=VMEM_LIMIT),
        cost_estimate=SMALL,
        name="key_value_back",
    )(d_kv, kv_raw, cos, sin, k_gain)
    kv_part = kv_cols // n_tensor
    t_kv_back = Direct(
        [
            lax.dynamic_slice_in_dim(d_kv_low, (tensor ^ s) * kv_part, kv_part, axis=1)
            for s in tensor_order
        ]
    )
    grad_rel, d_gain_one = pl.pallas_call(
        back_kernel,
        grid=(n_tensor,),
        in_specs=[
            head_spec,
            both_spec,
            whole((sp_rows, kv_cols)),
            whole((width, kv_cols)),
            square,
            whole((1, width)),
            square,
        ],
        out_specs=(square, whole((1, width))),
        out_shape=(
            jax.ShapeDtypeStruct((sp_rows, width), bf16),
            jax.ShapeDtypeStruct((1, width), f32),
        ),
        scratch_shapes=[pltpu.VMEM((sp_rows, width), f32)],
        compiler_params=params(),
        cost_estimate=SMALL,
        name="h_one_back",
    )(d_q_low, query_all, d_kv_low, kv_all, inputs, gain_one[None], d_mixed)
    def collect(first, last, *held):
        terms = [[lows[c], *s_ff[c].raw] for c in range(first, last)]
        flat = [x for group in terms for x in group]
        if not held:
            flat[0] = after(flat[0], grad_rel)
        return pl.pallas_call(
            functools.partial(collect_kernel, len(terms), len(terms[0])),
            grid=(len(terms),),
            in_specs=[pl.BlockSpec((1,) + x.shape[1:], lambda i: (0, 0, 0)) for x in flat]
            + [pl.BlockSpec(memory_space=pl.ANY)] * len(held),
            out_specs=(
                pl.BlockSpec((cols, 2, unit), lambda i: (0, 0, first + i)),
                pl.BlockSpec((unit, cols), lambda i: (first + i, 0)),
            ),
            out_shape=(
                jax.ShapeDtypeStruct((cols, 2, ff), f32),
                jax.ShapeDtypeStruct((ff, cols), f32),
            ),
            input_output_aliases={len(flat) + i: i for i in range(len(held))},
            compiler_params=params(),
            cost_estimate=SMALL,
            name="collect",
        )(*flat, *held)

    early_sums = collect(0, FF_LAST)
    link.done += [*query_halves, *early_sums, grad_rel]
    ffn_terms = t_ffn.terms()
    outputs = pl.pallas_call(
        functools.partial(finish_kernel, tuple(order)),
        grid=(1,),
        in_specs=[smem, square, whole((sp_rows, 1))] + [first_spec] * len(ffn_terms),
        out_specs=square,
        out_shape=low_square,
        compiler_params=params(),
        cost_estimate=SMALL,
        name="finish",
    )(index, mixed, live, *ffn_terms)
    link.go(t_kv_back, s_out, s_query, during=[outputs])
    grad_inputs = call(
        functools.partial(leave_kernel, tuple(order)),
        low_square,
        "leave",
        index,
        grad_rel,
        specs=[smem, vmem],
    )

    gain_parts = jnp.concatenate([d_gain_one, d_gain_two]).reshape(2, n, cols).transpose(1, 0, 2)
    head_rows = max(2 * HEAD // cols, 1)
    head_parts = jnp.concatenate([d_q_gain, d_k_gain]).reshape(1, -1)
    head_parts = jnp.pad(head_parts, ((0, 0), (0, head_rows * cols - 2 * HEAD)))
    head_parts = jnp.broadcast_to(head_parts.reshape(1, head_rows, cols), (n, head_rows, cols))
    small_parts = jnp.concatenate([gain_parts, head_parts], axis=1)
    kv_halves_back = product(h_one_all, t_kv_back.rows())

    def with_small(side):
        begin = side * n // 2
        small_here = small_parts[begin : begin + n // 2].astype(bf16)
        return jnp.concatenate([kv_halves_back[side], small_here], axis=1)

    s_kv = ScatterSoon(with_small(0), with_small(1))
    link.go(s_kv, s_query, s_out, s_ff[5])
    s_kv.advance(s_kv.value())
    t_sums = TensorAll(s_kv.result().astype(bf16))
    t_sums.advance(t_sums.value())
    sum_in, sum_down = collect(FF_LAST, len(sizes), *early_sums)
    link.go(s_query, during=[sum_in, sum_down])
    stack = t_sums.stack
    small = jnp.sum(stack[:, kv_part:].astype(f32), axis=0)
    stack = stack[:, :kv_part]
    sum_gains = small[:2]
    sum_heads = small[2:].reshape(-1)[: 2 * HEAD].reshape(2, HEAD)
    places = [
        sum((((tensor ^ i) // mask) & 1) << k for k, mask in enumerate(masks_of("tensor")))
        for i in range(n_tensor)
    ]
    sum_kv = jnp.concatenate(
        [
            lax.dynamic_index_in_dim(stack, places[i], axis=0, keepdims=False)
            for i in range(n_tensor)
        ],
        axis=0,
    ).T.astype(f32)
    sum_out = s_out.result()
    sum_query = s_query.result().T
    return (
        outputs,
        grad_inputs,
        sum_query,
        sum_kv.astype(f32),
        sum_out,
        sum_in,
        sum_down,
        sum_gains,
        sum_heads,
    )


def solution(mesh):
    in_specs = (
        P(("dp", "tensor"), None),
        P(("dp", "tensor"), None),
        P("dp", "tensor"),
        P("dp", None),
        P("tensor", "dp"),
        P("dp", None, "tensor"),
        P("tensor", "dp"),
        P(None, "dp"),
        P(),
        P(),
        P(),
    )
    out_specs = (
        P(("dp", "tensor"), None),
        P(("dp", "tensor"), None),
        P("dp", "tensor"),
        P("dp", None),
        P("tensor", "dp"),
        P("dp", None, "tensor"),
        P("tensor", "dp"),
        P(None, "dp"),
        P(),
    )
    return jax.shard_map(local, mesh=mesh, in_specs=in_specs, out_specs=out_specs, check_vma=False)
```

```python
import functools

import jax
import jax.numpy as jnp
from jax import lax
from jax.experimental import layout
from jax.experimental import pallas as pl
from jax.experimental.pallas import tpu as pltpu
from jax.sharding import PartitionSpec as P

HEADS_KV = 5
HEAD = 64
SLOTS = 2048
STRETCH = 64
LANES = 128
FF_PARTS = (1, 1, 1, 1, 1, 1)
FF_LAST = len(FF_PARTS) - 1
VMEM_LIMIT = 48 * 1024 * 1024
SMALL = pl.CostEstimate(flops=1000, bytes_accessed=1000, transcendentals=0)

eps_norm = 1e-06
rope_base = 10000.0
neg_large = -1e30
f32 = jnp.float32
bf16 = jnp.bfloat16
contract_rows = (((0,), (0,)), ((), ()))
contract_cols = (((1,), (1,)), ((), ()))


def dot(a, b, dims=(((1,), (0,)), ((), ()))):
    return lax.dot_general(a, b, dims, preferred_element_type=f32)


def after(value, *deps):
    return lax.optimization_barrier((value, *deps))[0]


def masks_of(axis):
    size = lax.axis_size(axis)
    bits = [1 << i for i in range(1, size.bit_length() - 1)]
    return bits + [1]


def order_of(axis):
    order = [0]
    for mask in masks_of(axis):
        order = order + [r ^ mask for r in order]
    return order


def swap(value, axis, mask):
    size = lax.axis_size(axis)
    return lax.ppermute(value, axis, [(i, i ^ mask) for i in range(size)])


def join(first, second):
    both = jnp.concatenate([first, second], axis=0)
    return layout.with_layout_constraint(both, layout.Layout(tuple(range(both.ndim))))


def gather(value, axis):
    stack = value[None]
    for mask in masks_of(axis):
        stack = join(stack, swap(stack, axis, mask))
    return stack


def gather_rows(value, axis):
    index = lax.axis_index(axis)
    stack = value
    size = lax.axis_size(axis)
    bit = size // 2
    at = value.ndim - 2
    while bit:
        other = swap(stack, axis, bit)
        upper = (index & bit) != 0
        stack = jnp.stack(
            [jnp.where(upper, other, stack), jnp.where(upper, stack, other)], axis=at
        )
        bit //= 2
        at += 1
    return stack.reshape(value.shape[:-2] + (size,) + value.shape[-2:])


def scatter(make, axis):
    half = lax.axis_size(axis)
    arrived = []
    for mask in reversed(masks_of(axis)):
        half //= 2
        sent = make(half, 2 * half, [x[half : 2 * half] for x in arrived], bf16)
        arrived = [x[:half] for x in arrived] + [swap(sent, axis, mask)]
    return make(0, 1, arrived, f32)[0]


def phases():
    masks = masks_of("dp")
    return [masks[:1], masks[1:-1], masks[-1:]]


class Item:
    late = ()

    def bring(self, value, axis, mask):
        got = swap(value, axis, mask)
        return after(got, *self.late) if self.late else got


class Gather(Item):
    def __init__(self, value):
        self.stack, self.halves, self.phase = value[None], None, 0

    def value(self):
        return self.stack

    def advance(self, value):
        for mask in phases()[self.phase]:
            got = self.bring(value, "dp", mask)
            self.halves = (value, got)
            value = join(value, got)
        self.stack = value
        self.phase += 1
        return got

    def pieces(self):
        half = order_of("dp")[: lax.axis_size("dp") // 2]
        return [(x, [r ^ m for r in half]) for x, m in zip(self.halves, (0, masks_of("dp")[-1]))]


class GatherSoon(Item):
    def __init__(self, value):
        self.stack, self.phase = value[None], 0

    def value(self):
        return self.stack

    def advance(self, value):
        order = order_of("dp")
        if self.phase:
            got = [self.bring(value, "dp", masks_of("dp")[-1])]
        else:
            got = [self.bring(value, "dp", r) for r in order[1 : len(order) // 2]]
        both = jnp.concatenate([value, *got], axis=0)
        self.stack = layout.with_layout_constraint(both, layout.Layout(tuple(range(both.ndim))))
        self.phase += 1
        return got


class ScatterSoon(Item):
    def __init__(self, low, high):
        self.low, self.high, self.phase = low, high, 0

    def value(self):
        if self.phase == 0:
            return self.high
        self.total = self.low.astype(f32) + self.first.astype(f32)
        return self.total[1:].astype(bf16)

    def advance(self, value):
        order = order_of("dp")
        self.phase += 1
        if self.phase == 1:
            self.first = self.bring(value, "dp", order[len(order) // 2])
            return self.first
        self.rest = [
            self.bring(value[p - 1], "dp", order[p]) for p in range(1, len(order) // 2)
        ]
        return self.rest

    def result(self):
        return self.total[0] + sum(x.astype(f32) for x in self.rest)


class TensorAll(Item):
    def __init__(self, value):
        self.own = value

    def value(self):
        return self.own

    def advance(self, value):
        got = [self.bring(value, "tensor", r) for r in order_of("tensor")[1:]]
        self.stack = jnp.stack([value, *got])
        return got


class GatherLate(Item):
    def __init__(self, value):
        self.parts, self.phase = [(value[None], [0])], 0

    def value(self):
        return self.parts[max(self.phase - 2, 0)][0]

    def advance(self, value):
        masks = masks_of("dp")
        masks = [masks[-1:], masks[:1], masks[1:-1], masks[1:-1]][self.phase]
        at = max(self.phase - 2, 0)
        places = self.parts[at][1]
        for mask in masks:
            got = self.bring(value, "dp", mask)
            halves = [(value, places), (got, [r ^ mask for r in places])]
            places = places + halves[1][1]
            if mask != masks[-1] or self.phase == 0:
                value = join(value, got)
        if self.phase == 0:
            self.parts = [(value, places)]
        elif self.phase == 1:
            self.parts = halves
        elif self.phase == 2:
            self.parts, self.first = [None, self.parts[1]], halves
        else:
            self.parts = self.first + halves
        self.phase += 1
        return got

    def pieces(self):
        return self.parts


class Scatter(Item):
    def __init__(self, make):
        self.make, self.half, self.arrived, self.phase = make, lax.axis_size("dp"), [], 2
        self.raw = []

    def value(self):
        half = self.half // 2
        return self.make(half, 2 * half, [x[half : 2 * half] for x in self.arrived], bf16)

    def advance(self, value):
        for k, mask in enumerate(reversed(phases()[self.phase])):
            if k:
                value = self.value()
            self.half //= 2
            got = self.bring(value, "dp", mask)
            self.arrived = [x[: self.half] for x in self.arrived] + [got]
            self.raw.append(got)
        self.phase -= 1
        return got

    def result(self):
        return self.make(0, 1, self.arrived, f32)[0]


class TensorGather(Item):
    def __init__(self, value):
        self.stack, self.masks = value[None], masks_of("tensor")

    def value(self):
        return self.stack

    def advance(self, value):
        got = self.bring(value, "tensor", self.masks[0])
        self.halves = (value, got)
        self.stack, self.masks = join(value, got), self.masks[1:]
        return got

    def rows(self):
        return [x.reshape(-1, x.shape[-1]) for x in self.halves]


class PairRows(Item):
    def __init__(self, value):
        self.stack = value

    def value(self):
        return self.stack

    def advance(self, value):
        got = self.bring(value, "tensor", 1)
        upper = (lax.axis_index("tensor") & 1) != 0
        self.stack = jnp.stack(
            [jnp.where(upper, got, value), jnp.where(upper, value, got)], axis=value.ndim - 2
        )
        return got


class TensorScatter(Item):
    def __init__(self, sums):
        self.sums, self.masks, self.arrived = sums, masks_of("tensor")[::-1], []

    def value(self):
        half = 1 << (len(self.masks) - 1)
        if half == self.sums[1].shape[0]:
            return self.sums[1]
        return plus(
            self.sums[0][half : 2 * half].astype(f32),
            [x[half : 2 * half] for x in self.arrived],
            bf16,
        )

    def advance(self, value):
        self.arrived.append(self.bring(value, "tensor", self.masks[0]))
        self.masks = self.masks[1:]
        return self.arrived[-1]

    def terms(self):
        return [self.sums[0], *self.arrived]


class TensorExchange(Item):
    def __init__(self, stack):
        self.stack, self.masks = stack[:, None], masks_of("tensor")

    def value(self):
        return self.stack[1::2]

    def advance(self, value):
        got = self.bring(value, "tensor", self.masks[0])
        self.stack = jnp.concatenate([self.stack[0::2], got], axis=1)
        self.masks = self.masks[1:]
        return got

    def rows(self):
        return self.stack.reshape((-1,) + self.stack.shape[3:])


class Direct(Item):
    def __init__(self, parts):
        self.parts = parts

    def value(self):
        return jnp.stack(self.parts)

    def advance(self, value):
        order = order_of("tensor")
        got = [value[0]] + [
            self.bring(value[p], "tensor", order[p]) for p in range(1, len(order))
        ]
        self.all = jnp.concatenate(got, axis=0)
        return self.all

    def rows(self):
        return self.all


class Rounds:
    def __init__(self):
        self.done = []

    def go(self, *items, ends=(), during=()):
        done = list(ends)
        for item in items:
            value = item.value()
            if self.done:
                value = after(value, *self.done)
            item.late = during
            got = item.advance(value)
            done += got if isinstance(got, list) else [got]
        self.done = done


def plus(total, arrived, kind):
    for other in arrived:
        total = total + other.astype(f32)
    return total.astype(kind)


def scaled_norm(value_in, gain_vec):
    return (
        value_in
        * lax.rsqrt(jnp.mean(value_in * value_in, axis=-1, keepdims=True) + eps_norm)
        * gain_vec
    )


def silu_product(gate, up_part):
    return gate * jax.nn.sigmoid(gate) * up_part


def params(steps=1):
    return pltpu.CompilerParams(
        dimension_semantics=("arbitrary",) * steps, vmem_limit_bytes=VMEM_LIMIT
    )


def swap_halves(value):
    half = HEAD // 2
    return jnp.concatenate([value[:, half:], value[:, :half]], axis=1)


def rope_one(raw, gain, cos, sin, factor):
    scale = lax.rsqrt(jnp.mean(raw * raw, axis=-1, keepdims=True) + eps_norm)
    normed = raw * scale * gain
    return (normed * cos + swap_halves(normed) * sin) * factor


def rope_back(raw, gain, cos, sin, factor, grad):
    grad = grad * factor
    grad = grad * cos - swap_halves(grad) * sin
    scale = lax.rsqrt(jnp.mean(raw * raw, axis=-1, keepdims=True) + eps_norm)
    weighted = grad * gain
    back = scale * weighted - raw * (
        scale * scale * scale * jnp.mean(raw * weighted, axis=-1, keepdims=True)
    )
    return back, jnp.sum(grad * raw * scale, axis=0, keepdims=True)


def query_kernel(h_ref, w_ref, cos_ref, sin_ref, gain_ref, raw_ref, out_ref):
    cols = w_ref.shape[3]
    raw = sum(
        dot(h_ref[:, r * cols : (r + 1) * cols], w_ref[0, r], contract_cols)
        for r in range(w_ref.shape[1])
    )
    raw_ref[0] = raw
    rows, blocks = out_ref.shape[0], out_ref.shape[2]
    for h in range(HEADS_KV):
        turned = rope_one(
            raw[:, h * HEAD : (h + 1) * HEAD], gain_ref[...], cos_ref[...], sin_ref[...], 0.125
        )
        wide = jnp.concatenate([turned, jnp.zeros_like(turned)], axis=1).astype(bf16)
        out_ref[:, h, :, 0] = wide.reshape(rows, blocks, STRETCH, LANES)


def key_kernel(h_ref, w_ref, cos_ref, sin_ref, gain_ref, raw_ref, out_ref):
    raw = dot(h_ref[...], w_ref[...])
    raw_ref[...] = raw
    rows, blocks = out_ref.shape[0], out_ref.shape[2]
    for h in range(HEADS_KV):
        turned = rope_one(
            raw[:, h * HEAD : (h + 1) * HEAD], gain_ref[...], cos_ref[...], sin_ref[...], 1.0
        )
        start = (HEADS_KV + h) * HEAD
        wide = jnp.concatenate([turned, raw[:, start : start + HEAD]], axis=1).astype(bf16)
        out_ref[:, h] = wide.reshape(rows, blocks, STRETCH, LANES)


def load_keys(halves, kv, kvt):
    places = [(half, i) for half in halves for i in range(half.shape[0])]
    group = len(places) * STRETCH
    for g in range(halves[0].shape[3]):
        for r, (half, i) in enumerate(places):
            start = g * group + r * STRETCH
            kv[start : start + STRETCH, :] = half[i, 0, 0, g]
    kvt[...] = kv[...].T
    return group


def attend_kernel(q_ref, limit_ref, keypos_ref, low_ref, high_ref, out_ref, kv, kvt):
    blocks = q_ref.shape[2]
    group = load_keys((low_ref, high_ref), kv, kvt)
    for b in range(blocks):
        span = (b + 1) * group
        q = q_ref[0, 0, b].reshape(-1, LANES)
        scores = dot(kv[:span], q, contract_cols)
        scores = jnp.where(keypos_ref[0, :span] <= limit_ref[0, b], scores, neg_large)
        top = jnp.max(scores, axis=0, keepdims=True)
        weights = jnp.exp(scores - top)
        total = jnp.sum(weights, axis=0, keepdims=True)
        heads = dot(kvt[:, :span], weights.astype(bf16)) / total
        out_ref[0, 0, b] = heads.T.astype(bf16).reshape(q_ref.shape[3:])


def attend_back_kernel(q_ref, g_ref, limit_ref, keypos_ref, low_ref, high_ref, *rest):
    dq_ref, dlow_ref, dhigh_ref, kv, kvt, acc = rest[-6:]
    blocks = q_ref.shape[2]
    group = load_keys((low_ref, high_ref), kv, kvt)
    acc[...] = jnp.zeros_like(acc)
    for b in range(blocks):
        span = (b + 1) * group
        q = q_ref[0, 0, b].reshape(-1, LANES)
        grad = g_ref[0, 0, b].reshape(-1, LANES)
        scores = dot(kv[:span], q, contract_cols)
        scores = jnp.where(keypos_ref[0, :span] <= limit_ref[0, b], scores, neg_large)
        top = jnp.max(scores, axis=0, keepdims=True)
        weights = jnp.exp(scores - top)
        probs = weights * (1.0 / jnp.sum(weights, axis=0, keepdims=True))
        d_probs = dot(kv[:span], grad, contract_cols)
        delta = jnp.sum(probs * d_probs, axis=0, keepdims=True)
        d_scores = (probs * (d_probs - delta)).astype(bf16)
        dq = dot(kvt[:, :span], d_scores)
        dq_ref[0, 0, b] = dq.T.reshape(q_ref.shape[3:])
        acc[:span] += dot(d_scores, q) + dot(probs.astype(bf16), grad)
    count = dlow_ref.shape[0]
    for out, first in ((dlow_ref, 0), (dhigh_ref, count)):
        for r in range(count):
            for g in range(blocks):
                start = g * group + (first + r) * STRETCH
                out[r, 0, 0, g] = acc[start : start + STRETCH].astype(bf16)


def out_kernel(o_ref, w_low, w_high, x_ref, live_ref, gain_ref, mixed_ref, h_ref, heads_ref):
    rows = heads_ref.shape[1]
    heads = jnp.concatenate(
        [o_ref[:, h, :, 0].reshape(rows, LANES)[:, HEAD:] for h in range(HEADS_KV)], axis=1
    )
    heads_ref[0] = heads
    cols = w_low.shape[3]
    low = pl.program_id(0) < pl.num_programs(0) // 2

    @pl.when(pl.program_id(0) == 0)
    def _():
        mixed_ref[...] = jnp.zeros_like(mixed_ref)

    for r in range(w_low.shape[1]):
        here = jnp.where(low, w_low[0, r], w_high[0, r])
        mixed_ref[:, r * cols : (r + 1) * cols] += dot(heads, here)

    @pl.when(pl.program_id(0) == pl.num_programs(0) - 1)
    def _():
        mixed = x_ref[...].astype(f32) + live_ref[...] * mixed_ref[...]
        mixed_ref[...] = mixed
        h_ref[...] = scaled_norm(mixed, gain_ref[...]).astype(bf16)


def norm_back(value, gain, grad):
    scale = lax.rsqrt(jnp.mean(value * value, axis=-1, keepdims=True) + eps_norm)
    weighted = grad * gain
    inner = jnp.mean(value * weighted, axis=-1, keepdims=True)
    back = scale * weighted - value * (scale * scale * scale * inner)
    return back, jnp.sum(grad * value * scale, axis=0, keepdims=True)


def mixed_back_kernel(mixed_ref, cot_ref, gain_ref, live_ref, *rest):
    terms, (d_mixed_ref, d_attn_ref, dgain_ref) = rest[:-3], rest[-3:]
    grad = sum(ref[0].astype(f32) for ref in terms)
    back, dgain_ref[...] = norm_back(mixed_ref[...], gain_ref[...], grad)
    d_mixed = cot_ref[...].astype(f32) + back
    d_mixed_ref[...] = d_mixed
    d_attn_ref[...] = (live_ref[...] * d_mixed).astype(bf16)


def heads_back_kernel(d_ref, w_low, w_high, out_ref):
    cols = w_low.shape[3]
    low = pl.program_id(0) < pl.num_programs(0) // 2
    grad = sum(
        dot(
            d_ref[:, r * cols : (r + 1) * cols],
            jnp.where(low, w_low[0, r], w_high[0, r]),
            contract_cols,
        )
        for r in range(w_low.shape[1])
    )
    rows, blocks = out_ref.shape[0], out_ref.shape[2]
    for h in range(HEADS_KV):
        part = grad[:, h * HEAD : (h + 1) * HEAD]
        wide = jnp.concatenate([jnp.zeros_like(part), part], axis=1).astype(bf16)
        out_ref[:, h, :, 0] = wide.reshape(rows, blocks, STRETCH, LANES)


def query_back_kernel(dq_ref, raw_ref, cos_ref, sin_ref, gain_ref, out_ref, dgain_ref):
    @pl.when(pl.program_id(0) == 0)
    def _():
        dgain_ref[...] = jnp.zeros_like(dgain_ref)

    raw = raw_ref[0]
    parts = []
    for h in range(HEADS_KV):
        grad = dq_ref[:, h, :, 0].reshape(raw.shape[0], LANES)[:, :HEAD]
        back, dgain = rope_back(
            raw[:, h * HEAD : (h + 1) * HEAD],
            gain_ref[...],
            cos_ref[...],
            sin_ref[...],
            0.125,
            grad,
        )
        parts.append(back)
        dgain_ref[...] += dgain
    out_ref[0] = jnp.concatenate(parts, axis=1).astype(bf16)


def key_back_kernel(sum_ref, raw_ref, cos_ref, sin_ref, gain_ref, out_ref, dgain_ref):
    raw = raw_ref[...]
    keys, values = [], []
    total = jnp.zeros_like(dgain_ref)
    for h in range(HEADS_KV):
        both = sum_ref[:, h].reshape(raw.shape[0], LANES)
        back, dgain = rope_back(
            raw[:, h * HEAD : (h + 1) * HEAD],
            gain_ref[...],
            cos_ref[...],
            sin_ref[...],
            1.0,
            both[:, :HEAD],
        )
        keys.append(back)
        values.append(both[:, HEAD:])
        total = total + dgain
    dgain_ref[...] = total
    out_ref[...] = jnp.concatenate(keys + values, axis=1).astype(bf16)


def back_kernel(
    dq_ref, wq_ref, dkv_ref, wkv_ref, x_ref, gain_ref, d_mixed_ref, out_ref, dgain_ref, acc
):
    @pl.when(pl.program_id(0) == 0)
    def _():
        acc[...] = dot(dkv_ref[...], wkv_ref[...], contract_cols)

    cols = wq_ref.shape[3]
    for r in range(wq_ref.shape[1]):
        acc[:, r * cols : (r + 1) * cols] += dot(dq_ref[0], wq_ref[0, r])

    @pl.when(pl.program_id(0) == pl.num_programs(0) - 1)
    def _():
        back, dgain_ref[...] = norm_back(x_ref[...].astype(f32), gain_ref[...], acc[...])
        out_ref[...] = (d_mixed_ref[...] + back).astype(bf16)


def turn_kernel(x_ref, out_ref):
    out_ref[...] = x_ref[...].T


def shards_kernel(in_ref, down_ref, *parts):
    ff = down_ref.shape[0]
    start = 0
    for ref in parts:
        part = ref.shape[1] // 3
        ref[:, :part] = in_ref[:, start : start + part]
        ref[:, part : 2 * part] = in_ref[:, ff + start : ff + start + part]
        ref[:, 2 * part :] = down_ref[start : start + part, :].T
        start += part


def turn_columns(order, back, index, value):
    size = len(order)
    cols = value.shape[1] // size

    def pick(value, places):
        return jnp.concatenate([value[:, p * cols : (p + 1) * cols] for p in places], axis=1)

    if back:
        value = pick(value, [order.index(i) for i in range(size)])
    bit = 1
    while bit < size:
        value = jnp.where((index & bit) != 0, pick(value, [i ^ bit for i in range(size)]), value)
        bit *= 2
    return value if back else pick(value, order)


def enter_kernel(order, index_ref, x_ref, cot_ref, live_ref, x_out, cot_out, d_ffn_out):
    x_out[...] = turn_columns(order, False, index_ref[0], x_ref[...].astype(f32)).astype(bf16)
    cot = turn_columns(order, False, index_ref[0], cot_ref[...].astype(f32))
    cot_out[...] = cot.astype(bf16)
    d_ffn_out[...] = (cot * live_ref[...]).astype(bf16)


def leave_kernel(order, index_ref, x_ref, out_ref):
    value = x_ref[...].astype(f32)
    out_ref[...] = turn_columns(order, True, index_ref[0], value).astype(bf16)


def finish_kernel(order, index_ref, mixed_ref, live_ref, *rest):
    terms, out_ref = rest[:-1], rest[-1]
    ffn = sum(ref[0].astype(f32) for ref in terms)
    value = mixed_ref[...] + live_ref[...] * ffn
    out_ref[...] = turn_columns(order, True, index_ref[0], value).astype(bf16)


def product_kernel(left_low, left_high, right_ref, low_ref, high_ref, turned):
    @pl.when(pl.program_id(0) == 0)
    def _():
        turned[...] = right_ref[...].T

    out = halves_product(turned[...], left_low, left_high).astype(bf16)
    low = pl.program_id(0) < pl.num_programs(0) // 2
    span = low_ref.shape[2]
    for out_ref, here in ((low_ref, low), (high_ref, jnp.logical_not(low))):

        @pl.when(here)
        def _(out_ref=out_ref):
            for p in range(out_ref.shape[0]):
                out_ref[p] = out[:, p * span : (p + 1) * span]


def pick_columns(value, places, cols):
    if places == list(range(places[0], places[0] + len(places))):
        return value[:, places[0] * cols : (places[-1] + 1) * cols]
    return jnp.concatenate([value[:, p * cols : (p + 1) * cols] for p in places], axis=1)


def hidden_kernel(all_places, h_low, h_high, d_low, d_high, *refs):
    pieces, (hidden_ref, d_gate_up_ref, turned_ref) = refs[:-3], refs[-3:]
    part = hidden_ref.shape[1]
    low = pl.program_id(0) < pl.num_programs(0) // 2
    h = jnp.where(low, h_low[...], h_high[...])
    d = jnp.where(low, d_low[...], d_high[...])
    gate_up = d_hidden = None
    for places, ref in zip(all_places, pieces):
        cols = ref.shape[0] // len(places)
        first = dot(pick_columns(h, places, cols), ref[:, : 2 * part])
        second = dot(pick_columns(d, places, cols), ref[:, 2 * part :])
        gate_up = first if gate_up is None else gate_up + first
        d_hidden = second if d_hidden is None else d_hidden + second
    gate, up = gate_up[:, :part], gate_up[:, part:]
    sig = jax.nn.sigmoid(gate)
    swish = gate * sig
    hidden = (swish * up).astype(bf16)
    d_gate = (d_hidden * up * (sig + swish * (1.0 - sig))).astype(bf16)
    d_up = (d_hidden * swish).astype(bf16)
    hidden_ref[...] = hidden
    d_gate_up_ref[:, :part] = d_gate
    d_gate_up_ref[:, part:] = d_up
    turned_ref[:part] = d_gate.T
    turned_ref[part : 2 * part] = d_up.T
    turned_ref[2 * part :] = hidden.T


def halves_product(left, low_ref, high_ref):
    middle = low_ref.shape[0]
    return dot(left[:, :middle], low_ref[...]) + dot(left[:, middle:], high_ref[...])


def grads_kernel(h_low, h_high, d_low, d_high, turned_ref, low_ref, high_ref):
    split = turned_ref.shape[0] // 3 * 2
    first = halves_product(turned_ref[:split], h_low, h_high).astype(bf16)
    second = halves_product(turned_ref[split:], d_low, d_high).astype(bf16)
    low = pl.program_id(0) < pl.num_programs(0) // 2
    span = low_ref.shape[2]
    for out_ref, here in ((low_ref, low), (high_ref, jnp.logical_not(low))):

        @pl.when(here)
        def _(out_ref=out_ref):
            for p in range(out_ref.shape[0]):
                out_ref[p, :split] = first[:, p * span : (p + 1) * span]
                out_ref[p, split:] = second[:, p * span : (p + 1) * span]


def collect_kernel(count, each, *refs):
    in_ref, down_ref = refs[-2:]
    part = down_ref.shape[0]
    for c in range(count):

        @pl.when(pl.program_id(0) == c)
        def _(c=c):
            total = sum(ref[0].astype(f32) for ref in refs[c * each : (c + 1) * each])
            in_ref[:, 0, :] = total[:part].T
            in_ref[:, 1, :] = total[part : 2 * part].T
            down_ref[...] = total[2 * part :]


def back_sum_kernel(all_places, *refs):
    count = len(all_places)
    half = refs[-1].shape[1] // 2
    totals = [None, None]
    at = count
    for c, pieces in enumerate(all_places):
        terms = [dot(refs[c][...], refs[at + i][...], contract_cols) for i in range(len(pieces))]
        at += len(pieces)
        if len(pieces) > 2:
            blocks = {}
            for places, term in zip(pieces, terms):
                cols = term.shape[1] // len(places)
                for i, p in enumerate(places):
                    blocks[p] = term[:, i * cols : (i + 1) * cols]
            middle = len(blocks) // 2
            terms = [
                jnp.concatenate([blocks[side * middle + i] for i in range(middle)], axis=1)
                for side in range(2)
            ]
        totals = [t if old is None else old + t for old, t in zip(totals, terms)]
    outs = refs[at:]
    span = outs[0].shape[0]
    rows = totals[0].shape[0]
    each = max(rows // span, 1)
    for step in range(len(outs) // each):

        @pl.when(pl.program_id(0) == step)
        def _(step=step):
            for i in range(each):
                for side in range(2):
                    block = totals[side][i * span : (i + 1) * span].astype(bf16)
                    outs[step * each + i][:, side * half : (side + 1) * half] = block


def whole(shape):
    return pl.BlockSpec(shape, lambda *_: (0,) * len(shape))


def local(
    inputs,
    cotangent,
    w_query,
    w_kv,
    w_out,
    w_in,
    w_down,
    norm_gains,
    head_gains,
    lengths,
    slot_blocks,
):
    sp_rows, width = inputs.shape
    n = lax.axis_size("dp")
    n_tensor = lax.axis_size("tensor")
    dp = lax.axis_index("dp")
    tensor = lax.axis_index("tensor")
    seq_count = lengths.shape[0]
    row_span = sp_rows * n_tensor // seq_count
    blocks = row_span // STRETCH
    rows = sp_rows // row_span
    per_row = SLOTS // STRETCH
    cols = width // n
    q_cols = w_query.shape[1]
    kv_cols = w_kv.shape[1]
    ff = w_down.shape[0]
    order = order_of("dp")
    tensor_order = order_of("tensor")
    rels = jnp.array(order, jnp.int32)

    smem = pl.BlockSpec(memory_space=pltpu.SMEM)

    def call(kernel, out_shape, name, *args, specs=None):
        return pl.pallas_call(
            kernel,
            in_specs=specs,
            out_shape=out_shape,
            compiler_params=pltpu.CompilerParams(vmem_limit_bytes=VMEM_LIMIT),
            cost_estimate=SMALL,
            name=name,
        )(*args)

    table = slot_blocks.reshape(n, n_tensor, rows, blocks)
    mine = lax.dynamic_index_in_dim(table, tensor, axis=1, keepdims=False)[dp ^ rels]
    inside = jnp.arange(STRETCH, dtype=jnp.int32)
    key_pos = (mine % per_row * STRETCH)[..., None] + inside
    own_pos = key_pos[0]
    own_len = lengths[mine[0] // per_row][..., None]
    live = (own_pos < own_len).astype(f32).reshape(sp_rows, 1)
    limit = jnp.minimum(own_pos, own_len - 1)
    limit = jnp.broadcast_to(limit[:, :, None, None, :], (rows, blocks, 1, n_tensor, STRETCH))
    limit = limit.reshape(rows, blocks, 1, n_tensor * STRETCH)
    key_pos = key_pos.transpose(1, 2, 0, 3).reshape(rows, SLOTS, 1)
    half = HEAD // 2
    frequency = rope_base ** (-2.0 * jnp.arange(half, dtype=f32) / HEAD)
    angles = own_pos.reshape(sp_rows, 1).astype(f32) * frequency
    cosine, sine = jnp.cos(angles), jnp.sin(angles)
    cos = jnp.concatenate([cosine, cosine], axis=1)
    sin = jnp.concatenate([-sine, sine], axis=1)
    head_float = head_gains.astype(f32)
    q_gain, k_gain = head_float[0:1], head_float[1:2]

    vmem = pl.BlockSpec(memory_space=pltpu.VMEM)
    index = dp.reshape(1)
    low_square = jax.ShapeDtypeStruct((sp_rows, width), bf16)
    inputs, cotangent, d_ffn_own = call(
        functools.partial(enter_kernel, tuple(order)),
        [low_square] * 3,
        "enter",
        index,
        inputs,
        cotangent,
        live,
        specs=[smem, vmem, vmem, vmem],
    )
    inputs_f = inputs.astype(f32)
    part = w_kv.shape[0] // 2
    kv_shard = lax.dynamic_slice_in_dim(w_kv, (tensor & 1) * part, part, axis=0)
    unit = ff // sum(FF_PARTS)
    sizes = [size * unit for size in FF_PARTS]
    query_shard = call(
        turn_kernel, jax.ShapeDtypeStruct((q_cols, cols), bf16), "turn", w_query, specs=[vmem]
    )
    shards = call(
        shards_kernel,
        [jax.ShapeDtypeStruct((cols, 3 * part), bf16) for part in sizes],
        "shards",
        w_in.reshape(cols, 2 * ff),
        w_down,
        specs=[vmem, vmem],
    )
    link = Rounds()
    g_kv, g_gains = GatherSoon(kv_shard), Gather(norm_gains)
    g_query, g_out = Gather(query_shard), Gather(w_out)
    g_ff = [Gather(x) for x in shards[:-1]] + [GatherLate(shards[-1])]
    link.go(g_kv, g_gains, g_query, during=[d_ffn_own, cos, sin, limit, *shards])
    link.go(g_kv, g_gains, g_query, g_out)
    t_kv = PairRows(g_kv.stack)
    link.go(t_kv, g_gains, g_query, g_out, g_ff[0])
    gains = g_gains.stack.transpose(1, 0, 2).reshape(2, width).astype(f32)
    gain_one, gain_two = gains[0], gains[1]
    h_one = scaled_norm(inputs_f, gain_one).astype(bf16)
    t_query = TensorGather(g_query.stack)
    kv_all = t_kv.stack.reshape(width, kv_cols)
    t_d_ffn = TensorGather(d_ffn_own)

    packed = (rows, HEADS_KV, blocks, n_tensor, STRETCH, LANES)
    packed_kv = (rows, HEADS_KV, blocks, STRETCH, LANES)
    both_spec = pl.BlockSpec((1, n, q_cols, cols), lambda s: (s, 0, 0, 0))
    half_specs = [
        pl.BlockSpec(
            (1, n, q_cols, cols), lambda s: (jnp.minimum(s, n_tensor // 2 - 1), 0, 0, 0)
        ),
        pl.BlockSpec(
            (1, n, q_cols, cols), lambda s: (jnp.maximum(s - n_tensor // 2, 0), 0, 0, 0)
        ),
    ]
    kv_raw, kv_own = pl.pallas_call(
        key_kernel,
        out_shape=(
            jax.ShapeDtypeStruct((sp_rows, kv_cols), f32),
            jax.ShapeDtypeStruct(packed_kv, bf16),
        ),
        compiler_params=pltpu.CompilerParams(vmem_limit_bytes=VMEM_LIMIT),
        cost_estimate=SMALL,
        name="key_value",
    )(h_one, kv_all, cos, sin, k_gain)
    g_keys = Gather(kv_own)
    link.go(t_query, g_out, g_ff[5], g_ff[0], g_keys)
    t_out = TensorGather(g_out.stack)
    link.go(t_query, t_out, g_keys, g_ff[0], g_ff[1])
    query_all = t_query.stack
    one_head = (sp_rows, HEAD)
    part_spec = pl.BlockSpec(
        (rows, HEADS_KV, blocks, 1, STRETCH, LANES), lambda s: (0, 0, 0, s, 0, 0)
    )
    q_raw, queries = pl.pallas_call(
        query_kernel,
        grid=(n_tensor,),
        in_specs=[
            whole((sp_rows, width)),
            both_spec,
            whole(one_head),
            whole(one_head),
            whole((1, HEAD)),
        ],
        out_specs=(pl.BlockSpec((1, sp_rows, q_cols), lambda s: (s, 0, 0)), part_spec),
        out_shape=(
            jax.ShapeDtypeStruct((n_tensor, sp_rows, q_cols), f32),
            jax.ShapeDtypeStruct(packed, bf16),
        ),
        compiler_params=params(),
        cost_estimate=SMALL,
        name="query",
    )(h_one, query_all, cos, sin, q_gain)
    link.go(t_out, t_d_ffn, g_keys, g_ff[1], g_ff[2], during=[queries, key_pos])
    kv_halves = g_keys.halves
    q_spec = pl.BlockSpec(
        (1, 1, blocks, n_tensor, STRETCH, LANES), lambda i, h: (i, h, 0, 0, 0, 0)
    )
    kv_spec = pl.BlockSpec(
        (n // 2, 1, 1, blocks, STRETCH, LANES), lambda i, h: (0, i, h, 0, 0, 0)
    )
    limit_spec = pl.BlockSpec(
        (1, blocks, 1, n_tensor * STRETCH), lambda i, h: (i, 0, 0, 0)
    )
    pos_spec = pl.BlockSpec((1, SLOTS, 1), lambda i, h: (i, 0, 0))
    heads_packed = pl.pallas_call(
        attend_kernel,
        grid=(rows, HEADS_KV),
        in_specs=[q_spec, limit_spec, pos_spec] + [kv_spec] * 2,
        out_specs=q_spec,
        out_shape=jax.ShapeDtypeStruct(packed, bf16),
        scratch_shapes=[pltpu.VMEM((SLOTS, LANES), bf16), pltpu.VMEM((LANES, SLOTS), bf16)],
        compiler_params=params(2),
        cost_estimate=SMALL,
        name="attend",
    )(queries, limit, key_pos, *kv_halves)

    heads_shape = (n_tensor, sp_rows, q_cols)
    head_spec = pl.BlockSpec((1, sp_rows, q_cols), lambda s: (s, 0, 0))
    square = whole((sp_rows, width))
    mixed, h_two_own, attn_heads = pl.pallas_call(
        out_kernel,
        grid=(n_tensor,),
        in_specs=[
            part_spec,
            *half_specs,
            square,
            whole((sp_rows, 1)),
            whole((1, width)),
        ],
        out_specs=(square, square, head_spec),
        out_shape=(
            jax.ShapeDtypeStruct((sp_rows, width), f32),
            jax.ShapeDtypeStruct((sp_rows, width), bf16),
            jax.ShapeDtypeStruct(heads_shape, bf16),
        ),
        compiler_params=params(),
        cost_estimate=SMALL,
        name="out",
    )(heads_packed, *t_out.halves, inputs, live, gain_two[None])
    t_heads = TensorExchange(attn_heads)

    t_h_two = TensorGather(h_two_own)
    t_h_one = TensorGather(h_one)
    rows_all = sp_rows * n_tensor
    link.go(g_ff[1], g_ff[2], g_ff[3], during=[h_two_own], ends=[t_d_ffn.stack])
    link.go(t_h_two, t_d_ffn, g_ff[2], g_ff[3], g_ff[4])
    d_ffn = t_d_ffn.rows()
    link.go(t_h_two, t_h_one, g_ff[3], g_ff[4], g_ff[5])
    h_two = t_h_two.rows()
    steps = n_tensor // 2
    row_block = lambda span: pl.BlockSpec((rows_all // steps, span), lambda i: (i, 0))
    low_rows = pl.BlockSpec((sp_rows, width), lambda i: (jnp.minimum(i, n_tensor // 2 - 1), 0))
    high_rows = pl.BlockSpec((sp_rows, width), lambda i: (jnp.maximum(i - n_tensor // 2, 0), 0))
    weights, hiddens, d_gate_ups, turned = [], [], [], []

    def hidden_part(g, part):
        pieces = [
            (x.reshape(len(rs) * cols, 3 * part), [order.index(r) for r in rs])
            for x, rs in g.pieces()
        ]
        weights.append(pieces)
        hidden, d_gate_up, flipped = pl.pallas_call(
            functools.partial(hidden_kernel, [places for _, places in pieces]),
            grid=(n_tensor,),
            in_specs=[low_rows, high_rows] * 2 + [whole(x.shape) for x, _ in pieces],
            out_specs=(
                pl.BlockSpec((sp_rows, part), lambda i: (i, 0)),
                pl.BlockSpec((sp_rows, 2 * part), lambda i: (i, 0)),
                pl.BlockSpec((3 * part, sp_rows), lambda i: (0, i)),
            ),
            out_shape=(
                jax.ShapeDtypeStruct((rows_all, part), bf16),
                jax.ShapeDtypeStruct((rows_all, 2 * part), bf16),
                jax.ShapeDtypeStruct((3 * part, rows_all), bf16),
            ),
            compiler_params=params(),
            cost_estimate=SMALL,
        name="hidden",
        )(*h_two, *d_ffn, *[x for x, _ in pieces])
        hiddens.append(hidden)
        d_gate_ups.append(d_gate_up)
        turned.append(flipped)

    def split_places(halves, wide):
        if cols == 256:
            return halves
        return [
            x.reshape(-1, wide, 256 // cols, cols).transpose(0, 2, 1, 3).reshape(n // 2, wide, cols)
            for x in halves
        ]

    def grads_of(flipped):
        wide = flipped.shape[0]
        count = width // 256
        grid = width // 512
        low_spec = pl.BlockSpec((2, wide, 256), lambda j: (jnp.minimum(j, grid // 2 - 1), 0, 0))
        high_spec = pl.BlockSpec((2, wide, 256), lambda j: (jnp.maximum(j - grid // 2, 0), 0, 0))
        block = pl.BlockSpec((rows_all // 2, 512), lambda j: (0, j))
        halves = pl.pallas_call(
            grads_kernel,
            grid=(grid,),
            in_specs=[block] * 4 + [whole(flipped.shape)],
            out_specs=(low_spec, high_spec),
            out_shape=[jax.ShapeDtypeStruct((count // 2, wide, 256), bf16)] * 2,
            compiler_params=params(),
            cost_estimate=SMALL,
            name="weight_grads",
        )(*h_two, *d_ffn, flipped)
        halves = split_places(halves, wide)

        def make(begin, end, arrived, kind):
            if begin >= n // 2:
                return halves[1]
            return plus(halves[0][begin:end].astype(f32), arrived, kind)

        lows.append(halves[0])
        return Scatter(make), halves[1]

    s_ff, sent, lows = [], [], []

    def add_grads(c):
        item, first = grads_of(after(turned[c], *link.done) if c > 2 else turned[c])
        s_ff.append(item)
        sent.append(first)

    def back_sum(parts, down, pieces):
        span = rows_all // pieces
        def weight_spec(x, w):
            span = x.shape[1]
            at = (w.shape[1] - span) // span if down else 0
            return pl.BlockSpec(
                (w.shape[0], span), lambda i: (0, at), pipeline_mode=pl.Buffered(1)
            )

        return pl.pallas_call(
            functools.partial(
                back_sum_kernel, [[places for _, places in pieces] for pieces in weights]
            ),
            grid=(steps,),
            in_specs=[row_block(x.shape[1]) for x in parts]
            + [weight_spec(x, w) for x, pieces in zip(parts, weights) for w, _ in pieces],
            out_specs=[whole((span, width))] * pieces,
            out_shape=[jax.ShapeDtypeStruct((span, width), bf16)] * pieces,
            compiler_params=params(),
            cost_estimate=SMALL,
            name="back_sum",
        )(*parts, *[w for pieces in weights for w, _ in pieces])

    hidden_part(g_ff[0], sizes[0])
    hidden_part(g_ff[1], sizes[1])
    hidden_part(g_ff[2], sizes[2])
    add_grads(0)
    link.go(t_h_one, t_heads, g_ff[4], g_ff[5], during=[*turned, *sent])
    h_one_all = t_h_one.rows()
    hidden_part(g_ff[3], sizes[3])
    hidden_part(g_ff[4], sizes[4])
    add_grads(1)
    add_grads(2)
    link.go(t_heads, s_ff[0], g_ff[5], during=[*turned[3:], *sent[1:]])
    hidden_part(g_ff[5], sizes[5])
    t_back = TensorScatter(
        [x.reshape(n_tensor // 2, sp_rows, width) for x in back_sum(d_gate_ups, False, 2)]
    )
    link.go(s_ff[1], s_ff[0], during=t_back.sums)
    t_back.advance(after(t_back.value(), *link.done))
    add_grads(3)
    add_grads(4)
    t_ffn = TensorScatter(
        [x.reshape(n_tensor // 2, sp_rows, width) for x in back_sum(hiddens, True, 2)]
    )
    link.go(t_back, s_ff[2], s_ff[1], during=[*t_ffn.sums, *sent[3:]])
    first_spec = pl.BlockSpec((1, sp_rows, width), lambda i: (0, 0, 0))
    back_terms = t_back.terms()
    d_mixed, d_attn_own, d_gain_two = pl.pallas_call(
        mixed_back_kernel,
        grid=(1,),
        in_specs=[square, square, whole((1, width)), whole((sp_rows, 1))]
        + [first_spec] * len(back_terms),
        out_specs=(square, square, whole((1, width))),
        out_shape=(
            jax.ShapeDtypeStruct((sp_rows, width), f32),
            jax.ShapeDtypeStruct((sp_rows, width), bf16),
            jax.ShapeDtypeStruct((1, width), f32),
        ),
        compiler_params=params(),
        cost_estimate=SMALL,
        name="mixed_back",
    )(mixed, cotangent, gain_two[None], live, *back_terms)

    d_heads = pl.pallas_call(
        heads_back_kernel,
        grid=(n_tensor,),
        in_specs=[whole((sp_rows, width)), *half_specs],
        out_specs=part_spec,
        out_shape=jax.ShapeDtypeStruct(packed, bf16),
        compiler_params=params(),
        cost_estimate=SMALL,
        name="heads_back",
    )(d_attn_own, *t_out.halves)
    def attend_back(first, count, grads, *held):
        shift = lambda spec: pl.BlockSpec(
            spec.block_shape, lambda i, h: spec.index_map(i, h + first)
        )
        q_part, kv_part = shift(q_spec), shift(kv_spec)
        return pl.pallas_call(
            attend_back_kernel,
            grid=(rows, count),
            in_specs=[q_part, q_part, limit_spec, pos_spec]
            + [kv_part] * 2
            + [pl.BlockSpec(memory_space=pl.ANY)] * len(held),
            out_specs=[q_part] + [kv_part] * 2,
            out_shape=[jax.ShapeDtypeStruct(packed, f32)]
            + [jax.ShapeDtypeStruct((n // 2,) + packed_kv, bf16)] * 2,
            scratch_shapes=[
                pltpu.VMEM((SLOTS, LANES), bf16),
                pltpu.VMEM((LANES, SLOTS), bf16),
                pltpu.VMEM((SLOTS, LANES), f32),
            ],
            input_output_aliases={6 + i: i for i in range(len(held))},
            compiler_params=params(2),
            cost_estimate=SMALL,
            name="attend_back",
        )(queries, grads, limit, key_pos, *kv_halves, *held)

    held = attend_back(0, 3, d_heads)
    t_attn = TensorGather(d_attn_own)
    link.go(t_ffn, s_ff[3], s_ff[2], s_ff[0], s_ff[1], during=held)
    d_query, d_low, d_high = attend_back(3, HEADS_KV - 3, after(d_heads, *link.done), *held)

    def key_grads(begin, end, arrived, kind):
        if begin >= n // 2:
            return d_high
        return plus(d_low[begin:end].astype(f32), arrived, kind)

    s_keys = Scatter(key_grads)
    d_q_low, d_q_gain = pl.pallas_call(
        query_back_kernel,
        grid=(n_tensor,),
        in_specs=[part_spec, head_spec, whole(one_head), whole(one_head), whole((1, HEAD))],
        out_specs=(head_spec, whole((1, HEAD))),
        out_shape=(
            jax.ShapeDtypeStruct(heads_shape, bf16),
            jax.ShapeDtypeStruct((1, HEAD), f32),
        ),
        compiler_params=params(),
        cost_estimate=SMALL,
        name="query_back",
    )(d_query, q_raw, cos, sin, q_gain)

    def product(left, right):
        wide = right.shape[1]
        count = width // 256
        grid = width // 512
        halves = pl.pallas_call(
            product_kernel,
            grid=(grid,),
            in_specs=[pl.BlockSpec((rows_all // 2, 512), lambda j: (0, j))] * 2
            + [whole(right.shape)],
            out_specs=(
                pl.BlockSpec((2, wide, 256), lambda j: (jnp.minimum(j, grid // 2 - 1), 0, 0)),
                pl.BlockSpec((2, wide, 256), lambda j: (jnp.maximum(j - grid // 2, 0), 0, 0)),
            ),
            out_shape=[jax.ShapeDtypeStruct((count // 2, wide, 256), bf16)] * 2,
            scratch_shapes=[pltpu.VMEM((wide, rows_all), bf16)],
            compiler_params=params(),
            cost_estimate=SMALL,
            name="product",
        )(*left, right)
        return split_places(halves, wide)

    def sum_of(halves):
        def make(begin, end, arrived, kind):
            if begin >= n // 2:
                return halves[1]
            return plus(halves[0][begin:end].astype(f32), arrived, kind)

        return Scatter(make)

    t_query_back = TensorExchange(d_q_low)
    link.go(t_attn, s_ff[4], s_ff[3], s_ff[2], during=[d_q_low])
    add_grads(5)
    link.go(t_attn, t_query_back, s_keys, s_ff[4], s_ff[3], during=[sent[5]])
    d_attn = t_attn.rows()
    out_halves = product(d_attn, t_heads.rows())
    link.go(t_query_back, s_keys, s_ff[5], s_ff[4], during=out_halves)
    s_out = sum_of(out_halves)
    link.go(s_keys, s_out, s_ff[5], t_ffn)
    d_kv = s_keys.result()
    query_halves = product(h_one_all, after(t_query_back.rows(), d_kv))
    s_query = sum_of(query_halves)
    d_kv_low, d_k_gain = pl.pallas_call(
        key_back_kernel,
        out_shape=(
            jax.ShapeDtypeStruct((sp_rows, kv_cols), bf16),
            jax.ShapeDtypeStruct((1, HEAD), f32),
        ),
        compiler_params=pltpu.CompilerParams(vmem_limit_bytes=VMEM_LIMIT),
        cost_estimate=SMALL,
        name="key_value_back",
    )(d_kv, kv_raw, cos, sin, k_gain)
    kv_part = kv_cols // n_tensor
    t_kv_back = Direct(
        [
            lax.dynamic_slice_in_dim(d_kv_low, (tensor ^ s) * kv_part, kv_part, axis=1)
            for s in tensor_order
        ]
    )
    grad_rel, d_gain_one = pl.pallas_call(
        back_kernel,
        grid=(n_tensor,),
        in_specs=[
            head_spec,
            both_spec,
            whole((sp_rows, kv_cols)),
            whole((width, kv_cols)),
            square,
            whole((1, width)),
            square,
        ],
        out_specs=(square, whole((1, width))),
        out_shape=(
            jax.ShapeDtypeStruct((sp_rows, width), bf16),
            jax.ShapeDtypeStruct((1, width), f32),
        ),
        scratch_shapes=[pltpu.VMEM((sp_rows, width), f32)],
        compiler_params=params(),
        cost_estimate=SMALL,
        name="h_one_back",
    )(d_q_low, query_all, d_kv_low, kv_all, inputs, gain_one[None], d_mixed)
    def collect(first, last, *held):
        terms = [[lows[c], *s_ff[c].raw] for c in range(first, last)]
        flat = [x for group in terms for x in group]
        if not held:
            flat[0] = after(flat[0], grad_rel)
        return pl.pallas_call(
            functools.partial(collect_kernel, len(terms), len(terms[0])),
            grid=(len(terms),),
            in_specs=[pl.BlockSpec((1,) + x.shape[1:], lambda i: (0, 0, 0)) for x in flat]
            + [pl.BlockSpec(memory_space=pl.ANY)] * len(held),
            out_specs=(
                pl.BlockSpec((cols, 2, unit), lambda i: (0, 0, first + i)),
                pl.BlockSpec((unit, cols), lambda i: (first + i, 0)),
            ),
            out_shape=(
                jax.ShapeDtypeStruct((cols, 2, ff), f32),
                jax.ShapeDtypeStruct((ff, cols), f32),
            ),
            input_output_aliases={len(flat) + i: i for i in range(len(held))},
            compiler_params=params(),
            cost_estimate=SMALL,
            name="collect",
        )(*flat, *held)

    early_sums = collect(0, FF_LAST)
    link.done += [*query_halves, *early_sums, grad_rel]
    ffn_terms = t_ffn.terms()
    outputs = pl.pallas_call(
        functools.partial(finish_kernel, tuple(order)),
        grid=(1,),
        in_specs=[smem, square, whole((sp_rows, 1))] + [first_spec] * len(ffn_terms),
        out_specs=square,
        out_shape=low_square,
        compiler_params=params(),
        cost_estimate=SMALL,
        name="finish",
    )(index, mixed, live, *ffn_terms)
    link.go(t_kv_back, s_out, s_query, during=[outputs])
    grad_inputs = call(
        functools.partial(leave_kernel, tuple(order)),
        low_square,
        "leave",
        index,
        grad_rel,
        specs=[smem, vmem],
    )

    gain_parts = jnp.concatenate([d_gain_one, d_gain_two]).reshape(2, n, cols).transpose(1, 0, 2)
    head_rows = max(2 * HEAD // cols, 1)
    head_parts = jnp.concatenate([d_q_gain, d_k_gain]).reshape(1, -1)
    head_parts = jnp.pad(head_parts, ((0, 0), (0, head_rows * cols - 2 * HEAD)))
    head_parts = jnp.broadcast_to(head_parts.reshape(1, head_rows, cols), (n, head_rows, cols))
    small_parts = jnp.concatenate([gain_parts, head_parts], axis=1)
    kv_halves_back = product(h_one_all, t_kv_back.rows())

    def with_small(side):
        begin = side * n // 2
        small_here = small_parts[begin : begin + n // 2].astype(bf16)
        return jnp.concatenate([kv_halves_back[side], small_here], axis=1)

    s_kv = ScatterSoon(with_small(0), with_small(1))
    link.go(s_kv, s_query, s_out, s_ff[5])
    s_kv.advance(s_kv.value())
    t_sums = TensorAll(s_kv.result().astype(bf16))
    t_sums.advance(t_sums.value())
    sum_in, sum_down = collect(FF_LAST, len(sizes), *early_sums)
    link.go(s_query, during=[sum_in, sum_down])
    stack = t_sums.stack
    small = jnp.sum(stack[:, kv_part:].astype(f32), axis=0)
    stack = stack[:, :kv_part]
    sum_gains = small[:2]
    sum_heads = small[2:].reshape(-1)[: 2 * HEAD].reshape(2, HEAD)
    places = [
        sum((((tensor ^ i) // mask) & 1) << k for k, mask in enumerate(masks_of("tensor")))
        for i in range(n_tensor)
    ]
    sum_kv = jnp.concatenate(
        [
            lax.dynamic_index_in_dim(stack, places[i], axis=0, keepdims=False)
            for i in range(n_tensor)
        ],
        axis=0,
    ).T.astype(f32)
    sum_out = s_out.result()
    sum_query = s_query.result().T
    return (
        outputs,
        grad_inputs,
        sum_query,
        sum_kv.astype(f32),
        sum_out,
        sum_in,
        sum_down,
        sum_gains,
        sum_heads,
    )


def solution(mesh):
    in_specs = (
        P(("dp", "tensor"), None),
        P(("dp", "tensor"), None),
        P("dp", "tensor"),
        P("dp", None),
        P("tensor", "dp"),
        P("dp", None, "tensor"),
        P("tensor", "dp"),
        P(None, "dp"),
        P(),
        P(),
        P(),
    )
    out_specs = (
        P(("dp", "tensor"), None),
        P(("dp", "tensor"), None),
        P("dp", "tensor"),
        P("dp", None),
        P("tensor", "dp"),
        P("dp", None, "tensor"),
        P("tensor", "dp"),
        P(None, "dp"),
        P(),
    )
    return jax.shard_map(local, mesh=mesh, in_specs=in_specs, out_specs=out_specs, check_vma=False)
```
